32 devices in a mesh: dp: 8 (over z, x), tensor: 4 (over y, core).
Axes of the slice: x: 2, y: 2, z: 4, core: 2. Of those that a mesh axis runs over, the one named last changes fastest.
Arguments:
- block_input: float32 [32768, 512], P(('dp', 'tensor')), may hold values from -6 to 6
- long_rows: int32 [8], P('dp'), may hold values from 0 to 2, as said below
- short_rows: int32 [8], P('dp'), may hold values from 0 to 4, as said below
- prev_states: float32 [32, 1024], P('dp', 'tensor'), may hold values from 0 to 2
- norm1_gain: float32 [512], replicated, may hold values from 0.5 to 1.5
- conv_weight: float32 [4, 512], replicated, may hold values from -3 to 3
- mixer_weight: float32 [2, 512, 1024], P(None, None, 'tensor'), may hold values from -0.25 to 0.25
- gate_bias: float32 [1024], P('tensor'), may hold values from -7 to 1
- out_weight: float32 [1024, 512], P('tensor'), may hold values from -0.1875 to 0.1875
- norm2_gain: float32 [512], replicated, may hold values from 0.5 to 1.5
- up_weight: float32 [512, 2048], P(None, 'tensor'), may hold values from -0.25 to 0.25
- down_weight: float32 [2048, 512], P('tensor'), may hold values from -0.125 to 0.125
- cotangent: float32 [32768, 512], P(('dp', 'tensor')), may hold values from -6 to 6
Outputs:
- output: float32 [32768, 512], P(('dp', 'tensor'))
- final_states: float32 [32, 1024], P('dp', 'tensor')
- input_grad: float32 [32768, 512], P(('dp', 'tensor'))
- norm1_gain_grad: float32 [512], replicated
- conv_weight_grad: float32 [4, 512], replicated
- mixer_weight_grad: float32 [2, 512, 1024], P(None, None, 'tensor')
- gate_bias_grad: float32 [1024], P('tensor')
- out_weight_grad: float32 [1024, 512], P('tensor')
- norm2_gain_grad: float32 [512], replicated
- up_weight_grad: float32 [512, 2048], P(None, 'tensor')
- down_weight_grad: float32 [2048, 512], P('tensor')
The draws below stay inside these ranges and needn't reach their ends.
Inputs may be any that keep to these rules, and one draw needn't show every extreme that they name: In each group 2048 long_rows + 1024 short_rows lies between half of 4096 and 4096; in every draw one group is filled by long rows alone and another by short rows alone. `short_rows`: see long_rows.
All inputs are finite; a program needn't handle non-finite values.
Results may differ from the reference program's by a relative error of at most 0.0084.
Values may be sent and summed in bfloat16 or wider, within the bound.
A program may use at most 320 MiB of HBM per device.

```python
import jax
import jax.numpy as jnp
from jax import lax

D = 512
H = 1024
FF = 2048
KW = 4
SHORT = 1024
LONG = 2048
GROUP = 4096
SLOTS = 4
TOKENS = 32768
N_DP = 8


def row_counts(key):
    key_long, key_short, key_first, key_second = jax.random.split(key, 4)
    most_long = GROUP // LONG
    long_count = jax.random.randint(key_long, (N_DP,), 0, most_long + 1)
    room = GROUP - LONG * long_count
    lowest = jnp.maximum(0, (GROUP // 2 - LONG * long_count + SHORT - 1) // SHORT)
    highest_short = room // SHORT
    spread = jax.random.randint(key_short, (N_DP,), 0, 1 << 20)
    short_count = lowest + spread % (highest_short - lowest + 1)
    full_long = jax.random.randint(key_first, (), 0, N_DP)
    full_short = (full_long + jax.random.randint(key_second, (), 1, N_DP)) % N_DP
    index = jnp.arange(N_DP, dtype=jnp.int32)
    long_count = jnp.where(index == full_long, most_long, jnp.where(index == full_short, 0, long_count))
    short_count = jnp.where(index == full_long, 0, jnp.where(index == full_short, GROUP // SHORT, short_count))
    return (long_count.astype(jnp.int32), short_count.astype(jnp.int32))


def draw_long_rows(key, part):
    return row_counts(key)[0]


def draw_short_rows(key, part):
    return row_counts(key)[1]


def steps_of(key, extent, pieces, smallest, top_value):
    factor_of = 1.0
    for dim, blocks in pieces:
        draws = jax.random.uniform(jax.random.fold_in(jax.random.fold_in(key, 6), dim), (blocks,), jnp.float32, smallest / len(pieces), top_value / len(pieces))
        factor_of = factor_of * jnp.repeat(jnp.exp(draws), extent[dim] // blocks).reshape((-1,) + (1,) * (len(extent) - 1 - dim))
    return factor_of


def scatter_about(own_key, extent, deviation, most, cuts=(), kind=jnp.bfloat16):
    result = jax.random.normal(own_key, extent, jnp.float32) * deviation
    if len(cuts) > 0:
        result = steps_of(own_key, extent, cuts, -0.22, 0.18) * result
    return jnp.clip(result, min=-most, max=most).astype(kind)


def setup_inputs(seed: int = 0) -> dict:
    seeds = jax.random.split(jax.random.key(seed), 14)
    return {
        "block_input": scatter_about(seeds[0], (TOKENS, D), 1.0, 6.0, ((0, 32),), jnp.float32),
        "long_rows": draw_long_rows(jax.random.fold_in(seeds[13], 71), 0),
        "short_rows": draw_short_rows(jax.random.fold_in(seeds[13], 71), 0),
        "prev_states": jnp.clip(2.0 * jax.random.uniform(seeds[3], (N_DP * SLOTS, H), jnp.float32) ** steps_of(seeds[3], (N_DP * SLOTS, H), ((0, 8), (1, 4)), -0.2, 0.2), 0.0, 2.0),
        "norm1_gain": jnp.clip(1.0 + 0.1 * jax.random.normal(seeds[4], (D,), jnp.float32), 0.5, 1.5),
        "conv_weight": scatter_about(seeds[5], (KW, D), 0.5, 3.0, (), jnp.float32),
        "mixer_weight": scatter_about(seeds[6], (2, D, H), D ** -0.5, 0.25, ((2, 4),), jnp.float32),
        "gate_bias": jnp.clip(-7.0 + 8.0 * jax.random.uniform(seeds[7], (H,), jnp.float32) ** steps_of(seeds[7], (H,), ((0, 4),), -0.2, 0.2), -7.0, 1.0),
        "out_weight": scatter_about(seeds[8], (H, D), H ** -0.5, 0.1875, ((0, 4),), jnp.float32),
        "norm2_gain": jnp.clip(1.0 + 0.1 * jax.random.normal(seeds[9], (D,), jnp.float32), 0.5, 1.5),
        "up_weight": scatter_about(seeds[10], (D, FF), D ** -0.5, 0.25, ((1, 4),), jnp.float32),
        "down_weight": scatter_about(seeds[11], (FF, D), FF ** -0.5, 0.125, ((0, 4),), jnp.float32),
        "cotangent": scatter_about(seeds[12], (TOKENS, D), 1.0, 6.0, ((0, 32),), jnp.float32),
    }


@jax.custom_vjp
def low(v):
    return lax.optimization_barrier(v.astype(jnp.bfloat16)).astype(jnp.float32)

@jax.custom_vjp
def low_back(v):
    return v

def low_keep(v):
    return (low(v), None)

def low_pass(kept, grad):
    return (grad,)

def back_keep(v):
    return (v, None)

def back_low(kept, grad):
    return (low(grad),)
low.defvjp(low_keep, low_pass)
low_back.defvjp(back_keep, back_low)
epsilon = 1e-06
highest = lax.Precision.HIGHEST

def rms_norm(values, gain):
    return values * lax.rsqrt(lax.optimization_barrier(jnp.mean(values * values, axis=-1, keepdims=True)) + epsilon) * gain

def combine(before_pair, after_pair):
    return (before_pair[0] * after_pair[0], after_pair[0] * before_pair[1] + after_pair[1])

def layout(long_rows, short_rows, group_tokens):
    token = jnp.arange(group_tokens, dtype=jnp.int32)[None, :]
    long_count = long_rows[:, None]
    short_count = short_rows[:, None]
    long_end = LONG * long_count
    short_end = long_end + SHORT * short_count
    in_long = token < long_end
    in_short = (token >= long_end) & (token < short_end)
    position = jnp.where(in_long, token % LONG, jnp.where(in_short, (token - long_end) % SHORT, 0))
    slot_index = jnp.where(in_long, token // LONG, jnp.where(in_short, long_count + (token - long_end) // SHORT, -1))
    length = jnp.where(in_long, LONG, SHORT)
    in_row = in_long | in_short
    row_end = in_row & (position == length - 1)
    return (position, slot_index, in_row, row_end)

def reference(block_input, long_rows, short_rows, prev_states, norm1_gain, conv_weight, mixer_weight, gate_bias, out_weight, norm2_gain, up_weight, down_weight, cotangent):
    position, slot_index, in_row, row_end = layout(long_rows, short_rows, GROUP)
    slot_table = (slot_index[..., None] == jnp.arange(SLOTS, dtype=jnp.int32)).astype(jnp.float32)
    end_table = slot_table * row_end[..., None].astype(jnp.float32)
    start = (in_row & (position == 0)).astype(jnp.float32)[..., None]
    linked = (in_row & (position > 0)).astype(jnp.float32)[..., None]
    row_mask = in_row.reshape(-1, 1).astype(jnp.float32)
    tap_masks = [(position >= tap)[..., None].astype(jnp.float32) for tap in range(KW)]

    def forward(inputs, gain_one, taps, mixer, bias, project_out, gain_two, up_proj, down_proj):
        seed_state = jnp.einsum('gts,gsh->gth', slot_table, prev_states.reshape(N_DP, SLOTS, H), precision=highest) * start
        normed = rms_norm(inputs.reshape(N_DP, GROUP, D), gain_one)
        conv = jnp.zeros_like(normed)
        for tap in range(KW):
            moved = jnp.pad(normed, ((0, 0), (tap, 0), (0, 0)))[:, :GROUP]
            conv = conv + taps[tap] * moved * tap_masks[tap]
        conv = low(conv)
        projected = low_back(jnp.einsum('gtd,idh->igth', conv, low(mixer), precision=highest))
        logit = projected[0] + bias
        keep = jax.nn.sigmoid(-logit)
        update = jax.nn.sigmoid(logit) * jax.nn.softplus(projected[1])
        _, states = lax.associative_scan(combine, (keep * linked, update + keep * seed_state), axis=1)
        finals = jnp.einsum('gts,gth->gsh', end_table, states, precision=highest).reshape(N_DP * SLOTS, H)
        state_low = low(states.reshape(-1, H))
        mixed = low_back(jnp.dot(state_low, low(project_out), precision=highest))
        resid = inputs + row_mask * mixed
        normed_two = low(rms_norm(resid, gain_two))
        upward = low_back(jnp.dot(normed_two, low(up_proj), precision=highest))
        activation = low(jax.nn.gelu(upward, approximate=True))
        branch = low_back(jnp.dot(activation, low(down_proj), precision=highest))
        return (resid + row_mask * branch, finals)
    (output, finals), pull = jax.vjp(forward, block_input, norm1_gain, conv_weight, mixer_weight, gate_bias, out_weight, norm2_gain, up_weight, down_weight)
    grads = pull((cotangent, jnp.zeros_like(finals)))
    return (output, finals, grads[0], grads[1], grads[2], grads[3], grads[4], grads[5], grads[6], grads[7], grads[8])
```

```python
import functools

import jax
import jax.numpy as jnp
from jax import lax
from jax.experimental import pallas as pl
from jax.experimental.pallas import tpu as pltpu
from jax.sharding import PartitionSpec as P

SHORT = 1024
LONG = 2048
VMEM_LIMIT = 63 * 1024 * 1024
epsilon = 1e-06
BF16 = jnp.bfloat16
F32 = jnp.float32


def rms_norm(values, gain):
    return values * lax.rsqrt(jnp.mean(values * values, axis=-1, keepdims=True) + epsilon) * gain


def contract(left, right, dims):
    return lax.dot_general(left, right, ((dims[:1], dims[1:]), ((), ())), preferred_element_type=F32)


def combine(before_pair, after_pair):
    return (before_pair[0] * after_pair[0], after_pair[0] * before_pair[1] + after_pair[1])


def row_facts(long_rows, short_rows, chunk):
    long_count, short_count = long_rows[0], short_rows[0]
    in_long = chunk < 2 * long_count
    in_row = chunk < 2 * long_count + short_count
    second = in_long & (chunk % 2 == 1)
    ends = in_row & (second | ~in_long)
    slot = jnp.where(in_long, chunk // 2, chunk - long_count)
    return in_row, second, ends, slot


def pair_swap(values, count):
    return lax.ppermute(values, "tensor", [(i, i ^ 1) for i in range(count)])


def plain(
    block_input, long_rows, short_rows, prev_states, norm1_gain, conv_weight, mixer_weight, gate_bias,
    out_weight, norm2_gain, up_weight, down_weight, cotangent,
):
    tokens, width = block_input.shape
    parts = lax.axis_size("tensor")
    me = lax.axis_index("tensor")
    rim = conv_weight.shape[0] - 1
    in_row, second, ends, slot = row_facts(long_rows, short_rows, me)
    mask = in_row.astype(F32)
    joined = second.astype(F32)
    even = (me % 2 == 0).astype(F32)
    slots = jnp.arange(prev_states.shape[0], dtype=jnp.int32)
    first_half = in_row & ~ends

    mixer_full = lax.all_gather(mixer_weight.astype(BF16), "tensor", axis=2, tiled=True)
    out_full = lax.all_gather(out_weight.astype(BF16), "tensor", axis=0, tiled=True)
    up_full = lax.all_gather(up_weight.astype(BF16), "tensor", axis=1, tiled=True)
    down_full = lax.all_gather(down_weight.astype(BF16), "tensor", axis=0, tiled=True)
    bias = lax.all_gather(gate_bias, "tensor", axis=0, tiled=True)
    prev = lax.all_gather(prev_states, "tensor", axis=1, tiled=True)
    start_state = jnp.sum(
        jnp.where((slots == slot)[:, None] & in_row & ~second, prev, 0.0), axis=0, keepdims=True
    )

    normed, norm1_back = jax.vjp(rms_norm, block_input, norm1_gain)
    rim_rows = pair_swap(normed[tokens - rim :], parts) * joined

    def convolve(extended, weight):
        total = weight[0] * extended[rim:]
        for tap in range(1, rim + 1):
            total = total + mask * weight[tap] * extended[rim - tap : rim - tap + tokens]
        return total

    conv_out, conv_back = jax.vjp(convolve, jnp.concatenate([rim_rows, normed], 0), conv_weight)
    conv_low = conv_out.astype(BF16)
    gate = contract(conv_low, mixer_full[0], (1, 0))
    cand = contract(conv_low, mixer_full[1], (1, 0))
    logit = gate + bias
    keep = jax.nn.sigmoid(-logit)
    opened = jax.nn.sigmoid(logit)
    soft = jax.nn.softplus(cand)
    factors, values = lax.associative_scan(combine, (keep, opened * soft), axis=0)
    ending = factors[-1:] * start_state + values[-1:]
    carry = start_state + joined * pair_swap(ending, parts)
    states = values + factors * carry
    before = jnp.concatenate([carry, states[:-1]], 0)
    end_table = jnp.where((slots == slot) & ends, 1.0, 0.0)[:, None]
    finals = lax.psum_scatter(end_table * states[-1:], "tensor", scatter_dimension=1, tiled=True)
    state_low = states.astype(BF16)
    mixed = contract(state_low, out_full, (1, 0))
    resid = block_input + mask * mixed
    normed_two, norm2_back = jax.vjp(rms_norm, resid, norm2_gain)
    normed_low = normed_two.astype(BF16)
    grad_branch = (mask * cotangent).astype(BF16)
    upward = contract(normed_low, up_full, (1, 0))
    activation, gelu_back = jax.vjp(lambda v: jax.nn.gelu(v, approximate=True), upward)
    activation_low = activation.astype(BF16)
    output = resid + mask * contract(activation_low, down_full, (1, 0))
    grad_act = contract(grad_branch, down_full, (1, 1))
    grad_up = gelu_back(grad_act)[0].astype(BF16)
    grad_norm_two = contract(grad_up, up_full, (1, 1))
    up_grad = contract(normed_low, grad_up, (0, 0))
    down_grad = contract(activation_low, grad_branch, (0, 0))
    grad_resid_norm, gain_two_part = norm2_back(grad_norm_two)
    grad_resid = cotangent + grad_resid_norm
    grad_mixed = (mask * grad_resid).astype(BF16)
    out_grad = contract(state_low, grad_mixed, (0, 0))
    grad_states = contract(grad_mixed, out_full, (1, 1))
    later_keep = jnp.concatenate([keep[1:], jnp.ones_like(keep[:1])], 0)
    back_factors, back_values = lax.associative_scan(combine, (later_keep, grad_states), axis=0, reverse=True)
    joins_next = (first_half & (me % 2 == 0)).astype(F32)
    back_carry = joins_next * pair_swap(keep[:1] * back_values[:1], parts)
    carried = back_values + back_factors * back_carry
    grad_logit = carried * (soft - before) * opened * (1 - opened)
    grad_cand = carried * opened * jax.nn.sigmoid(cand)
    bias_part = jnp.sum(grad_logit, axis=0)
    grad_logit_low = grad_logit.astype(BF16)
    grad_cand_low = grad_cand.astype(BF16)
    mixer_grad = jnp.stack([contract(conv_low, grad_logit_low, (0, 0)), contract(conv_low, grad_cand_low, (0, 0))])
    grad_conv = contract(grad_logit_low, mixer_full[0], (1, 1)) + contract(grad_cand_low, mixer_full[1], (1, 1))
    grad_extended, taps_part = conv_back(grad_conv)
    returned = joins_next * pair_swap(joined * grad_extended[:rim], parts)
    grad_normed = grad_extended[rim:] + jnp.concatenate(
        [jnp.zeros((tokens - rim, width), F32), returned], 0
    )
    grad_input_norm, gain_one_part = norm1_back(grad_normed)
    input_grad = grad_resid + grad_input_norm

    def scatter(grad, dim):
        return lax.psum_scatter(grad.astype(BF16), "tensor", scatter_dimension=dim, tiled=True)

    sharded = (
        scatter(mixer_grad, 2), scatter(out_grad, 0), scatter(up_grad, 1), scatter(down_grad, 0),
    )
    summed = tuple(g.astype(F32) for g in lax.psum(sharded, "dp"))
    shared = lax.psum((gain_one_part, taps_part, gain_two_part, bias_part), ("dp", "tensor"))
    channels = gate_bias.shape[0]
    bias_grad = lax.dynamic_slice_in_dim(shared[3], me * channels, channels)
    return (
        output, finals, input_grad, shared[0], shared[1], summed[0], bias_grad, summed[1], shared[2], summed[2], summed[3],
    )


LANES = 8
COLUMN = 128
MESH = pl.DeviceIdType.MESH
GELU_A = 0.7978845608028654
GELU_B = 0.044715


def dot(left, right, dims=(1, 0)):
    return lax.dot_general(left, right, ((dims[:1], dims[1:]), ((), ())), preferred_element_type=F32)


def rows_of(block, width):
    return block.reshape(-1, width)


class Wires:
    def __init__(self, send, recv):
        self.send, self.recv, self.used = send, recv, 0

    def copy(self, src, dst, device):
        k = self.used
        self.used += 1
        return pltpu.make_async_remote_copy(
            src_ref=src, dst_ref=dst, send_sem=self.send.at[k], recv_sem=self.recv.at[k],
            device_id=device, device_id_type=MESH,
        )


def count_wires(n, z_count, units):
    chips = n // 2
    gather = 4 * (1 + 4 * (chips - 1))
    unit = chips + (chips - 1) + 1 + 3 * (z_count - 1) + 1
    small = 1 + (chips - 1) + 1 + (z_count - 1)
    return gather + units * unit + small + 2 * (n - 1) + 2 + 1 + 2


def block_kernel(
    sizes, long_ref, short_ref, x_hbm, cot_hbm, lead_ref, gain1_ref, taps_ref, gain2_ref, mix_hbm, outw_hbm, up_hbm, down_hbm,
    output_hbm, igrad_hbm, finals_ref, small_ref, fin_up, fin_down, fin_out, fin_mix,
    xb, cb, n1h, res, gn2, fo, conv, t1, t2, n2, gm, act, gup, sig, st, ab, sp, sl,
    mix, outw, up, down,
    p_up, p_down, p_out,
    rc_up, ry_up, kx_up, rx_up, rz_up,
    rc_down, ry_down, kx_down, rx_down, rz_down,
    rc_out, ry_out, kx_out, rx_out, rz_out,
    ry_mix, kx_mix, rx_mix, rz_mix,
    lead, halo1, halo2, endrow, endin, tot, brow, bin_, fsend, frecv,
    acc_n1, acc_n2, acc_t, acc_b, pk, pk_core, pk_chip, pk_x, pk_z,
    send_sem, recv_sem, local_sem,
):
    n, z_count, tokens, width, hs, fs, slots, rim = sizes
    chips = n // 2
    steps = tokens // LANES
    columns = width // COLUMN
    tile = 256
    tiles = tokens // tile
    me = lax.axis_index("tensor")
    q, c = me // 2, me % 2
    dp = lax.axis_index("dp")
    z, x = dp // 2, dp % 2
    wires = Wires(send_sem, recv_sem)
    started = []

    def column(b):
        return pl.ds(b * COLUMN, COLUMN)

    def tensor(j):
        return (dp, j)

    sibling = tensor(me + 1 - 2 * c)
    partner = (dp + 1 - 2 * x, me)

    def z_peer(d):
        return ((((z + d) % z_count) * 2) + x, me)

    def shard_of(d, core):
        return ((q + d) % chips) * 2 + core

    def go(copy):
        copy.start()
        started.append(copy)
        return copy

    locals_ = [
        (mix_hbm.at[0], ab.at[0, pl.ds(0, width)]), (mix_hbm.at[1], ab.at[0, pl.ds(width, width)]),
        (outw_hbm, gn2.at[pl.ds(0, hs)]), (up_hbm, fo.at[pl.ds(0, width)]), (down_hbm, fo.at[pl.ds(width, fs)]),
    ]
    loads = [pltpu.make_async_copy(s, d, local_sem.at[i]) for i, (s, d) in enumerate(locals_)]
    x_loads = [pltpu.make_async_copy(x_hbm.at[:, column(b)], xb.at[b], local_sem.at[5 + b]) for b in range(columns)]
    cot_loads = [
        pltpu.make_async_copy(cot_hbm.at[:, column(b)], cb.at[b], local_sem.at[5 + columns + b]) for b in range(columns)
    ]
    for copy in loads[:3] + x_loads + loads[3:] + cot_loads:
        copy.start()

    barrier = pltpu.get_barrier_semaphore()
    peers = [tensor((me + d) % n) for d in range(1, n)] + [partner] + [z_peer(d) for d in range(1, z_count)]
    for peer in peers:
        pl.semaphore_signal(barrier, inc=1, device_id=peer, device_id_type=MESH)
    pl.semaphore_wait(barrier, len(peers))

    long_count, short_count = long_ref[0], short_ref[0]
    is_long = jnp.where(me < 2 * long_count, 1.0, 0.0)
    in_row = jnp.where(me < 2 * long_count + short_count, 1.0, 0.0)
    odd = (me % 2).astype(F32)
    joined = is_long * odd
    joins_next = is_long * (1.0 - odd)
    starts = in_row * (1.0 - joined)
    ends = in_row * (1.0 - joins_next)
    slot = jnp.where(me < 2 * long_count, me // 2, me - long_count)
    slot_mask = [jnp.where(slot == s, 1.0, 0.0) for s in range(slots)]

    gathers = {}

    def gather(name, ref):
        sib = go(wires.copy(ref.at[me], ref.at[me], sibling))
        far = [go(wires.copy(ref.at[me, x], ref.at[me, x], tensor(shard_of(d, c)))) for d in range(1, chips)]
        across, passed = [], []
        for d in range(1, chips):
            r = shard_of(chips - d, c)
            across.append(wires.copy(ref.at[r, x], ref.at[r, x], partner))
            passed.append((wires.copy(ref.at[r, x], ref.at[r, x], sibling), wires.copy(ref.at[r, 1 - x], ref.at[r, 1 - x], sibling)))
        gathers[name] = (sib, far, across, passed)

    def gather_far(name):
        _, far, across, passed = gathers[name]
        for d in range(chips - 1):
            far[d].wait_recv()
            go(across[d])
            go(passed[d][0])

    def gather_across(name):
        _, far, across, passed = gathers[name]
        for d in range(chips - 1):
            across[d].wait_recv()
            go(passed[d][1])

    def gather_passed(name):
        for one, two in gathers[name][3]:
            one.wait_recv()
            two.wait_recv()

    lead[me] = lead_ref[...]
    lead_copies = [go(wires.copy(lead.at[me], lead.at[me], tensor((me + d) % n))) for d in range(1, n)]
    loads[0].wait()
    loads[1].wait()
    half = width // 2
    for h in range(2):
        mix[me, h] = jnp.concatenate(
            [ab[0, pl.ds(h * half, half), :], ab[0, pl.ds(width + h * half, half), :]], axis=1
        ).astype(BF16)
    gather("mix", mix)
    loads[2].wait()
    outw[me] = gn2[pl.ds(0, hs), :].astype(BF16).reshape(2, hs // 2, width)

    def rest_of_weights():
        gather("out", outw)
        loads[3].wait()
        up[me] = fo[pl.ds(0, width), :].astype(BF16).reshape(up.shape[1:])
        gather("up", up)
        loads[4].wait()
        down[me] = fo[pl.ds(width, fs), :].astype(BF16).reshape(down.shape[1:])
        gather("down", down)

    rest_of_weights()

    def take(ref, i, count):
        return jnp.concatenate(
            [
                jnp.concatenate([ref[b, pl.ds(i * count + k, LANES, stride=steps), :] for b in range(columns)], axis=1)
                for k in range(count)
            ],
            axis=0,
        )

    def put(ref, i, count, value):
        for k in range(count):
            for b in range(columns):
                ref[b, pl.ds(i * count + k, LANES, stride=steps), :] = value[
                    k * LANES : (k + 1) * LANES, b * COLUMN : (b + 1) * COLUMN
                ]

    group = 4
    span = group * LANES
    spans = steps // group

    def at(i, shift=0, size=span):
        return pl.ds(pl.multiple_of(i * size + shift, LANES), size)

    def eights(value):
        return jnp.sum(value.reshape(-1, LANES, value.shape[-1]), axis=0)

    for copy in x_loads:
        copy.wait()
    gain1 = gain1_ref[...]
    gain2 = gain2_ref[...]

    @pl.loop(0, spans)
    def _(i):
        v = take(xb, i, group)
        scale = lax.rsqrt(jnp.mean(v * v, axis=-1, keepdims=True) + epsilon)
        n1h[at(i, rim * LANES), :] = v * scale * gain1
        res[at(i), :] = v

    edge = rim * LANES
    halo_copy = go(wires.copy(n1h.at[pl.ds(tokens, edge)], halo1, sibling))
    for copy in cot_loads:
        copy.wait()

    @pl.loop(0, spans)
    def _(i):
        gm[at(i), :] = (in_row * take(cb, i, group)).astype(BF16)

    halo_copy.wait_recv()
    sub = lax.broadcasted_iota(jnp.int32, (LANES, width), 0)
    for k in range(rim):
        own = pltpu.roll(n1h[pl.ds(tokens + k * LANES, LANES), :], 1, 0)
        other = pltpu.roll(halo1[pl.ds(k * LANES, LANES), :], 1, 0)
        n1h[pl.ds(k * LANES, LANES), :] = jnp.where(sub == 0, joined * other, own)
    tap = [taps_ref[pl.ds(k, 1), :] * (1.0 if k == 0 else in_row) for k in range(rim + 1)]

    @pl.loop(0, spans)
    def _(i):
        total = tap[0] * n1h[at(i, edge), :]
        for k in range(1, rim + 1):
            total = total + tap[k] * n1h[at(i, edge - k * LANES), :]
        conv[at(i), :] = total.astype(BF16)

    def project(j):
        weight = rows_of(mix[j], 2 * hs)
        bias = lead[j, pl.ds(slots, 1), :]

        @pl.loop(0, tiles)
        def _(t):
            rows = at(t, 0, tile)
            pre = dot(conv[rows, :], weight)
            logit = pre[:, :hs] + bias
            cand = pre[:, hs:]
            e = jnp.exp(-jnp.abs(logit))
            r = 1.0 / (1.0 + e)
            opened = jnp.where(logit >= 0, r, e * r)
            keep = jnp.where(logit >= 0, e * r, r)
            soft = jnp.maximum(cand, 0.0) + jnp.log1p(jnp.exp(-jnp.abs(cand)))
            sig[j, rows, :] = opened
            sp[j, rows, :] = soft
            ab[j, rows, :] = keep * in_row
            st[j, at(t, LANES, tile), :] = opened * soft

    for copy in lead_copies:
        copy.wait_recv()
    project(me)
    gathers["mix"][0].wait_recv()
    project(me + 1 - 2 * c)
    gather_far("mix")

    def transpose_to(dst, src):
        @pl.loop(0, tiles)
        def _(t):
            dst[:, pl.ds(pl.multiple_of(t * tile, tile), tile)] = src[at(t, 0, tile), :].T

    transpose_to(t2, gm)
    gather_far("out")
    gather_across("mix")
    for d in range(1, chips):
        project(shard_of(d, c))
    gather_across("out")
    gather_passed("mix")
    for d in range(1, chips):
        project(shard_of(d, 1 - c))
    gather_far("up")

    def scan_step(s, carry):
        rows = at(s, 0, LANES)
        later = at(s, LANES, LANES)
        out = []
        for j in range(n):
            fac, val = carry[j]
            a = ab[j, rows, :]
            b = st[j, later, :]
            fac = a * fac
            val = a * val + b
            ab[j, rows, :] = fac
            st[j, later, :] = val
            out.append((fac, val))
        return tuple(out)

    def unrolled(count, step, carry, by=4):
        def some(i, carry):
            for k in range(by):
                carry = step(i * by + k, carry)
            return carry

        return lax.fori_loop(0, count // by, some, carry)

    one = jnp.ones((LANES, hs), F32)
    zero = jnp.zeros((LANES, hs), F32)
    unrolled(steps, scan_step, tuple((one, zero) for _ in range(n)))
    last = pl.ds(tokens - LANES, LANES)

    def chain(j, carry, keep_rows):
        fac = ab[j, last, :]
        val = st[j, pl.ds(tokens, LANES), :]
        rows = []
        for g in range(LANES):
            rows.append(carry)
            carry = fac[g : g + 1] * carry + val[g : g + 1]
        if keep_rows:
            st[j, pl.ds(0, LANES), :] = jnp.concatenate(rows, axis=0)
        return carry

    first = []
    for j in range(n):
        begin = jnp.zeros((1, hs), F32)
        for s in range(slots):
            begin = begin + (starts * slot_mask[s]) * lead[j, pl.ds(s, 1), :]
        first.append(begin)
        endrow[j] = chain(j, begin, False)
    end_copy = go(wires.copy(endrow, endin, sibling))
    gather_across("up")
    gathers["out"][0].wait_recv()
    gather_passed("out")
    end_copy.wait_recv()
    for j in range(n):
        ending = chain(j, first[j] + joined * endin[j], True)
        for s in range(slots):
            fsend[j, pl.ds(s, 1), :] = (ends * slot_mask[s]) * ending
    final_copies = [
        go(wires.copy(fsend.at[(me + d) % n], frecv.at[d - 1], tensor((me + d) % n))) for d in range(1, n)
    ]

    @pl.loop(0, tiles)
    def _(t):
        rows = at(t, 0, tile)
        mixed = jnp.zeros((tile, width), F32)
        for j in range(n):
            into = st[j, pl.ds(0, LANES), :]
            value = st[j, at(t, LANES, tile), :] + (
                ab[j, rows, :].reshape(-1, LANES, hs) * into[None]
            ).reshape(tile, hs)
            st[j, at(t, LANES, tile), :] = value
            low = value.astype(BF16)
            sl[j, rows, :] = low
            mixed = mixed + dot(low, rows_of(outw[j], width))
        resid = res[rows, :] + in_row * mixed
        res[rows, :] = resid
        scale = lax.rsqrt(jnp.mean(resid * resid, axis=-1, keepdims=True) + epsilon)
        n2[rows, :] = (resid * scale * gain2).astype(BF16)

    gather_far("down")
    transpose_to(t1, n2)
    gather_passed("up")
    gather_across("down")
    gather_passed("down")
    gathers["up"][0].wait_recv()
    gathers["down"][0].wait_recv()

    sent_weights = list(started)

    class Sum:
        def __init__(self, part, rc, ry, kx, rx, rz, fin):
            self.part, self.rc, self.ry, self.kx, self.rx, self.rz, self.fin = part, rc, ry, kx, rx, rz, fin
            self.cols = part.shape[-1]
            self.piece = part.shape[-2]
            self.c1 = [None] * chips
            self.c1_wires = [wires.used + i for i in range(chips)]
            wires.used += chips

        def one(self, d):
            k = (q + d) % chips
            copy = pltpu.make_async_remote_copy(
                src_ref=self.part.at[shard_of(d, 1 - c)], dst_ref=self.rc.at[d], send_sem=send_sem.at[self.c1_wires[d]],
                recv_sem=recv_sem.at[self.c1_wires[d]], device_id=sibling, device_id_type=MESH,
            )
            self.c1[d] = go(copy)

        def two(self):
            self.c2 = []
            for d in range(1, chips):
                self.c1[d].wait_recv()
                j = shard_of(d, c)

                @pl.loop(0, 2)
                def _(h, j=j, d=d):
                    self.part[j, h] = (self.part[j, h].astype(F32) + self.rc[d, h].astype(F32)).astype(BF16)

                self.c2.append(go(wires.copy(self.part.at[j], self.ry.at[d - 1], tensor(j))))

        def total(self, h):
            v = self.part[me, h].astype(F32) + self.rc[0, h].astype(F32)
            for d in range(chips - 1):
                v = v + self.ry[d, h].astype(F32)
            return v

        def three(self):
            self.c1[0].wait_recv()
            for copy in self.c2:
                copy.wait_recv()
            self.part[me, 1 - x] = self.total(1 - x).astype(BF16)
            self.c3 = go(wires.copy(self.part.at[me, 1 - x], self.rx, partner))
            self.kx[...] = self.total(x)

        def four(self):
            self.c3.wait_recv()
            v = self.kx[...] + self.rx[...].astype(F32)
            self.kx[...] = v
            self.part[me, x] = v.astype(BF16)
            self.c4 = [
                go(wires.copy(self.part.at[me, x, (z + d) % z_count], self.rz.at[d - 1], z_peer(d))) for d in range(1, z_count)
            ]

        def five(self):
            for copy in self.c4:
                copy.wait_recv()
            v = self.kx[z]
            for d in range(z_count - 1):
                v = v + self.rz[d].astype(F32)
            self.fin[x, z] = v.astype(BF16)
            mine = self.fin.at[x, z]
            self.c5 = [go(wires.copy(mine, mine, z_peer(d))) for d in range(1, z_count)]
            self.c6 = [go(wires.copy(mine, mine, partner))]

        def six(self):
            for d in range(1, z_count):
                self.c5[d - 1].wait_recv()
                theirs = self.fin.at[x, (z + z_count - d) % z_count]
                self.c6.append(go(wires.copy(theirs, theirs, partner)))

        def end(self):
            for copy in self.c6:
                copy.wait_recv()

    s_up = Sum(p_up, rc_up, ry_up, kx_up, rx_up, rz_up, fin_up)
    s_down = Sum(p_down, rc_down, ry_down, kx_down, rx_down, rz_down, fin_down)
    s_out = Sum(p_out, rc_out, ry_out, kx_out, rx_out, rz_out, fin_out)
    s_mix = Sum(up, down, ry_mix, kx_mix, rx_mix, rz_mix, fin_mix)

    def weight_grad(unit, j, left, right, cols):
        step = 256
        for k in range(cols // step):
            value = dot(left[...], right(pl.ds(k * step, step)))
            unit.part[j, :, :, :, pl.ds(k * step, step)] = value.astype(BF16).reshape(unit.part.shape[1:-1] + (step,))

    def feed(j, begin):
        @pl.loop(0, tiles)
        def _(t):
            rows = at(t, 0, tile)
            upw = rows_of(up[j], fs)
            downw = rows_of(down[j], width)
            u = dot(n2[rows, :], upw)
            ga = dot(gm[rows, :], downw, (1, 1))
            u2 = u * u
            th = jnp.tanh(GELU_A * u * (1.0 + GELU_B * u2))
            hp = 0.5 + 0.5 * th
            a = (u * hp).astype(BF16)
            slope = hp + (0.5 * GELU_A) * u * (1.0 - th * th) * (1.0 + 3.0 * GELU_B * u2)
            gu = (ga * slope).astype(BF16)
            act[rows, :] = a
            gup[rows, :] = gu
            o = dot(a, downw)
            g = dot(gu, upw, (1, 1))
            if begin:
                fo[rows, :] = o
                gn2[rows, :] = g
            else:
                fo[rows, :] = fo[rows, :] + o
                gn2[rows, :] = gn2[rows, :] + g

        weight_grad(s_up, j, t1, lambda k: gup[:, k], fs)
        weight_grad(s_down, j, t2, lambda k: act[:, k], fs)

    for d in range(1, chips):
        feed(shard_of(d, 1 - c), d == 1)
        s_up.one(d)
        s_down.one(d)
        feed(shard_of(d, c), False)
    s_up.two()
    s_down.two()
    feed(me + 1 - 2 * c, False)
    s_up.one(0)
    s_down.one(0)
    feed(me, False)

    acc_n2[...] = jnp.zeros_like(acc_n2)

    @pl.loop(0, spans)
    def _(i):
        r = res[at(i), :]
        g = gn2[at(i), :]
        scale = lax.rsqrt(jnp.mean(r * r, axis=-1, keepdims=True) + epsilon)
        gg = g * gain2
        m = jnp.mean(gg * r, axis=-1, keepdims=True)
        gr = take(cb, i, group) + scale * gg - r * (scale * scale * scale * m)
        acc_n2[...] += eights(g * r * scale)
        gn2[at(i), :] = gr
        gm[at(i), :] = (in_row * gr).astype(BF16)
        put(cb, i, group, r + in_row * fo[at(i), :])

    def store(ref, hbm):
        copies = [
            pltpu.make_async_copy(ref.at[b], hbm.at[:, column(b)], local_sem.at[next_local[0] + b]) for b in range(columns)
        ]
        next_local[0] += columns
        for copy in copies:
            copy.start()
        return copies

    next_local = [5 + 2 * columns]
    stores = store(cb, output_hbm)
    for copy in sent_weights:
        copy.wait_send()
        started.remove(copy)
    s_up.three()

    transpose_to(t2, gm)
    for d in list(range(1, chips)) + [0]:
        for core in (1 - c, c):
            j = shard_of(d, core)
            weight_grad(s_out, j, t2, lambda k, j=j: sl[j, :, k], hs)
        s_out.one(d)
    s_down.three()
    transpose_to(t1, conv)
    s_out.two()
    s_up.four()

    for j in range(n):
        acc_b[j] = jnp.zeros((LANES, hs), F32)

    def recur_back(d, begin, between):
        js = [shard_of(d, core) for core in range(2)]
        for k in range(2):
            j = js[k]

            @pl.loop(0, tiles)
            def _(t, j=j, k=k):
                ab[k, at(t, 0, tile), :] = dot(gm[at(t, 0, tile), :], rows_of(outw[j], width), (1, 1))

        def back_step(i, carry):
            s = steps - 1 - i
            rows = at(s, 0, LANES)
            out = []
            for k in range(2):
                fac, val, keep = carry[k]
                fac = keep * fac
                val = ab[k, rows, :] + keep * val
                ab[2 + k, rows, :] = fac
                ab[k, rows, :] = val
                out.append((fac, val, 1.0 - sig[js[k], rows, :]))
            return tuple(out)

        unrolled(steps, back_step, ((one, zero, one), (one, zero, one)))

        def chain_back(k, carry):
            fac = ab[2 + k, pl.ds(0, LANES), :]
            val = ab[k, pl.ds(0, LANES), :]
            keep = 1.0 - sig[js[k], pl.ds(0, LANES), :]
            rows = []
            for g in reversed(range(LANES)):
                rows.append(carry)
                carry = keep[g : g + 1] * (val[g : g + 1] + fac[g : g + 1] * carry)
            return carry, jnp.concatenate(rows[::-1], axis=0)

        slot_ = 2 * d
        for k in range(2):
            brow[slot_ + k] = chain_back(k, jnp.zeros((1, hs), F32))[0]
        copy = go(wires.copy(brow.at[pl.ds(slot_, 2)], bin_.at[pl.ds(slot_, 2)], sibling))
        between()
        copy.wait_recv()
        for k in (0, 1):
            j = js[k]
            into = chain_back(k, joins_next * bin_[slot_ + k])[1]
            weight = rows_of(mix[j], 2 * hs)

            @pl.loop(0, tiles)
            def _(t, j=j, k=k, into=into, weight=weight):
                rows = at(t, 0, tile)
                carried = ab[k, rows, :] + (ab[2 + k, rows, :].reshape(-1, LANES, hs) * into[None]).reshape(tile, hs)
                opened = sig[j, rows, :]
                soft = sp[j, rows, :]
                weighted = carried * opened
                gl = weighted * (soft - st[j, rows, :]) * (1.0 - opened)
                close = jnp.where(soft < 0.01, soft * (1.0 - soft * (0.5 - soft * (1.0 / 6.0))), 1.0 - jnp.exp(-soft))
                gc = weighted * close
                acc_b[j] += eights(gl)
                gp = jnp.concatenate([gl.astype(BF16), gc.astype(BF16)], axis=1)
                act[rows, :] = gp
                back = dot(gp, weight, (1, 1))
                if begin and k == 0:
                    res[rows, :] = back
                else:
                    res[rows, :] = res[rows, :] + back

            weight_grad(s_mix, j, t1, lambda kk: act[:, kk], 2 * hs)

    def after_first():
        s_down.four()

    for d in range(1, chips):
        recur_back(d, d == 1, after_first if d == 1 else (lambda: None))
        s_mix.one(d)
    s_up.five()

    def between_last():
        s_mix.two()
        s_out.three()

    recur_back(0, chips == 1, between_last)
    s_mix.one(0)
    halo_back = go(wires.copy(res.at[pl.ds(0, edge)], halo2, sibling))
    s_down.five()
    s_up.six()
    s_out.four()
    s_mix.three()

    halo_back.wait_recv()
    for k in range(rim):
        own = pltpu.roll(res[pl.ds(k * LANES, LANES), :], LANES - 1, 0)
        other = pltpu.roll(halo2[pl.ds(k * LANES, LANES), :], LANES - 1, 0)
        res[pl.ds(tokens + k * LANES, LANES), :] = jnp.where(sub == LANES - 1, joins_next * other, own)
    acc_n1[...] = jnp.zeros_like(acc_n1)
    acc_t[...] = jnp.zeros_like(acc_t)

    def norm1_back(i):
        g0 = res[at(i), :]
        total = tap[0] * g0
        acc_t[0] += eights(g0 * n1h[at(i, edge), :])
        for k in range(1, rim + 1):
            total = total + tap[k] * res[at(i, k * LANES), :]
            acc_t[k] += eights(g0 * n1h[at(i, edge - k * LANES), :])
        v = take(xb, i, group)
        scale = lax.rsqrt(jnp.mean(v * v, axis=-1, keepdims=True) + epsilon)
        gg = total * gain1
        m = jnp.mean(gg * v, axis=-1, keepdims=True)
        acc_n1[...] += eights(total * v * scale)
        put(xb, i, group, gn2[at(i), :] + scale * gg - v * (scale * scale * scale * m))

    pl.loop(0, spans)(norm1_back)
    stores += store(xb, igrad_hbm)

    pk[...] = jnp.zeros_like(pk)
    pk[pl.ds(0, 1), :] = jnp.sum(acc_n1[...], axis=0, keepdims=True)
    for k in range(rim + 1):
        pk[pl.ds(1 + k, 1), :] = jnp.sum(acc_t[k], axis=0, keepdims=True)
    pk[pl.ds(6, 1), :] = jnp.sum(acc_n2[...], axis=0, keepdims=True)
    for j in range(n):
        pk[pl.ds(8 + j, 1), pl.ds(0, hs)] = jnp.sum(acc_b[j], axis=0, keepdims=True)
    k1 = go(wires.copy(pk, pk_core, sibling))
    s_mix.four()
    s_out.five()
    k1.wait_recv()
    pk_chip[q] = pk[...] + pk_core[...]
    k2 = [go(wires.copy(pk_chip.at[q], pk_chip.at[q], tensor(shard_of(d, c)))) for d in range(1, chips)]
    s_down.six()
    for copy in k2:
        copy.wait_recv()
    value = pk_chip[0]
    for k in range(1, chips):
        value = value + pk_chip[k]
    pk_x[0] = value
    k3 = go(wires.copy(pk_x.at[0], pk_x.at[1], partner))
    s_mix.five()
    s_out.six()
    k3.wait_recv()
    pk_z[z] = pk_x[0] + pk_x[1]
    k4 = [go(wires.copy(pk_z.at[z], pk_z.at[z], z_peer(d))) for d in range(1, z_count)]
    s_mix.six()
    for copy in final_copies:
        copy.wait_recv()
    total = fsend[me]
    for d in range(n - 1):
        total = total + frecv[d]
    finals_ref[...] = total
    for copy in k4:
        copy.wait_recv()
    value = pk_z[0]
    for k in range(1, z_count):
        value = value + pk_z[k]
    small_ref[...] = value
    for unit in (s_up, s_down, s_out, s_mix):
        unit.end()
    for copy in started:
        copy.wait_send()
    for copy in stores:
        copy.wait()


def fused(
    block_input, long_rows, short_rows, prev_states, norm1_gain, conv_weight, mixer_weight, gate_bias,
    out_weight, norm2_gain, up_weight, down_weight, cotangent,
):
    tokens, width = block_input.shape
    n = lax.axis_size("tensor")
    z_count = lax.axis_size("dp") // 2
    chips = n // 2
    slots, hs = prev_states.shape
    fs = up_weight.shape[1]
    rim = conv_weight.shape[0] - 1
    steps = tokens // LANES
    piece = width // (2 * z_count)
    lead_in = jnp.concatenate([prev_states, gate_bias[None]], axis=0)
    pk_rows = 8 + -(-n // 8) * 8
    units = [fs, fs, hs, 2 * hs]

    def full(cols):
        return pltpu.VMEM((n, 2, z_count, piece, cols), BF16)

    def sums(cols):
        return [
            pltpu.VMEM((chips, 2, z_count, piece, cols), BF16),
            pltpu.VMEM((max(chips - 1, 1), 2, z_count, piece, cols), BF16),
            pltpu.VMEM((z_count, piece, cols), F32),
            pltpu.VMEM((z_count, piece, cols), BF16),
            pltpu.VMEM((max(z_count - 1, 1), piece, cols), BF16),
        ]

    def wide(rows, kind=F32):
        return pltpu.VMEM((rows, width), kind)

    by_column = pltpu.VMEM((width // COLUMN, tokens, COLUMN), F32)
    per_block = pltpu.VMEM((n, tokens, hs), F32)
    scratch = [
        by_column, by_column, wide(tokens + rim * LANES), wide(tokens + rim * LANES), wide(tokens), wide(tokens),
        wide(tokens, BF16), pltpu.VMEM((width, tokens), BF16), pltpu.VMEM((width, tokens), BF16), wide(tokens, BF16),
        wide(tokens, BF16), pltpu.VMEM((tokens, fs), BF16), pltpu.VMEM((tokens, fs), BF16),
        per_block, pltpu.VMEM((n, tokens + LANES, hs), F32), per_block, per_block, pltpu.VMEM((n, tokens, hs), BF16),
        pltpu.VMEM((n, 2, width // 2, 2 * hs), BF16), pltpu.VMEM((n, 2, hs // 2, width), BF16), full(fs),
        full(fs),
        full(fs), full(fs), full(hs),
        *sums(fs), *sums(fs), *sums(hs), *sums(2 * hs)[1:],
        pltpu.VMEM((n, slots + 1, hs), F32), wide(rim * LANES), wide(rim * LANES), pltpu.VMEM((n, 1, hs), F32),
        pltpu.VMEM((n, 1, hs), F32), pltpu.VMEM((8, 128), F32), pltpu.VMEM((n, 1, hs), F32), pltpu.VMEM((n, 1, hs), F32),
        pltpu.VMEM((n, slots, hs), F32), pltpu.VMEM((n - 1, slots, hs), F32),
        wide(LANES), wide(LANES), pltpu.VMEM((rim + 1, LANES, width), F32), pltpu.VMEM((n, LANES, hs), F32),
        wide(pk_rows), wide(pk_rows), pltpu.VMEM((chips, pk_rows, width), F32), pltpu.VMEM((2, pk_rows, width), F32),
        pltpu.VMEM((z_count, pk_rows, width), F32),
    ]
    wire_count = count_wires(n, z_count, 4)
    scratch += [
        pltpu.SemaphoreType.DMA((wire_count,)), pltpu.SemaphoreType.DMA((wire_count,)), pltpu.SemaphoreType.DMA((5 + 4 * (width // COLUMN),)),
    ]
    vmem = pl.BlockSpec(memory_space=pltpu.VMEM)
    smem = pl.BlockSpec(memory_space=pltpu.SMEM)
    hbm = pl.BlockSpec(memory_space=pl.ANY)

    def shape(dims, kind=F32):
        return jax.ShapeDtypeStruct(dims, kind)

    outs = pl.pallas_call(
        functools.partial(block_kernel, (n, z_count, tokens, width, hs, fs, slots, rim)),
        out_shape=[
            shape((tokens, width)), shape((tokens, width)), shape((slots, hs)), shape((pk_rows, width)),
            *[shape((2, z_count, piece, cols), BF16) for cols in units],
        ],
        in_specs=[smem, smem, hbm, hbm, vmem, vmem, vmem, vmem, hbm, hbm, hbm, hbm],
        out_specs=[hbm, hbm] + [vmem] * 6,
        scratch_shapes=scratch,
        compiler_params=pltpu.CompilerParams(collective_id=0, has_side_effects=True, vmem_limit_bytes=VMEM_LIMIT),
    )(
        long_rows, short_rows, block_input, cotangent, lead_in, norm1_gain[None], conv_weight, norm2_gain[None],
        mixer_weight, out_weight, up_weight, down_weight,
    )
    output, input_grad, finals, small, g_up, g_down, g_out, g_mix = outs
    me = lax.axis_index("tensor")
    g_up, g_down, g_out, g_mix = (g.reshape(width, -1).astype(F32) for g in (g_up, g_down, g_out, g_mix))
    mixer_grad = jnp.stack([g_mix[:, :hs], g_mix[:, hs:]])
    bias_grad = lax.dynamic_slice(small, (8 + me, 0), (1, hs))[0]
    return (
        output, finals, input_grad, small[0], small[1 : 2 + rim], mixer_grad, bias_grad, g_out.T, small[6], g_up, g_down.T,
    )


def solution(mesh):
    takes_kernel = mesh.shape["tensor"] == 4 and mesh.shape["dp"] % 2 == 0
    rows = P(("dp", "tensor"), None)
    placed = (
        rows, P("dp"), P("dp"), P("dp", "tensor"), P(), P(), P(None, None, "tensor"), P("tensor"),
        P("tensor", None), P(), P(None, "tensor"), P("tensor", None), rows,
    )
    return jax.shard_map(
        fused if takes_kernel else plain,
        mesh=mesh,
        in_specs=placed,
        out_specs=(
            rows, P("dp", "tensor"), rows, P(), P(), P(None, None, "tensor"), P("tensor"), P("tensor", None),
            P(), P(None, "tensor"), P("tensor", None),
        ),
        check_vma=False,
    )
```

```python
import functools

import jax
import jax.numpy as jnp
from jax import lax
from jax.experimental import pallas as pl
from jax.experimental.pallas import tpu as pltpu
from jax.sharding import PartitionSpec as P

SHORT = 1024
LONG = 2048
VMEM_LIMIT = 63 * 1024 * 1024
epsilon = 1e-06
BF16 = jnp.bfloat16
F32 = jnp.float32


def rms_norm(values, gain):
    return values * lax.rsqrt(jnp.mean(values * values, axis=-1, keepdims=True) + epsilon) * gain


def contract(left, right, dims):
    return lax.dot_general(left, right, ((dims[:1], dims[1:]), ((), ())), preferred_element_type=F32)


def combine(before_pair, after_pair):
    return (before_pair[0] * after_pair[0], after_pair[0] * before_pair[1] + after_pair[1])


def row_facts(long_rows, short_rows, chunk):
    long_count, short_count = long_rows[0], short_rows[0]
    in_long = chunk < 2 * long_count
    in_row = chunk < 2 * long_count + short_count
    second = in_long & (chunk % 2 == 1)
    ends = in_row & (second | ~in_long)
    slot = jnp.where(in_long, chunk // 2, chunk - long_count)
    return in_row, second, ends, slot


def pair_swap(values, count):
    return lax.ppermute(values, "tensor", [(i, i ^ 1) for i in range(count)])


def plain(
    block_input, long_rows, short_rows, prev_states, norm1_gain, conv_weight, mixer_weight, gate_bias,
    out_weight, norm2_gain, up_weight, down_weight, cotangent,
):
    tokens, width = block_input.shape
    parts = lax.axis_size("tensor")
    me = lax.axis_index("tensor")
    rim = conv_weight.shape[0] - 1
    in_row, second, ends, slot = row_facts(long_rows, short_rows, me)
    mask = in_row.astype(F32)
    joined = second.astype(F32)
    even = (me % 2 == 0).astype(F32)
    slots = jnp.arange(prev_states.shape[0], dtype=jnp.int32)
    first_half = in_row & ~ends

    mixer_full = lax.all_gather(mixer_weight.astype(BF16), "tensor", axis=2, tiled=True)
    out_full = lax.all_gather(out_weight.astype(BF16), "tensor", axis=0, tiled=True)
    up_full = lax.all_gather(up_weight.astype(BF16), "tensor", axis=1, tiled=True)
    down_full = lax.all_gather(down_weight.astype(BF16), "tensor", axis=0, tiled=True)
    bias = lax.all_gather(gate_bias, "tensor", axis=0, tiled=True)
    prev = lax.all_gather(prev_states, "tensor", axis=1, tiled=True)
    start_state = jnp.sum(
        jnp.where((slots == slot)[:, None] & in_row & ~second, prev, 0.0), axis=0, keepdims=True
    )

    normed, norm1_back = jax.vjp(rms_norm, block_input, norm1_gain)
    rim_rows = pair_swap(normed[tokens - rim :], parts) * joined

    def convolve(extended, weight):
        total = weight[0] * extended[rim:]
        for tap in range(1, rim + 1):
            total = total + mask * weight[tap] * extended[rim - tap : rim - tap + tokens]
        return total

    conv_out, conv_back = jax.vjp(convolve, jnp.concatenate([rim_rows, normed], 0), conv_weight)
    conv_low = conv_out.astype(BF16)
    gate = contract(conv_low, mixer_full[0], (1, 0))
    cand = contract(conv_low, mixer_full[1], (1, 0))
    logit = gate + bias
    keep = jax.nn.sigmoid(-logit)
    opened = jax.nn.sigmoid(logit)
    soft = jax.nn.softplus(cand)
    factors, values = lax.associative_scan(combine, (keep, opened * soft), axis=0)
    ending = factors[-1:] * start_state + values[-1:]
    carry = start_state + joined * pair_swap(ending, parts)
    states = values + factors * carry
    before = jnp.concatenate([carry, states[:-1]], 0)
    end_table = jnp.where((slots == slot) & ends, 1.0, 0.0)[:, None]
    finals = lax.psum_scatter(end_table * states[-1:], "tensor", scatter_dimension=1, tiled=True)
    state_low = states.astype(BF16)
    mixed = contract(state_low, out_full, (1, 0))
    resid = block_input + mask * mixed
    normed_two, norm2_back = jax.vjp(rms_norm, resid, norm2_gain)
    normed_low = normed_two.astype(BF16)
    grad_branch = (mask * cotangent).astype(BF16)
    upward = contract(normed_low, up_full, (1, 0))
    activation, gelu_back = jax.vjp(lambda v: jax.nn.gelu(v, approximate=True), upward)
    activation_low = activation.astype(BF16)
    output = resid + mask * contract(activation_low, down_full, (1, 0))
    grad_act = contract(grad_branch, down_full, (1, 1))
    grad_up = gelu_back(grad_act)[0].astype(BF16)
    grad_norm_two = contract(grad_up, up_full, (1, 1))
    up_grad = contract(normed_low, grad_up, (0, 0))
    down_grad = contract(activation_low, grad_branch, (0, 0))
    grad_resid_norm, gain_two_part = norm2_back(grad_norm_two)
    grad_resid = cotangent + grad_resid_norm
    grad_mixed = (mask * grad_resid).astype(BF16)
    out_grad = contract(state_low, grad_mixed, (0, 0))
    grad_states = contract(grad_mixed, out_full, (1, 1))
    later_keep = jnp.concatenate([keep[1:], jnp.ones_like(keep[:1])], 0)
    back_factors, back_values = lax.associative_scan(combine, (later_keep, grad_states), axis=0, reverse=True)
    joins_next = (first_half & (me % 2 == 0)).astype(F32)
    back_carry = joins_next * pair_swap(keep[:1] * back_values[:1], parts)
    carried = back_values + back_factors * back_carry
    grad_logit = carried * (soft - before) * opened * (1 - opened)
    grad_cand = carried * opened * jax.nn.sigmoid(cand)
    bias_part = jnp.sum(grad_logit, axis=0)
    grad_logit_low = grad_logit.astype(BF16)
    grad_cand_low = grad_cand.astype(BF16)
    mixer_grad = jnp.stack([contract(conv_low, grad_logit_low, (0, 0)), contract(conv_low, grad_cand_low, (0, 0))])
    grad_conv = contract(grad_logit_low, mixer_full[0], (1, 1)) + contract(grad_cand_low, mixer_full[1], (1, 1))
    grad_extended, taps_part = conv_back(grad_conv)
    returned = joins_next * pair_swap(joined * grad_extended[:rim], parts)
    grad_normed = grad_extended[rim:] + jnp.concatenate(
        [jnp.zeros((tokens - rim, width), F32), returned], 0
    )
    grad_input_norm, gain_one_part = norm1_back(grad_normed)
    input_grad = grad_resid + grad_input_norm

    def scatter(grad, dim):
        return lax.psum_scatter(grad.astype(BF16), "tensor", scatter_dimension=dim, tiled=True)

    sharded = (
        scatter(mixer_grad, 2), scatter(out_grad, 0), scatter(up_grad, 1), scatter(down_grad, 0),
    )
    summed = tuple(g.astype(F32) for g in lax.psum(sharded, "dp"))
    shared = lax.psum((gain_one_part, taps_part, gain_two_part, bias_part), ("dp", "tensor"))
    channels = gate_bias.shape[0]
    bias_grad = lax.dynamic_slice_in_dim(shared[3], me * channels, channels)
    return (
        output, finals, input_grad, shared[0], shared[1], summed[0], bias_grad, summed[1], shared[2], summed[2], summed[3],
    )


LANES = 8
MESH = pl.DeviceIdType.MESH
CHUNKS = (2, 2, 1, 4)
WIRES = 256
SCHEDULE = {
    "own": (("g", "mix", "far", 0),),
    "gm": (("g", "mix", "far", 1),),
    "mixfar!": (("g", "out", "far", 0), ("g", "mix", "across", 0), ("g", "up", "far", 0), ("g", "mix", "across", 1)),
    "scan2": (("g", "out", "across", 0), ("g", "up", "far", 1)),
    "end!": (("g", "down", "far", 0), ("g", "up", "across", 0)),
    "states": (("g", "down", "far", 1), ("g", "up", "across", 1)),
    "updown!": (("g", "down", "across", 0), ("g", "down", "across", 1)),
    "f2a": (("up", "y", 0), ("up", "y", 1), ("down", "xa", 1, 0), ("down", "xa", 1, 1)),
    "f3b": (("down", "ya", 0),),
    "f3d": (("down", "ya", 1),),
    "B1a": (("up", "x", 0), ("down", "xa", 0, 0), ("down", "xa", 0, 1)),
    "r1g": (("up", "x", 1),),
    "r1w!": (("out", "y", 0), ("up", "z", 0)),
    "r1w0": (("down", "z", 0),),
    "r0g": (("up", "zb", 0), ("down", "z", 1)),
    "r0w!": (("up", "z", 1), ("mix", "y", 0), ("mix", "y", 1), ("mix", "y", 2), ("mix", "y", 3), ("down", "zb", 0), ("out", "x", 0)),
    "r0k1": (("up", "xb", 0),),
    "halo!": (("out", "z", 0), ("down", "zb", 1), ("mix", "x", 0), ("mix", "x", 1)),
    "n1b": (("up", "zb", 1),),
    "drain": (("mix", "x", 2), ("mix", "z", 0), ("down", "xb", 0), ("pk", "chip"), ("mix", "z", 1), ("mix", "x", 3), ("pk", "x"), ("mix", "z", 2), ("out", "zb", 0), ("down", "xb", 1), ("mix", "z", 3), ("pk", "z"), ("up", "xb", 1), ("mix", "zb", 0), ("mix", "zb", 1), ("mix", "zb", 2), ("out", "xb", 0), ("mix", "zb", 3), ("mix", "xb", 0), ("mix", "xb", 1), ("mix", "xb", 2), ("mix", "xb", 3)),
}
GELU_A = 0.7978845608028654
GELU_B = 0.044715


def dot(left, right, dims=(1, 0)):
    return lax.dot_general(left, right, ((dims[:1], dims[1:]), ((), ())), preferred_element_type=F32)


def rows_of(block, width):
    return block.reshape(-1, width)


class Wires:
    def __init__(self, send, recv):
        self.send, self.recv, self.used = send, recv, 0

    def copy(self, src, dst, device):
        k = self.used
        self.used += 1
        return pltpu.make_async_remote_copy(
            src_ref=src, dst_ref=dst, send_sem=self.send.at[k], recv_sem=self.recv.at[k],
            device_id=device, device_id_type=MESH,
        )


def block_kernel(
    sizes, long_ref, short_ref, x_hbm, cot_hbm, prev_ref, bias_ref, gain1_ref, taps_ref, gain2_ref, mix_hbm, outw_hbm, up_hbm,
    down_hbm,
    output_hbm, igrad_hbm, finals_ref, small_ref, fin_up, fin_down, fin_out, fin_mix,
    xb, cb, n1h, res, gn2, fo, conv, n2, gm, act, gup, sig, st, ab, sp, sl,
    mix, outw, up, down,
    p_up, p_down, p_out,
    rc_up, ry_up, kx_up, rx_up, rz_up,
    rc_down, ry_down, kx_down, rx_down, rz_down,
    rc_out, ry_out, kx_out, rx_out, rz_out,
    ry_mix, kx_mix, rx_mix, rz_mix,
    prev, biases, halo1, halo2, endrow, endin, brow, bin_, fsend, frecv,
    acc_n1, acc_n2, acc_t, acc_b, pk, pk_core, pk_chip, pk_x, pk_z,
    send_sem, recv_sem, local_sem,
):
    n, z_count, tokens, width, hs, fs, slots, rim = sizes
    chips = n // 2
    steps = tokens // LANES
    tile = 256
    tiles = tokens // tile
    me = lax.axis_index("tensor")
    q, c = me // 2, me % 2
    dp = lax.axis_index("dp")
    z, x = dp // 2, dp % 2
    wires = Wires(send_sem, recv_sem)
    started = []

    def tensor(j):
        return (dp, j)

    sibling = tensor(me + 1 - 2 * c)
    partner = (dp + 1 - 2 * x, me)

    def z_peer(d):
        return ((((z + d) % z_count) * 2) + x, me)

    def shard_of(d, core):
        return ((q + d) % chips) * 2 + core

    def go(copy):
        copy.start()
        started.append(copy)
        return copy

    locals_ = [
        (mix_hbm.at[0], ab.at[0, pl.ds(0, width)]), (mix_hbm.at[1], ab.at[0, pl.ds(width, width)]),
        (outw_hbm, gn2.at[pl.ds(0, hs)]), (up_hbm, fo.at[pl.ds(0, width)]), (down_hbm, fo.at[pl.ds(width, fs)]),
    ]
    loads = [pltpu.make_async_copy(s, d, local_sem.at[i]) for i, (s, d) in enumerate(locals_)]

    def run(ref, g):
        return ref.at[pl.ds(g * steps, steps)]

    x_loads = [pltpu.make_async_copy(run(x_hbm, g), xb.at[:, g, :], local_sem.at[5 + g]) for g in range(LANES)]
    cot_loads = [pltpu.make_async_copy(run(cot_hbm, g), cb.at[:, g, :], local_sem.at[5 + LANES + g]) for g in range(LANES)]
    for copy in loads[:2] + x_loads + loads[2:] + cot_loads:
        copy.start()

    barrier = pltpu.get_barrier_semaphore()
    peers = [tensor((me + d) % n) for d in range(1, n)] + [partner] + [z_peer(d) for d in range(1, z_count)]
    for peer in peers:
        pl.semaphore_signal(barrier, inc=1, device_id=peer, device_id_type=MESH)

    long_count, short_count = long_ref[0], short_ref[0]
    is_long = jnp.where(me < 2 * long_count, 1.0, 0.0)
    in_row = jnp.where(me < 2 * long_count + short_count, 1.0, 0.0)
    odd = (me % 2).astype(F32)
    joined = is_long * odd
    joins_next = is_long * (1.0 - odd)
    starts = in_row * (1.0 - joined)
    ends = in_row * (1.0 - joins_next)
    slot = jnp.where(me < 2 * long_count, me // 2, me - long_count)
    slot_mask = [jnp.where(slot == s, 1.0, 0.0) for s in range(slots)]

    gathers = {}

    def gather(name, ref):
        size = ref.shape[1] // 2
        far, across, passed = [], [], []
        for k in range(size):
            mine, r = ref.at[me, x * size + k], shard_of(1, c)
            ours, theirs = ref.at[r, x * size + k], ref.at[r, (1 - x) * size + k]
            far.append(go(wires.copy(mine, mine, tensor(r))))
            across.append(wires.copy(ours, ours, partner))
            passed.append((wires.copy(ours, ours, sibling), wires.copy(theirs, theirs, sibling)))
        sib = go(wires.copy(ref.at[me], ref.at[me], sibling))
        gathers[name] = (sib, far, across, passed)

    def gather_far(name, k):
        _, far, across, passed = gathers[name]
        far[k].wait_recv()
        go(across[k])
        go(passed[k][0])

    def gather_across(name, k):
        _, far, across, passed = gathers[name]
        across[k].wait_recv()
        go(passed[k][1])

    def gather_passed(name):
        for one, two in gathers[name][3]:
            one.wait_recv()
            two.wait_recv()

    stages = {("g", "far"): gather_far, ("g", "across"): gather_across}

    def run_stages(hook):
        for step in SCHEDULE.get(hook, ()):
            if step[0] == "g":
                stages["g", step[2]](step[1], *step[3:])
            else:
                stages[step[:2]](*step[2:])

    prev[me] = prev_ref[...]
    biases[me] = bias_ref[...]
    loads[0].wait()
    loads[1].wait()
    half = width // 2
    for h in range(2):
        mix[me, pl.ds(2 * h, 2)] = (
            jnp.concatenate([ab[0, pl.ds(h * half, half), :], ab[0, pl.ds(width + h * half, half), :]], axis=1)
            .astype(BF16)
            .reshape((2,) + mix.shape[2:])
        )
    pl.semaphore_wait(barrier, len(peers))
    gather("mix", mix)
    lead_copies = []
    for ref in (prev, biases):
        lead_copies += [go(wires.copy(ref.at[me], ref.at[me], tensor((me + d) % n))) for d in range(1, n)]
    loads[2].wait()
    outw[me] = gn2[pl.ds(0, hs), :].astype(BF16).reshape(2, hs // 2, width)
    gather("out", outw)
    loads[3].wait()
    up[me] = fo[pl.ds(0, width), :].astype(BF16).reshape(up.shape[1:])
    gather("up", up)
    loads[4].wait()
    down[me] = fo[pl.ds(width, fs), :].astype(BF16).reshape(down.shape[1:])
    gather("down", down)

    span = 64
    spans = tokens // span

    def at(i, shift=0, size=span):
        return pl.ds(pl.multiple_of(i * size + shift, LANES), size)

    def take(ref, i, size=span):
        return ref[pl.ds(i * (size // LANES), size // LANES)].reshape(size, width)

    def put(ref, i, value):
        ref[pl.ds(i * (span // LANES), span // LANES)] = value.reshape(span // LANES, LANES, width)

    def eights(value):
        return jnp.sum(value.reshape(-1, LANES, value.shape[-1]), axis=0)

    hook = run_stages
    for copy in x_loads:
        copy.wait()
    gain1 = gain1_ref[...]
    gain2 = gain2_ref[...]

    @pl.loop(0, spans, unroll=4)
    def _(i):
        v = take(xb, i)
        scale = lax.rsqrt(jnp.mean(v * v, axis=-1, keepdims=True) + epsilon)
        n1h[at(i, rim * LANES), :] = v * scale * gain1

    hook("norm1")
    edge = rim * LANES
    halo_copy = go(wires.copy(n1h.at[pl.ds(tokens, edge)], halo1, sibling))
    halo_copy.wait_recv()
    sub = lax.broadcasted_iota(jnp.int32, (LANES, width), 0)
    for k in range(rim):
        own = pltpu.roll(n1h[pl.ds(tokens + k * LANES, LANES), :], 1, 0)
        other = pltpu.roll(halo1[pl.ds(k * LANES, LANES), :], 1, 0)
        n1h[pl.ds(k * LANES, LANES), :] = jnp.where(sub == 0, joined * other, own)
    tap = [taps_ref[pl.ds(k, 1), :] * (1.0 if k == 0 else in_row) for k in range(rim + 1)]

    @pl.loop(0, spans, unroll=4)
    def _(i):
        total = tap[0] * n1h[at(i, edge), :]
        for k in range(1, rim + 1):
            total = total + tap[k] * n1h[at(i, edge - k * LANES), :]
        conv[at(i), :] = total.astype(BF16)

    def project(j):
        weight = rows_of(mix[j], 2 * hs)
        bias = biases[j]

        @pl.loop(0, tiles, unroll=tiles)
        def _(t):
            rows = at(t, 0, tile)
            pre = dot(conv[rows, :], weight)
            logit = pre[:, :hs] + bias
            cand = pre[:, hs:]
            e = jnp.exp(-jnp.abs(logit))
            r = 1.0 / (1.0 + e)
            opened = jnp.where(logit >= 0, r, e * r)
            keep = jnp.where(logit >= 0, e * r, r)
            soft = jnp.maximum(cand, 0.0) + jnp.log1p(jnp.exp(-jnp.abs(cand)))
            sig[j, rows, :] = opened
            sp[j, rows, :] = soft
            ab[j, rows, :] = keep * in_row
            st[j, at(t, LANES, tile), :] = opened * soft

    hook("conv")
    for copy in lead_copies:
        copy.wait_recv()
    project(me)
    hook("own")
    gathers["mix"][0].wait_recv()
    project(me + 1 - 2 * c)
    hook("sib")

    def unrolled(count, step, carry, by=4):
        def some(i, carry):
            for k in range(by):
                carry = step(i * by + k, carry)
            return carry

        return lax.fori_loop(0, count // by, some, carry)

    one = jnp.ones((LANES, hs), F32)
    zero = jnp.zeros((LANES, hs), F32)

    def scan(js):
        def step(s, carry):
            rows = at(s, 0, LANES)
            later = at(s, LANES, LANES)
            out = []
            for j, (fac, val) in zip(js, carry):
                a = ab[j, rows, :]
                fac = a * fac
                val = a * val + st[j, later, :]
                ab[j, rows, :] = fac
                st[j, later, :] = val
                out.append((fac, val))
            return tuple(out)

        unrolled(steps, step, tuple((one, zero) for _ in js))

    scan([me, me + 1 - 2 * c])
    hook("scan1")
    for copy in cot_loads:
        copy.wait()

    @pl.loop(0, spans, unroll=4)
    def _(i):
        gm[at(i), :] = (in_row * take(cb, i)).astype(BF16)

    hook("gm")
    hook("mixfar!")
    project(shard_of(1, c))
    hook("rown")
    hook("mixpass!")
    gather_passed("mix")
    project(shard_of(1, 1 - c))
    hook("rsib")
    scan([shard_of(1, c), shard_of(1, 1 - c)])
    hook("scan2")
    last = pl.ds(tokens - LANES, LANES)

    def chain(j, carry, keep_rows):
        fac = ab[j, last, :]
        val = st[j, pl.ds(tokens, LANES), :]
        rows = []
        for g in range(LANES):
            rows.append(carry)
            carry = fac[g : g + 1] * carry + val[g : g + 1]
        if keep_rows:
            st[j, pl.ds(0, LANES), :] = jnp.concatenate(rows, axis=0)
        return carry

    first = []
    for j in range(n):
        begin = jnp.zeros((1, hs), F32)
        for s in range(slots):
            begin = begin + (starts * slot_mask[s]) * prev[j, pl.ds(s, 1), :]
        first.append(begin)
        endrow[j] = chain(j, begin, False)
    end_copy = go(wires.copy(endrow, endin, sibling))
    hook("chain")
    hook("end!")
    end_copy.wait_recv()
    for j in range(n):
        ending = chain(j, first[j] + joined * endin[j], True)
        for s in range(slots):
            fsend[j, pl.ds(s, 1), :] = (ends * slot_mask[s]) * ending
    final_copies = [
        go(wires.copy(fsend.at[(me + d) % n], frecv.at[d - 1], tensor((me + d) % n))) for d in range(1, n)
    ]

    hook("chain2")
    hook("out!")
    gathers["out"][0].wait_recv()
    gather_passed("out")
    @pl.loop(0, tiles, unroll=tiles)
    def _(t):
        rows = at(t, 0, tile)
        mixed = jnp.zeros((tile, width), F32)
        for j in range(n):
            into = st[j, pl.ds(0, LANES), :]
            value = st[j, at(t, LANES, tile), :] + (
                ab[j, rows, :].reshape(-1, LANES, hs) * into[None]
            ).reshape(tile, hs)
            st[j, at(t, LANES, tile), :] = value
            low = value.astype(BF16)
            sl[j, rows, :] = low
            mixed = mixed + dot(low, rows_of(outw[j], width))
        resid = take(xb, t, tile) + in_row * mixed
        res[rows, :] = resid
        scale = lax.rsqrt(jnp.mean(resid * resid, axis=-1, keepdims=True) + epsilon)
        n2[rows, :] = (resid * scale * gain2).astype(BF16)

    hook("states")
    hook("updown!")
    gather_passed("up")
    gather_passed("down")
    gathers["up"][0].wait_recv()
    gathers["down"][0].wait_recv()
    sent_weights = list(started)

    class Sum:
        def __init__(self, part, rc, ry, kx, rx, rz, fin):
            self.part, self.rc, self.ry, self.kx, self.rx, self.rz, self.fin = part, rc, ry, kx, rx, rz, fin
            self.chunks = fin.shape[0]
            self.c1 = [None] * chips
            self.c2, self.c3, self.c4, self.c5, self.c6 = {}, {}, {}, {}, {}
            self.first = wires.used
            wires.used += chips

        def one(self, d):
            copy = pltpu.make_async_remote_copy(
                src_ref=self.part.at[shard_of(d, 1 - c)], dst_ref=self.rc.at[d], send_sem=send_sem.at[self.first + d],
                recv_sem=recv_sem.at[self.first + d], device_id=sibling, device_id_type=MESH,
            )
            self.c1[d] = go(copy)

        def both(self, j, d, k, h):
            return self.part[j, k, h].astype(F32) + self.rc[d, k, h].astype(F32)

        def y(self, k=0):
            self.c2[k] = []
            for d in range(1, chips):
                if k == 0:
                    self.c1[d].wait_recv()
                j = shard_of(d, c)
                for h in range(2):
                    self.part[j, k, h] = self.both(j, d, k, h).astype(BF16)
                self.c2[k].append(go(wires.copy(self.part.at[j, k], self.ry.at[d - 1, k], tensor(j))))

        def total(self, k, h):
            v = self.both(me, 0, k, h)
            for d in range(chips - 1):
                v = v + self.ry[d, k, h].astype(F32)
            return v

        def x(self, k=0):
            if k == 0:
                self.c1[0].wait_recv()
            for copy in self.c2[k]:
                copy.wait_recv()
            self.part[me, k, 1 - x] = self.total(k, 1 - x).astype(BF16)
            self.c3[k] = go(wires.copy(self.part.at[me, k, 1 - x], self.rx.at[k], partner))
            self.kx[k] = self.total(k, x)

        def z(self, k=0):
            self.c3[k].wait_recv()
            self.spread(k, self.kx[k] + self.rx[k].astype(F32))

        def spread(self, k, v):
            self.kx[k] = v
            self.part[me, k, x] = v.astype(BF16)
            self.c4[k] = [
                go(wires.copy(self.part.at[me, k, x, (z + d) % z_count], self.rz.at[d - 1, k], z_peer(d)))
                for d in range(1, z_count)
            ]

        def zb(self, k=0):
            for copy in self.c4[k]:
                copy.wait_recv()
            v = self.kx[k, z]
            for d in range(z_count - 1):
                v = v + self.rz[d, k].astype(F32)
            self.fin[k, x, z] = v.astype(BF16)
            mine = self.fin.at[k, x, z]
            self.c5[k] = [go(wires.copy(mine, mine, z_peer(d))) for d in range(1, z_count)]
            self.c6[k] = [go(wires.copy(mine, mine, partner))]

        def xb(self, k=0):
            for d in range(1, z_count):
                self.c5[k][d - 1].wait_recv()
                theirs = self.fin.at[k, x, (z + z_count - d) % z_count]
                self.c6[k].append(go(wires.copy(theirs, theirs, partner)))

        def end(self):
            for k in range(self.chunks):
                for copy in self.c6[k]:
                    copy.wait_recv()

    class SumAcross(Sum):
        def xa(self, d, k=0):
            if k == 0:
                self.c1[d].wait_recv()
            j = shard_of(d, c)
            self.part[j, k, 1 - x] = self.both(j, d, k, 1 - x).astype(BF16)
            self.c3[d, k] = go(wires.copy(self.part.at[j, k, 1 - x], self.rx.at[d, k], partner))

        def ya(self, k=0):
            self.c3[1, k].wait_recv()
            j = shard_of(1, c)
            self.part[j, k, x] = (self.both(j, 1, k, x) + self.rx[1, k].astype(F32)).astype(BF16)
            self.c2[k] = go(wires.copy(self.part.at[j, k, x], self.ry.at[k], tensor(j)))

        def z(self, k=0):
            self.c3[0, k].wait_recv()
            self.c2[k].wait_recv()
            self.spread(k, self.both(me, 0, k, x) + self.rx[0, k].astype(F32) + self.ry[k].astype(F32))

    s_up = Sum(p_up, rc_up, ry_up, kx_up, rx_up, rz_up, fin_up)
    s_down = SumAcross(p_down, rc_down, ry_down, kx_down, rx_down, rz_down, fin_down)
    s_out = Sum(p_out, rc_out, ry_out, kx_out, rx_out, rz_out, fin_out)
    s_mix = Sum(up, down, ry_mix, kx_mix, rx_mix, rz_mix, fin_mix)

    for name, unit in (("up", s_up), ("down", s_down), ("out", s_out), ("mix", s_mix)):
        for stage in ("y", "x", "xa", "ya", "z", "zb", "xb"):
            stages[name, stage] = getattr(unit, stage, None)

    def weight_grad(unit, j, left, right):
        unit.part[j] = dot(left, right, (0, 0)).astype(BF16).reshape(unit.part.shape[1:])

    def feed(j, begin, name):
        def some(t):
            rows = at(t, 0, tile)
            upw = rows_of(up[j], fs)
            downw = rows_of(down[j], width)
            u = dot(n2[rows, :], upw)
            ga = dot(gm[rows, :], downw, (1, 1))
            u2 = u * u
            th = jnp.tanh(GELU_A * u * (1.0 + GELU_B * u2))
            hp = 0.5 + 0.5 * th
            a = (u * hp).astype(BF16)
            slope = hp + (0.5 * GELU_A) * u * (1.0 - th * th) * (1.0 + 3.0 * GELU_B * u2)
            gu = (ga * slope).astype(BF16)
            act[rows, :] = a
            gup[rows, :] = gu
            o = dot(a, downw)
            g = dot(gu, upw, (1, 1))
            if begin:
                fo[rows, :] = o
                gn2[rows, :] = g
            else:
                fo[rows, :] = fo[rows, :] + o
                gn2[rows, :] = gn2[rows, :] + g

        half_tiles = tiles // 2
        pl.loop(0, half_tiles, unroll=half_tiles)(some)
        hook(name + "a")
        pl.loop(half_tiles, tiles, unroll=half_tiles)(some)
        hook(name + "b")
        weight_grad(s_up, j, n2[...], gup[...])
        hook(name + "u")
        weight_grad(s_down, j, gm[...], act[...])
        hook(name + "d")

    feed(shard_of(1, 1 - c), True, "f0")
    s_up.one(1)
    s_down.one(1)
    hook("f0e")
    feed(shard_of(1, c), False, "f1")
    hook("f1e")
    feed(me + 1 - 2 * c, False, "f2")
    s_up.one(0)
    s_down.one(0)
    hook("f2e")
    feed(me, False, "f3")
    hook("f3e")

    acc_n2[...] = jnp.zeros_like(acc_n2)

    def norm2_back(i):
        r = res[at(i), :]
        g = gn2[at(i), :]
        scale = lax.rsqrt(jnp.mean(r * r, axis=-1, keepdims=True) + epsilon)
        gg = g * gain2
        m = jnp.mean(gg * r, axis=-1, keepdims=True)
        gr = take(cb, i) + scale * gg - r * (scale * scale * scale * m)
        acc_n2[...] += eights(g * r * scale)
        gn2[at(i), :] = gr
        gm[at(i), :] = (in_row * gr).astype(BF16)
        put(cb, i, r + in_row * fo[at(i), :])

    pl.loop(0, spans // 2, unroll=2)(norm2_back)
    hook("B1a")
    pl.loop(spans // 2, spans, unroll=2)(norm2_back)
    hook("B1b")

    def store(ref, hbm, first):
        copies = [pltpu.make_async_copy(ref.at[:, g, :], run(hbm, g), local_sem.at[first + g]) for g in range(LANES)]
        for copy in copies:
            copy.start()
        return copies

    stores = store(cb, output_hbm, 5 + 2 * LANES)
    for copy in sent_weights:
        copy.wait_send()
        started.remove(copy)

    for d in (1, 0):
        for core in (1 - c, c):
            j = shard_of(d, core)
            weight_grad(s_out, j, gm[...], sl[j])
        s_out.one(d)
        hook(f"og{d}")
    hook("oge")

    for j in range(n):
        acc_b[j] = jnp.zeros((LANES, hs), F32)

    def recur_back(d, begin, name):
        js = [shard_of(d, core) for core in range(2)]
        for k in range(2):
            ab[k] = dot(gm[...], rows_of(outw[js[k]], width), (1, 1))
        hook(name + "g")

        def back_step(i, carry):
            s = steps - 1 - i
            rows = at(s, 0, LANES)
            out = []
            for k in range(2):
                fac, val, keep = carry[k]
                fac = keep * fac
                val = ab[k, rows, :] + keep * val
                ab[2 + k, rows, :] = fac
                ab[k, rows, :] = val
                out.append((fac, val, 1.0 - sig[js[k], rows, :]))
            return tuple(out)

        unrolled(steps, back_step, ((one, zero, one), (one, zero, one)))
        hook(name + "s")

        def chain_back(k, carry):
            fac = ab[2 + k, pl.ds(0, LANES), :]
            val = ab[k, pl.ds(0, LANES), :]
            keep = 1.0 - sig[js[k], pl.ds(0, LANES), :]
            rows = []
            for g in reversed(range(LANES)):
                rows.append(carry)
                carry = keep[g : g + 1] * (val[g : g + 1] + fac[g : g + 1] * carry)
            return carry, jnp.concatenate(rows[::-1], axis=0)

        slot_ = 2 * d
        for k in range(2):
            brow[slot_ + k] = chain_back(k, jnp.zeros((1, hs), F32))[0]
        copy = go(wires.copy(brow.at[pl.ds(slot_, 2)], bin_.at[pl.ds(slot_, 2)], sibling))
        hook(name + "c")
        hook(name + "w!")
        copy.wait_recv()
        for k in (0, 1):
            j = js[k]
            into = chain_back(k, joins_next * bin_[slot_ + k])[1]
            weight = rows_of(mix[j], 2 * hs)

            @pl.loop(0, tiles, unroll=tiles)
            def _(t, j=j, k=k, into=into, weight=weight):
                rows = at(t, 0, tile)
                carried = ab[k, rows, :] + (ab[2 + k, rows, :].reshape(-1, LANES, hs) * into[None]).reshape(tile, hs)
                opened = sig[j, rows, :]
                soft = sp[j, rows, :]
                weighted = carried * opened
                gl = weighted * (soft - st[j, rows, :]) * (1.0 - opened)
                close = jnp.where(soft < 0.01, soft * (1.0 - soft * (0.5 - soft * (1.0 / 6.0))), 1.0 - jnp.exp(-soft))
                gc = weighted * close
                acc_b[j] += eights(gl)
                gp = jnp.concatenate([gl.astype(BF16), gc.astype(BF16)], axis=1)
                act[rows, :] = gp
                back = dot(gp, weight, (1, 1))
                if begin and k == 0:
                    res[rows, :] = back
                else:
                    res[rows, :] = res[rows, :] + back

            hook(f"{name}k{k}")
            weight_grad(s_mix, j, conv[...], act[...])
            hook(f"{name}w{k}")

    recur_back(1, True, "r1")
    s_mix.one(1)
    hook("r1e")
    recur_back(0, False, "r0")
    s_mix.one(0)
    hook("r0e")
    halo_back = go(wires.copy(res.at[pl.ds(0, edge)], halo2, sibling))
    hook("h0")
    hook("halo!")
    halo_back.wait_recv()

    for k in range(rim):
        own = pltpu.roll(res[pl.ds(k * LANES, LANES), :], LANES - 1, 0)
        other = pltpu.roll(halo2[pl.ds(k * LANES, LANES), :], LANES - 1, 0)
        res[pl.ds(tokens + k * LANES, LANES), :] = jnp.where(sub == LANES - 1, joins_next * other, own)
    acc_n1[...] = jnp.zeros_like(acc_n1)
    acc_t[...] = jnp.zeros_like(acc_t)

    def norm1_back(i):
        g0 = res[at(i), :]
        total = tap[0] * g0
        acc_t[0] += eights(g0 * n1h[at(i, edge), :])
        for k in range(1, rim + 1):
            total = total + tap[k] * res[at(i, k * LANES), :]
            acc_t[k] += eights(g0 * n1h[at(i, edge - k * LANES), :])
        v = take(xb, i)
        scale = lax.rsqrt(jnp.mean(v * v, axis=-1, keepdims=True) + epsilon)
        gg = total * gain1
        m = jnp.mean(gg * v, axis=-1, keepdims=True)
        acc_n1[...] += eights(total * v * scale)
        put(xb, i, gn2[at(i), :] + scale * gg - v * (scale * scale * scale * m))

    pl.loop(0, spans // 2, unroll=2)(norm1_back)
    hook("n1a")
    pl.loop(spans // 2, spans, unroll=2)(norm1_back)
    stores += store(xb, igrad_hbm, 5 + 3 * LANES)
    hook("n1b")

    pk[...] = jnp.zeros_like(pk)
    pk[pl.ds(0, 1), :] = jnp.sum(acc_n1[...], axis=0, keepdims=True)
    for k in range(rim + 1):
        pk[pl.ds(1 + k, 1), :] = jnp.sum(acc_t[k], axis=0, keepdims=True)
    pk[pl.ds(6, 1), :] = jnp.sum(acc_n2[...], axis=0, keepdims=True)
    for j in range(n):
        pk[pl.ds(8 + j, 1), pl.ds(0, hs)] = jnp.sum(acc_b[j], axis=0, keepdims=True)
    k1 = go(wires.copy(pk, pk_core, sibling))
    small_copies = {}

    def small_chip():
        k1.wait_recv()
        pk_chip[q] = pk[...] + pk_core[...]
        small_copies[2] = go(wires.copy(pk_chip.at[q], pk_chip.at[q], tensor(shard_of(1, c))))

    def small_x():
        small_copies[2].wait_recv()
        pk_x[0] = pk_chip[0] + pk_chip[1]
        small_copies[3] = go(wires.copy(pk_x.at[0], pk_x.at[1], partner))

    def small_z():
        small_copies[3].wait_recv()
        pk_z[z] = pk_x[0] + pk_x[1]
        small_copies[4] = [go(wires.copy(pk_z.at[z], pk_z.at[z], z_peer(d))) for d in range(1, z_count)]

    stages["pk", "chip"], stages["pk", "x"], stages["pk", "z"] = small_chip, small_x, small_z
    hook("pk")
    hook("drain")
    for copy in final_copies:
        copy.wait_recv()
    total = fsend[me]
    for d in range(n - 1):
        total = total + frecv[d]
    finals_ref[...] = total
    for copy in small_copies[4]:
        copy.wait_recv()
    value = pk_z[0]
    for k in range(1, z_count):
        value = value + pk_z[k]
    small_ref[...] = value
    for unit in (s_up, s_down, s_out, s_mix):
        unit.end()
    for copy in started:
        copy.wait_send()
    for copy in stores:
        copy.wait()


def last_kernel(
    hs, output_in, igrad_in, finals_in, small, g_up, g_down, g_out, g_mix,
    output, finals, igrad, gain1, taps, mixer, bias, outw, gain2, up, down, big_a, big_b, mixer_v, outw_v, up_v, down_v, sem,
):
    width = up_v.shape[0]
    first = [pltpu.make_async_copy(output_in, big_a, sem.at[0]), pltpu.make_async_copy(igrad_in, big_b, sem.at[1])]
    for copy in first:
        copy.start()
    me = lax.axis_index("tensor")
    up_v[...] = rows_of(g_up[...], up_v.shape[1]).astype(F32)
    later = [pltpu.make_async_copy(up_v, up, sem.at[2])]
    later[-1].start()
    for copy, src, dst, k in zip(first, (big_a, big_b), (output, igrad), (3, 4)):
        copy.wait()
        later.append(pltpu.make_async_copy(src, dst, sem.at[k]))
        later[-1].start()
    both = rows_of(g_mix[...], 2 * hs).astype(F32)
    mixer_v[0] = both[:, :hs]
    mixer_v[1] = both[:, hs:]
    later.append(pltpu.make_async_copy(mixer_v, mixer, sem.at[5]))
    later[-1].start()
    down_v[...] = rows_of(g_down[...], width).astype(F32).T
    later.append(pltpu.make_async_copy(down_v, down, sem.at[6]))
    later[-1].start()
    outw_v[...] = rows_of(g_out[...], hs).astype(F32).T
    later.append(pltpu.make_async_copy(outw_v, outw, sem.at[7]))
    later[-1].start()
    finals[...] = finals_in[...]
    gain1[...] = small[pl.ds(0, 1), :]
    taps[...] = small[pl.ds(1, taps.shape[0]), :]
    gain2[...] = small[pl.ds(6, 1), :]
    bias[...] = small[pl.ds(8 + me, 1), pl.ds(0, hs)]
    for copy in later:
        copy.wait()


def fused(
    block_input, long_rows, short_rows, prev_states, norm1_gain, conv_weight, mixer_weight, gate_bias,
    out_weight, norm2_gain, up_weight, down_weight, cotangent,
):
    tokens, width = block_input.shape
    n = lax.axis_size("tensor")
    z_count = lax.axis_size("dp") // 2
    chips = n // 2
    slots, hs = prev_states.shape
    fs = up_weight.shape[1]
    rim = conv_weight.shape[0] - 1
    steps = tokens // LANES
    pk_rows = 8 + -(-n // 8) * 8
    units = [(CHUNKS[0], fs), (CHUNKS[1], fs), (CHUNKS[2], hs), (CHUNKS[3], 2 * hs)]

    def block(chunks, cols):
        return (chunks, 2, z_count, width // (2 * z_count * chunks), cols)

    def full(chunks, cols):
        return pltpu.VMEM((n,) + block(chunks, cols), BF16)

    def sums(chunks, cols, across=False):
        dims = block(chunks, cols)
        part = dims[2:]
        return [
            pltpu.VMEM((chips,) + dims, BF16),
            pltpu.VMEM((chunks,) + part if across else (chips - 1,) + dims, BF16),
            pltpu.VMEM((chunks,) + part, F32),
            pltpu.VMEM(((chips, chunks) if across else (chunks,)) + part, BF16),
            pltpu.VMEM((z_count - 1, chunks) + part[1:], BF16),
        ]

    def wide(rows, kind=F32):
        return pltpu.VMEM((rows, width), kind)

    permuted = pltpu.VMEM((steps, LANES, width), F32)
    per_block = pltpu.VMEM((n, tokens, hs), F32)
    scratch = [
        permuted, permuted, wide(tokens + rim * LANES), wide(tokens + rim * LANES), wide(tokens), wide(tokens),
        wide(tokens, BF16), wide(tokens, BF16), wide(tokens, BF16), pltpu.VMEM((tokens, fs), BF16), pltpu.VMEM((tokens, fs), BF16),
        per_block, pltpu.VMEM((n, tokens + LANES, hs), F32), per_block, per_block, pltpu.VMEM((n, tokens, hs), BF16),
        pltpu.VMEM((n, 4, width // 4, 2 * hs), BF16), pltpu.VMEM((n, 2, hs // 2, width), BF16), full(*units[3]), full(*units[3]),
        *[full(*unit) for unit in units[:3]],
        *sums(*units[0]), *sums(*units[1], True), *sums(*units[2]), *sums(*units[3])[1:],
        pltpu.VMEM((n, slots, hs), F32), pltpu.VMEM((n, 1, hs), F32), wide(rim * LANES), wide(rim * LANES),
        pltpu.VMEM((n, 1, hs), F32), pltpu.VMEM((n, 1, hs), F32), pltpu.VMEM((n, 1, hs), F32), pltpu.VMEM((n, 1, hs), F32),
        pltpu.VMEM((n, slots, hs), F32), pltpu.VMEM((n - 1, slots, hs), F32),
        wide(LANES), wide(LANES), pltpu.VMEM((rim + 1, LANES, width), F32), pltpu.VMEM((n, LANES, hs), F32),
        wide(pk_rows), wide(pk_rows), pltpu.VMEM((chips, pk_rows, width), F32), pltpu.VMEM((2, pk_rows, width), F32),
        pltpu.VMEM((z_count, pk_rows, width), F32),
        pltpu.SemaphoreType.DMA((WIRES,)), pltpu.SemaphoreType.DMA((WIRES,)), pltpu.SemaphoreType.DMA((5 + 4 * LANES,)),
    ]
    vmem = pl.BlockSpec(memory_space=pltpu.VMEM)
    smem = pl.BlockSpec(memory_space=pltpu.SMEM)
    hbm = pl.BlockSpec(memory_space=pl.ANY)

    def shape(dims, kind=F32):
        return jax.ShapeDtypeStruct(dims, kind)

    big = shape((tokens, width))
    outs = pl.pallas_call(
        functools.partial(block_kernel, (n, z_count, tokens, width, hs, fs, slots, rim)),
        out_shape=[big, big, shape((slots, hs)), shape((pk_rows, width)), *[shape(block(*unit), BF16) for unit in units]],
        in_specs=[smem, smem, hbm, hbm, vmem, vmem, vmem, vmem, vmem, hbm, hbm, hbm, hbm],
        out_specs=[hbm, hbm] + [vmem] * 6,
        scratch_shapes=scratch,
        compiler_params=pltpu.CompilerParams(collective_id=0, has_side_effects=True, vmem_limit_bytes=VMEM_LIMIT),
    )(
        long_rows, short_rows, block_input, cotangent, prev_states, gate_bias[None], norm1_gain[None], conv_weight,
        norm2_gain[None], mixer_weight, out_weight, up_weight, down_weight,
    )
    outs = pl.pallas_call(
        functools.partial(last_kernel, hs),
        out_shape=[
            big, shape((slots, hs)), big, shape((1, width)), shape((rim + 1, width)), shape((2, width, hs)), shape((1, hs)),
            shape((hs, width)), shape((1, width)), shape((width, fs)), shape((fs, width)),
        ],
        in_specs=[hbm, hbm] + [vmem] * 6,
        out_specs=[hbm, vmem, hbm, vmem, vmem, hbm, vmem, hbm, vmem, hbm, hbm],
        scratch_shapes=[
            wide(tokens), wide(tokens), pltpu.VMEM((2, width, hs), F32), wide(hs), pltpu.VMEM((width, fs), F32), wide(fs),
            pltpu.SemaphoreType.DMA((8,)),
        ],
        compiler_params=pltpu.CompilerParams(vmem_limit_bytes=VMEM_LIMIT),
    )(*outs)
    output, finals, input_grad, gain1, taps, mixer, bias, outw, gain2, up, down = outs
    return (output, finals, input_grad, gain1[0], taps, mixer, bias[0], outw, gain2[0], up, down)


def solution(mesh):
    takes_kernel = mesh.shape["tensor"] == 4 and mesh.shape["dp"] == 8
    rows = P(("dp", "tensor"), None)
    placed = (
        rows, P("dp"), P("dp"), P("dp", "tensor"), P(), P(), P(None, None, "tensor"), P("tensor"),
        P("tensor", None), P(), P(None, "tensor"), P("tensor", None), rows,
    )
    return jax.shard_map(
        fused if takes_kernel else plain,
        mesh=mesh,
        in_specs=placed,
        out_specs=(
            rows, P("dp", "tensor"), rows, P(), P(), P(None, None, "tensor"), P("tensor"), P("tensor", None),
            P(), P(None, "tensor"), P("tensor", None),
        ),
        check_vma=False,
    )
```

```python
import functools

import jax
import jax.numpy as jnp
from jax import lax
from jax.experimental import pallas as pl
from jax.experimental.pallas import tpu as pltpu
from jax.sharding import PartitionSpec as P

SHORT = 1024
LONG = 2048
VMEM_LIMIT = 58 * 1024 * 1024
VMEM_LAST = 24 * 1024 * 1024
epsilon = 1e-06
BF16 = jnp.bfloat16
F32 = jnp.float32


def rms_norm(values, gain):
    return values * lax.rsqrt(jnp.mean(values * values, axis=-1, keepdims=True) + epsilon) * gain


def contract(left, right, dims):
    return lax.dot_general(left, right, ((dims[:1], dims[1:]), ((), ())), preferred_element_type=F32)


def combine(before_pair, after_pair):
    return (before_pair[0] * after_pair[0], after_pair[0] * before_pair[1] + after_pair[1])


def row_facts(long_rows, short_rows, chunk):
    long_count, short_count = long_rows[0], short_rows[0]
    in_long = chunk < 2 * long_count
    in_row = chunk < 2 * long_count + short_count
    second = in_long & (chunk % 2 == 1)
    ends = in_row & (second | ~in_long)
    slot = jnp.where(in_long, chunk // 2, chunk - long_count)
    return in_row, second, ends, slot


def pair_swap(values, count):
    return lax.ppermute(values, "tensor", [(i, i ^ 1) for i in range(count)])


def plain(
    block_input, long_rows, short_rows, prev_states, norm1_gain, conv_weight, mixer_weight, gate_bias,
    out_weight, norm2_gain, up_weight, down_weight, cotangent,
):
    tokens, width = block_input.shape
    parts = lax.axis_size("tensor")
    me = lax.axis_index("tensor")
    rim = conv_weight.shape[0] - 1
    in_row, second, ends, slot = row_facts(long_rows, short_rows, me)
    mask = in_row.astype(F32)
    joined = second.astype(F32)
    even = (me % 2 == 0).astype(F32)
    slots = jnp.arange(prev_states.shape[0], dtype=jnp.int32)
    first_half = in_row & ~ends

    mixer_full = lax.all_gather(mixer_weight.astype(BF16), "tensor", axis=2, tiled=True)
    out_full = lax.all_gather(out_weight.astype(BF16), "tensor", axis=0, tiled=True)
    up_full = lax.all_gather(up_weight.astype(BF16), "tensor", axis=1, tiled=True)
    down_full = lax.all_gather(down_weight.astype(BF16), "tensor", axis=0, tiled=True)
    bias = lax.all_gather(gate_bias, "tensor", axis=0, tiled=True)
    prev = lax.all_gather(prev_states, "tensor", axis=1, tiled=True)
    start_state = jnp.sum(
        jnp.where((slots == slot)[:, None] & in_row & ~second, prev, 0.0), axis=0, keepdims=True
    )

    normed, norm1_back = jax.vjp(rms_norm, block_input, norm1_gain)
    rim_rows = pair_swap(normed[tokens - rim :], parts) * joined

    def convolve(extended, weight):
        total = weight[0] * extended[rim:]
        for tap in range(1, rim + 1):
            total = total + mask * weight[tap] * extended[rim - tap : rim - tap + tokens]
        return total

    conv_out, conv_back = jax.vjp(convolve, jnp.concatenate([rim_rows, normed], 0), conv_weight)
    conv_low = conv_out.astype(BF16)
    gate = contract(conv_low, mixer_full[0], (1, 0))
    cand = contract(conv_low, mixer_full[1], (1, 0))
    logit = gate + bias
    keep = jax.nn.sigmoid(-logit)
    opened = jax.nn.sigmoid(logit)
    soft = jax.nn.softplus(cand)
    factors, values = lax.associative_scan(combine, (keep, opened * soft), axis=0)
    ending = factors[-1:] * start_state + values[-1:]
    carry = start_state + joined * pair_swap(ending, parts)
    states = values + factors * carry
    before = jnp.concatenate([carry, states[:-1]], 0)
    end_table = jnp.where((slots == slot) & ends, 1.0, 0.0)[:, None]
    finals = lax.psum_scatter(end_table * states[-1:], "tensor", scatter_dimension=1, tiled=True)
    state_low = states.astype(BF16)
    mixed = contract(state_low, out_full, (1, 0))
    resid = block_input + mask * mixed
    normed_two, norm2_back = jax.vjp(rms_norm, resid, norm2_gain)
    normed_low = normed_two.astype(BF16)
    grad_branch = (mask * cotangent).astype(BF16)
    upward = contract(normed_low, up_full, (1, 0))
    activation, gelu_back = jax.vjp(lambda v: jax.nn.gelu(v, approximate=True), upward)
    activation_low = activation.astype(BF16)
    output = resid + mask * contract(activation_low, down_full, (1, 0))
    grad_act = contract(grad_branch, down_full, (1, 1))
    grad_up = gelu_back(grad_act)[0].astype(BF16)
    grad_norm_two = contract(grad_up, up_full, (1, 1))
    up_grad = contract(normed_low, grad_up, (0, 0))
    down_grad = contract(activation_low, grad_branch, (0, 0))
    grad_resid_norm, gain_two_part = norm2_back(grad_norm_two)
    grad_resid = cotangent + grad_resid_norm
    grad_mixed = (mask * grad_resid).astype(BF16)
    out_grad = contract(state_low, grad_mixed, (0, 0))
    grad_states = contract(grad_mixed, out_full, (1, 1))
    later_keep = jnp.concatenate([keep[1:], jnp.ones_like(keep[:1])], 0)
    back_factors, back_values = lax.associative_scan(combine, (later_keep, grad_states), axis=0, reverse=True)
    joins_next = (first_half & (me % 2 == 0)).astype(F32)
    back_carry = joins_next * pair_swap(keep[:1] * back_values[:1], parts)
    carried = back_values + back_factors * back_carry
    grad_logit = carried * (soft - before) * opened * (1 - opened)
    grad_cand = carried * opened * jax.nn.sigmoid(cand)
    bias_part = jnp.sum(grad_logit, axis=0)
    grad_logit_low = grad_logit.astype(BF16)
    grad_cand_low = grad_cand.astype(BF16)
    mixer_grad = jnp.stack([contract(conv_low, grad_logit_low, (0, 0)), contract(conv_low, grad_cand_low, (0, 0))])
    grad_conv = contract(grad_logit_low, mixer_full[0], (1, 1)) + contract(grad_cand_low, mixer_full[1], (1, 1))
    grad_extended, taps_part = conv_back(grad_conv)
    returned = joins_next * pair_swap(joined * grad_extended[:rim], parts)
    grad_normed = grad_extended[rim:] + jnp.concatenate(
        [jnp.zeros((tokens - rim, width), F32), returned], 0
    )
    grad_input_norm, gain_one_part = norm1_back(grad_normed)
    input_grad = grad_resid + grad_input_norm

    def scatter(grad, dim):
        return lax.psum_scatter(grad.astype(BF16), "tensor", scatter_dimension=dim, tiled=True)

    sharded = (
        scatter(mixer_grad, 2), scatter(out_grad, 0), scatter(up_grad, 1), scatter(down_grad, 0),
    )
    summed = tuple(g.astype(F32) for g in lax.psum(sharded, "dp"))
    shared = lax.psum((gain_one_part, taps_part, gain_two_part, bias_part), ("dp", "tensor"))
    channels = gate_bias.shape[0]
    bias_grad = lax.dynamic_slice_in_dim(shared[3], me * channels, channels)
    return (
        output, finals, input_grad, shared[0], shared[1], summed[0], bias_grad, summed[1], shared[2], summed[2], summed[3],
    )


LANES = 8
MESH = pl.DeviceIdType.MESH
CHUNKS = (4, 2, 1, 4)
WIRES = 256
SCHEDULE = {
    "own": (("g", "mix", "far", 0),),
    "gm": (("g", "mix", "far", 1),),
    "mixfar!": (("g", "out", "far", 0), ("g", "mix", "across", 0), ("g", "up", "far", 0), ("g", "mix", "across", 1)),
    "scan2": (("g", "out", "across", 0), ("g", "up", "far", 1)),
    "end!": (("g", "down", "far", 0), ("g", "up", "across", 0)),
    "states": (("g", "down", "far", 1), ("g", "up", "across", 1)),
    "updown!": (("g", "down", "across", 0), ("g", "down", "across", 1)),
    "f1u": (("up", "y", 0), ("up", "y", 1), ("up", "y", 2), ("up", "y", 3)),
    "f1d": (("down", "xa", 1, 0), ("down", "xa", 1, 1)),
    "f3a": (("down", "ya", 0),),
    "f3u": (("up", "x", 0), ("up", "x", 1), ("down", "ya", 1)),
    "f3d": (("up", "x", 2), ("down", "xa", 0, 0), ("down", "xa", 0, 1)),
    "og1": (("up", "z", 0), ("up", "x", 3)),
    "r1g": (("up", "z", 1),),
    "r1s": (("up", "z", 2),),
    "r1w!": (("out", "y", 0), ("up", "zb", 0)),
    "r1k0": (("down", "z", 0),),
    "r1w0": (("up", "zb", 1),),
    "r1w1": (("up", "zb", 2),),
    "r1e0": (("down", "z", 1), ("up", "xb", 0)),
    "r1e1": (("up", "z", 3),),
    "r0s": (("mix", "y", 0), ("mix", "y", 1), ("mix", "y", 2), ("down", "zb", 0), ("mix", "y", 3), ("out", "x", 0)),
    "r0w!": (("up", "xb", 1), ("up", "xb", 2)),
    "r0w1": (("down", "zb", 1),),
    "r0e0": (("out", "z", 0),),
    "r0e1": (("up", "zb", 3),),
    "halo!": (("mix", "x", 0), ("mix", "x", 1), ("down", "xb", 0)),
    "n1a": (("mix", "x", 2),),
    "drain": (("mix", "z", 0), ("down", "xb", 1), ("mix", "x", 3), ("mix", "z", 1), ("pk", "chip"), ("out", "zb", 0), ("pk", "x"), ("up", "xb", 3), ("mix", "z", 2), ("mix", "zb", 0), ("mix", "zb", 1), ("mix", "z", 3), ("pk", "z"), ("out", "xb", 0), ("mix", "zb", 2), ("mix", "xb", 0), ("mix", "xb", 1), ("mix", "zb", 3), ("mix", "xb", 2), ("mix", "xb", 3)),
}
GELU_A = 0.7978845608028654
GELU_B = 0.044715


def dot(left, right, dims=(1, 0)):
    return lax.dot_general(left, right, ((dims[:1], dims[1:]), ((), ())), preferred_element_type=F32)


def rows_of(block, width):
    return block.reshape(-1, width)


class Wires:
    def __init__(self, send, recv):
        self.send, self.recv, self.used = send, recv, 0

    def copy(self, src, dst, device):
        k = self.used
        self.used += 1
        return pltpu.make_async_remote_copy(
            src_ref=src, dst_ref=dst, send_sem=self.send.at[k], recv_sem=self.recv.at[k],
            device_id=device, device_id_type=MESH,
        )


def block_kernel(
    sizes, long_ref, short_ref, x_hbm, cot_hbm, prev_ref, bias_ref, gain1_ref, taps_ref, gain2_ref, mix_hbm, outw_hbm, up_hbm,
    down_hbm,
    cb, xb, finals_ref, small_ref, fin_up, fin_down, fin_out, fin_mix,
    n1h, res, gn2, fo, conv, n2, gm, act, gup, sig, st, ab, sp, sl,
    mix, outw, up, down,
    p_up, p_down, p_out,
    rc_up, ry_up, kx_up, rx_up, rz_up,
    rc_down, ry_down, kx_down, rx_down, rz_down,
    rc_out, ry_out, kx_out, rx_out, rz_out,
    ry_mix, kx_mix, rx_mix, rz_mix,
    prev, biases, halo1, halo2, endrow, endin, brow, bin_, fsend, frecv,
    acc_n1, acc_n2, acc_t, acc_b, pk, pk_core, pk_chip, pk_x, pk_z,
    send_sem, recv_sem, local_sem,
):
    n, z_count, tokens, width, hs, fs, slots, rim = sizes
    chips = n // 2
    steps = tokens // LANES
    tile = 256
    tiles = tokens // tile
    half_tiles = tiles // 2
    me = lax.axis_index("tensor")
    q, c = me // 2, me % 2
    dp = lax.axis_index("dp")
    z, x = dp // 2, dp % 2
    wires = Wires(send_sem, recv_sem)
    started = []

    def tensor(j):
        return (dp, j)

    sibling = tensor(me + 1 - 2 * c)
    partner = (dp + 1 - 2 * x, me)

    def z_peer(d):
        return ((((z + d) % z_count) * 2) + x, me)

    def shard_of(d, core):
        return ((q + d) % chips) * 2 + core

    def go(copy):
        copy.start()
        started.append(copy)
        return copy

    locals_ = [
        (mix_hbm.at[0], ab.at[0, pl.ds(0, width)]), (mix_hbm.at[1], ab.at[0, pl.ds(width, width)]),
        (outw_hbm, gn2.at[pl.ds(0, hs)]), (up_hbm, fo.at[pl.ds(0, width)]), (down_hbm, fo.at[pl.ds(width, fs)]),
    ]
    loads = [pltpu.make_async_copy(s, d, local_sem.at[i]) for i, (s, d) in enumerate(locals_)]

    def run(ref, g):
        return ref.at[pl.ds(g * steps, steps)]

    x_loads = [pltpu.make_async_copy(run(x_hbm, g), xb.at[:, g, :], local_sem.at[5 + g]) for g in range(LANES)]
    cot_loads = [pltpu.make_async_copy(run(cot_hbm, g), cb.at[:, g, :], local_sem.at[5 + LANES + g]) for g in range(LANES)]
    for copy in loads[:2] + x_loads + loads[2:] + cot_loads:
        copy.start()

    barrier = pltpu.get_barrier_semaphore()
    peers = [tensor((me + d) % n) for d in range(1, n)] + [partner] + [z_peer(d) for d in range(1, z_count)]
    for peer in peers:
        pl.semaphore_signal(barrier, inc=1, device_id=peer, device_id_type=MESH)

    long_count, short_count = long_ref[0], short_ref[0]
    is_long = jnp.where(me < 2 * long_count, 1.0, 0.0)
    in_row = jnp.where(me < 2 * long_count + short_count, 1.0, 0.0)
    odd = (me % 2).astype(F32)
    joined = is_long * odd
    joins_next = is_long * (1.0 - odd)
    starts = in_row * (1.0 - joined)
    ends = in_row * (1.0 - joins_next)
    slot = jnp.where(me < 2 * long_count, me // 2, me - long_count)
    slot_mask = [jnp.where(slot == s, 1.0, 0.0) for s in range(slots)]

    gathers = {}

    def gather(name, ref):
        size = ref.shape[1] // 2
        far, across, passed = [], [], []
        for k in range(size):
            mine, r = ref.at[me, x * size + k], shard_of(1, c)
            ours, theirs = ref.at[r, x * size + k], ref.at[r, (1 - x) * size + k]
            far.append(go(wires.copy(mine, mine, tensor(r))))
            across.append(wires.copy(ours, ours, partner))
            passed.append((wires.copy(ours, ours, sibling), wires.copy(theirs, theirs, sibling)))
        sib = go(wires.copy(ref.at[me], ref.at[me], sibling))
        gathers[name] = (sib, far, across, passed)

    def gather_far(name, k):
        _, far, across, passed = gathers[name]
        far[k].wait_recv()
        go(across[k])
        go(passed[k][0])

    def gather_across(name, k):
        _, far, across, passed = gathers[name]
        across[k].wait_recv()
        go(passed[k][1])

    def gather_passed(name):
        for one, two in gathers[name][3]:
            one.wait_recv()
            two.wait_recv()

    stages = {("g", "far"): gather_far, ("g", "across"): gather_across}

    def run_stages(hook):
        for step in SCHEDULE.get(hook, ()):
            if step[0] == "g":
                stages["g", step[2]](step[1], *step[3:])
            else:
                stages[step[:2]](*step[2:])

    prev[me] = prev_ref[...]
    biases[me] = bias_ref[...]
    loads[0].wait()
    loads[1].wait()
    half = width // 2
    for h in range(2):
        mix[me, pl.ds(2 * h, 2)] = (
            jnp.concatenate([ab[0, pl.ds(h * half, half), :], ab[0, pl.ds(width + h * half, half), :]], axis=1)
            .astype(BF16)
            .reshape((2,) + mix.shape[2:])
        )
    pl.semaphore_wait(barrier, len(peers))
    gather("mix", mix)
    lead_copies = []
    for ref in (prev, biases):
        lead_copies += [go(wires.copy(ref.at[me], ref.at[me], tensor((me + d) % n))) for d in range(1, n)]
    loads[2].wait()
    outw[me] = gn2[pl.ds(0, hs), :].astype(BF16).reshape(2, hs // 2, width)
    gather("out", outw)
    loads[3].wait()
    up[me] = fo[pl.ds(0, width), :].astype(BF16).reshape(up.shape[1:])
    gather("up", up)
    loads[4].wait()
    down[me] = fo[pl.ds(width, fs), :].astype(BF16).reshape(down.shape[1:])
    gather("down", down)

    span = 64
    spans = tokens // span

    def at(i, shift=0, size=span):
        return pl.ds(pl.multiple_of(i * size + shift, LANES), size)

    def take(ref, i, size=span):
        return ref[pl.ds(i * (size // LANES), size // LANES)].reshape(size, width)

    def put(ref, i, value):
        ref[pl.ds(i * (span // LANES), span // LANES)] = value.reshape(span // LANES, LANES, width)

    def eights(value):
        return jnp.sum(value.reshape(-1, LANES, value.shape[-1]), axis=0)

    hook = run_stages
    for copy in x_loads:
        copy.wait()
    gain1 = gain1_ref[...]
    gain2 = gain2_ref[...]

    @pl.loop(0, spans, unroll=4)
    def _(i):
        v = take(xb, i)
        scale = lax.rsqrt(jnp.mean(v * v, axis=-1, keepdims=True) + epsilon)
        n1h[at(i, rim * LANES), :] = v * scale * gain1

    hook("norm1")
    edge = rim * LANES
    halo_copy = go(wires.copy(n1h.at[pl.ds(tokens, edge)], halo1, sibling))
    halo_copy.wait_recv()
    sub = lax.broadcasted_iota(jnp.int32, (LANES, width), 0)
    for k in range(rim):
        own = pltpu.roll(n1h[pl.ds(tokens + k * LANES, LANES), :], 1, 0)
        other = pltpu.roll(halo1[pl.ds(k * LANES, LANES), :], 1, 0)
        n1h[pl.ds(k * LANES, LANES), :] = jnp.where(sub == 0, joined * other, own)
    tap = [taps_ref[pl.ds(k, 1), :] * (1.0 if k == 0 else in_row) for k in range(rim + 1)]

    @pl.loop(0, spans, unroll=4)
    def _(i):
        total = tap[0] * n1h[at(i, edge), :]
        for k in range(1, rim + 1):
            total = total + tap[k] * n1h[at(i, edge - k * LANES), :]
        conv[at(i), :] = total.astype(BF16)

    def project(j):
        weight = rows_of(mix[j], 2 * hs)
        bias = biases[j]

        @pl.loop(0, tiles, unroll=tiles)
        def _(t):
            rows = at(t, 0, tile)
            pre = dot(conv[rows, :], weight)
            logit = pre[:, :hs] + bias
            cand = pre[:, hs:]
            e = jnp.exp(-jnp.abs(logit))
            r = 1.0 / (1.0 + e)
            opened = jnp.where(logit >= 0, r, e * r)
            keep = jnp.where(logit >= 0, e * r, r)
            soft = jnp.maximum(cand, 0.0) + jnp.log1p(jnp.exp(-jnp.abs(cand)))
            sig[j, rows, :] = opened
            sp[j, rows, :] = soft
            ab[j, rows, :] = keep * in_row
            st[j, at(t, LANES, tile), :] = opened * soft

    hook("conv")
    for copy in lead_copies:
        copy.wait_recv()
    project(me)
    hook("own")
    gathers["mix"][0].wait_recv()
    project(me + 1 - 2 * c)
    hook("sib")

    def unrolled(count, step, carry, by=4):
        def some(i, carry):
            for k in range(by):
                carry = step(i * by + k, carry)
            return carry

        return lax.fori_loop(0, count // by, some, carry)

    one = jnp.ones((LANES, hs), F32)
    zero = jnp.zeros((LANES, hs), F32)

    def scan(js):
        def step(s, carry):
            rows = at(s, 0, LANES)
            later = at(s, LANES, LANES)
            out = []
            for j, (fac, val) in zip(js, carry):
                a = ab[j, rows, :]
                fac = a * fac
                val = a * val + st[j, later, :]
                ab[j, rows, :] = fac
                st[j, later, :] = val
                out.append((fac, val))
            return tuple(out)

        unrolled(steps, step, tuple((one, zero) for _ in js))

    scan([me, me + 1 - 2 * c])
    hook("scan1")
    for copy in cot_loads:
        copy.wait()

    @pl.loop(0, spans, unroll=4)
    def _(i):
        gm[at(i), :] = (in_row * take(cb, i)).astype(BF16)

    hook("gm")
    hook("mixfar!")
    project(shard_of(1, c))
    hook("rown")
    hook("mixpass!")
    gather_passed("mix")
    project(shard_of(1, 1 - c))
    hook("rsib")
    scan([shard_of(1, c), shard_of(1, 1 - c)])
    hook("scan2")
    last = pl.ds(tokens - LANES, LANES)

    def chain(j, carry, keep_rows):
        fac = ab[j, last, :]
        val = st[j, pl.ds(tokens, LANES), :]
        rows = []
        for g in range(LANES):
            rows.append(carry)
            carry = fac[g : g + 1] * carry + val[g : g + 1]
        if keep_rows:
            st[j, pl.ds(0, LANES), :] = jnp.concatenate(rows, axis=0)
        return carry

    first = []
    for j in range(n):
        begin = jnp.zeros((1, hs), F32)
        for s in range(slots):
            begin = begin + (starts * slot_mask[s]) * prev[j, pl.ds(s, 1), :]
        first.append(begin)
        endrow[j] = chain(j, begin, False)
    end_copy = go(wires.copy(endrow, endin, sibling))
    hook("chain")
    hook("end!")
    end_copy.wait_recv()
    for j in range(n):
        ending = chain(j, first[j] + joined * endin[j], True)
        for s in range(slots):
            fsend[j, pl.ds(s, 1), :] = (ends * slot_mask[s]) * ending
    final_copies = [
        go(wires.copy(fsend.at[(me + d) % n], frecv.at[d - 1], tensor((me + d) % n))) for d in range(1, n)
    ]

    hook("chain2")
    hook("out!")
    gathers["out"][0].wait_recv()
    gather_passed("out")
    @pl.loop(0, tiles, unroll=tiles)
    def _(t):
        rows = at(t, 0, tile)
        mixed = jnp.zeros((tile, width), F32)
        for j in range(n):
            into = st[j, pl.ds(0, LANES), :]
            value = st[j, at(t, LANES, tile), :] + (
                ab[j, rows, :].reshape(-1, LANES, hs) * into[None]
            ).reshape(tile, hs)
            st[j, at(t, LANES, tile), :] = value
            low = value.astype(BF16)
            sl[j, rows, :] = low
            mixed = mixed + dot(low, rows_of(outw[j], width))
        resid = take(xb, t, tile) + in_row * mixed
        res[rows, :] = resid
        scale = lax.rsqrt(jnp.mean(resid * resid, axis=-1, keepdims=True) + epsilon)
        n2[rows, :] = (resid * scale * gain2).astype(BF16)

    hook("states")
    hook("updown!")
    gather_passed("up")
    gather_passed("down")
    gathers["up"][0].wait_recv()
    gathers["down"][0].wait_recv()
    sent_weights = list(started)

    class Sum:
        def __init__(self, part, rc, ry, kx, rx, rz, fin):
            self.part, self.rc, self.ry, self.kx, self.rx, self.rz, self.fin = part, rc, ry, kx, rx, rz, fin
            self.chunks = fin.shape[0]
            self.c1 = [None] * chips
            self.c2, self.c3, self.c4, self.c5, self.c6 = {}, {}, {}, {}, {}
            self.first = wires.used
            wires.used += chips

        def one(self, d):
            copy = pltpu.make_async_remote_copy(
                src_ref=self.part.at[shard_of(d, 1 - c)], dst_ref=self.rc.at[d], send_sem=send_sem.at[self.first + d],
                recv_sem=recv_sem.at[self.first + d], device_id=sibling, device_id_type=MESH,
            )
            self.c1[d] = go(copy)

        def both(self, j, d, k, h):
            return self.part[j, k, h].astype(F32) + self.rc[d, k, h].astype(F32)

        def y(self, k=0):
            self.c2[k] = []
            for d in range(1, chips):
                if k == 0:
                    self.c1[d].wait_recv()
                j = shard_of(d, c)
                for h in range(2):
                    self.part[j, k, h] = self.both(j, d, k, h).astype(BF16)
                self.c2[k].append(go(wires.copy(self.part.at[j, k], self.ry.at[d - 1, k], tensor(j))))

        def total(self, k, h):
            v = self.both(me, 0, k, h)
            for d in range(chips - 1):
                v = v + self.ry[d, k, h].astype(F32)
            return v

        def x(self, k=0):
            if k == 0:
                self.c1[0].wait_recv()
            for copy in self.c2[k]:
                copy.wait_recv()
            self.part[me, k, 1 - x] = self.total(k, 1 - x).astype(BF16)
            self.c3[k] = go(wires.copy(self.part.at[me, k, 1 - x], self.rx.at[k], partner))
            self.kx[k] = self.total(k, x)

        def z(self, k=0):
            self.c3[k].wait_recv()
            self.spread(k, self.kx[k] + self.rx[k].astype(F32))

        def spread(self, k, v):
            self.kx[k] = v
            self.part[me, k, x] = v.astype(BF16)
            self.c4[k] = [
                go(wires.copy(self.part.at[me, k, x, (z + d) % z_count], self.rz.at[d - 1, k], z_peer(d)))
                for d in range(1, z_count)
            ]

        def zb(self, k=0):
            for copy in self.c4[k]:
                copy.wait_recv()
            v = self.kx[k, z]
            for d in range(z_count - 1):
                v = v + self.rz[d, k].astype(F32)
            self.fin[k, x, z] = v.astype(BF16)
            mine = self.fin.at[k, x, z]
            self.c5[k] = [go(wires.copy(mine, mine, z_peer(d))) for d in range(1, z_count)]
            self.c6[k] = [go(wires.copy(mine, mine, partner))]

        def xb(self, k=0):
            for d in range(1, z_count):
                self.c5[k][d - 1].wait_recv()
                theirs = self.fin.at[k, x, (z + z_count - d) % z_count]
                self.c6[k].append(go(wires.copy(theirs, theirs, partner)))

        def end(self):
            for k in range(self.chunks):
                for copy in self.c6[k]:
                    copy.wait_recv()

    class SumAcross(Sum):
        def xa(self, d, k=0):
            if k == 0:
                self.c1[d].wait_recv()
            j = shard_of(d, c)
            self.part[j, k, 1 - x] = self.both(j, d, k, 1 - x).astype(BF16)
            self.c3[d, k] = go(wires.copy(self.part.at[j, k, 1 - x], self.rx.at[d, k], partner))

        def ya(self, k=0):
            self.c3[1, k].wait_recv()
            j = shard_of(1, c)
            self.part[j, k, x] = (self.both(j, 1, k, x) + self.rx[1, k].astype(F32)).astype(BF16)
            self.c2[k] = go(wires.copy(self.part.at[j, k, x], self.ry.at[k], tensor(j)))

        def z(self, k=0):
            self.c3[0, k].wait_recv()
            self.c2[k].wait_recv()
            self.spread(k, self.both(me, 0, k, x) + self.rx[0, k].astype(F32) + self.ry[k].astype(F32))

    s_up = Sum(p_up, rc_up, ry_up, kx_up, rx_up, rz_up, fin_up)
    s_down = SumAcross(p_down, rc_down, ry_down, kx_down, rx_down, rz_down, fin_down)
    s_out = Sum(p_out, rc_out, ry_out, kx_out, rx_out, rz_out, fin_out)
    s_mix = Sum(up, down, ry_mix, kx_mix, rx_mix, rz_mix, fin_mix)

    for name, unit in (("up", s_up), ("down", s_down), ("out", s_out), ("mix", s_mix)):
        for stage in ("y", "x", "xa", "ya", "z", "zb", "xb"):
            stages[name, stage] = getattr(unit, stage, None)

    def weight_grad(unit, j, left, right):
        unit.part[j] = dot(left, right, (0, 0)).astype(BF16).reshape(unit.part.shape[1:])

    def feed(j, begin, name, d=None):
        def some(t):
            rows = at(t, 0, tile)
            upw = rows_of(up[j], fs)
            downw = rows_of(down[j], width)
            u = dot(n2[rows, :], upw)
            ga = dot(gm[rows, :], downw, (1, 1))
            u2 = u * u
            th = jnp.tanh(GELU_A * u * (1.0 + GELU_B * u2))
            hp = 0.5 + 0.5 * th
            a = (u * hp).astype(BF16)
            slope = hp + (0.5 * GELU_A) * u * (1.0 - th * th) * (1.0 + 3.0 * GELU_B * u2)
            gu = (ga * slope).astype(BF16)
            act[rows, :] = a
            gup[rows, :] = gu
            o = dot(a, downw)
            g = dot(gu, upw, (1, 1))
            if begin:
                fo[rows, :] = o
                gn2[rows, :] = g
            else:
                fo[rows, :] = fo[rows, :] + o
                gn2[rows, :] = gn2[rows, :] + g

        pl.loop(0, half_tiles, unroll=half_tiles)(some)
        hook(name + "a")
        pl.loop(half_tiles, tiles, unroll=half_tiles)(some)
        hook(name + "b")
        for unit, left, right, end in ((s_up, n2, gup, "u"), (s_down, gm, act, "d")):
            weight_grad(unit, j, left[...], right[...])
            if d is not None:
                unit.one(d)
            hook(name + end)

    feed(shard_of(1, 1 - c), True, "f0", 1)
    feed(shard_of(1, c), False, "f1")
    feed(me + 1 - 2 * c, False, "f2", 0)
    feed(me, False, "f3")

    acc_n2[...] = jnp.zeros_like(acc_n2)

    def norm2_back(i):
        r = res[at(i), :]
        g = gn2[at(i), :]
        scale = lax.rsqrt(jnp.mean(r * r, axis=-1, keepdims=True) + epsilon)
        gg = g * gain2
        m = jnp.mean(gg * r, axis=-1, keepdims=True)
        gr = take(cb, i) + scale * gg - r * (scale * scale * scale * m)
        acc_n2[...] += eights(g * r * scale)
        gn2[at(i), :] = gr
        gm[at(i), :] = (in_row * gr).astype(BF16)
        put(cb, i, r + in_row * fo[at(i), :])

    pl.loop(0, spans // 2, unroll=2)(norm2_back)
    hook("B1a")
    pl.loop(spans // 2, spans, unroll=2)(norm2_back)
    hook("B1b")

    def store(ref, hbm, first):
        copies = [pltpu.make_async_copy(ref.at[:, g, :], run(hbm, g), local_sem.at[first + g]) for g in range(LANES)]
        for copy in copies:
            copy.start()
        return copies

    for copy in sent_weights:
        copy.wait_send()
        started.remove(copy)

    for d in (1, 0):
        for core in (1 - c, c):
            j = shard_of(d, core)
            weight_grad(s_out, j, gm[...], sl[j])
        s_out.one(d)
        hook(f"og{d}")

    for j in range(n):
        acc_b[j] = jnp.zeros((LANES, hs), F32)

    def recur_back(d, begin, name):
        js = [shard_of(d, core) for core in range(2)]
        for k in range(2):
            ab[k] = dot(gm[...], rows_of(outw[js[k]], width), (1, 1))
        hook(name + "g")

        def back_step(i, carry):
            s = steps - 1 - i
            rows = at(s, 0, LANES)
            out = []
            for k in range(2):
                fac, val, keep = carry[k]
                fac = keep * fac
                val = ab[k, rows, :] + keep * val
                ab[2 + k, rows, :] = fac
                ab[k, rows, :] = val
                out.append((fac, val, 1.0 - sig[js[k], rows, :]))
            return tuple(out)

        unrolled(steps, back_step, ((one, zero, one), (one, zero, one)))
        hook(name + "s")

        def chain_back(k, carry):
            fac = ab[2 + k, pl.ds(0, LANES), :]
            val = ab[k, pl.ds(0, LANES), :]
            keep = 1.0 - sig[js[k], pl.ds(0, LANES), :]
            rows = []
            for g in reversed(range(LANES)):
                rows.append(carry)
                carry = keep[g : g + 1] * (val[g : g + 1] + fac[g : g + 1] * carry)
            return carry, jnp.concatenate(rows[::-1], axis=0)

        slot_ = 2 * d
        for k in range(2):
            brow[slot_ + k] = chain_back(k, jnp.zeros((1, hs), F32))[0]
        copy = go(wires.copy(brow.at[pl.ds(slot_, 2)], bin_.at[pl.ds(slot_, 2)], sibling))
        hook(name + "c")
        hook(name + "w!")
        copy.wait_recv()
        grads = (act, gup)
        for k in (0, 1):
            j = js[k]
            into = chain_back(k, joins_next * bin_[slot_ + k])[1]

            @pl.loop(0, tiles, unroll=tiles)
            def _(t, j=j, k=k, into=into):
                rows = at(t, 0, tile)
                carried = ab[k, rows, :] + (ab[2 + k, rows, :].reshape(-1, LANES, hs) * into[None]).reshape(tile, hs)
                opened = sig[j, rows, :]
                soft = sp[j, rows, :]
                weighted = carried * opened
                gl = weighted * (soft - st[j, rows, :]) * (1.0 - opened)
                close = jnp.where(soft < 0.01, soft * (1.0 - soft * (0.5 - soft * (1.0 / 6.0))), 1.0 - jnp.exp(-soft))
                gc = weighted * close
                acc_b[j] += eights(gl)
                grads[k][rows, :] = jnp.concatenate([gl.astype(BF16), gc.astype(BF16)], axis=1)

            hook(f"{name}k{k}")
            weight_grad(s_mix, j, conv[...], grads[k][...])
            if k == 0:
                hook(name + "w0")
        s_mix.one(d)
        hook(name + "w1")

        def gather_back(t):
            rows = at(t, 0, tile)
            back = dot(act[rows, :], rows_of(mix[js[0]], 2 * hs), (1, 1)) + dot(gup[rows, :], rows_of(mix[js[1]], 2 * hs), (1, 1))
            res[rows, :] = back if begin else res[rows, :] + back

        pl.loop(0, half_tiles, unroll=half_tiles)(gather_back)
        hook(name + "e0")
        pl.loop(half_tiles, tiles, unroll=half_tiles)(gather_back)
        hook(name + "e1")

    recur_back(1, True, "r1")
    recur_back(0, False, "r0")
    halo_back = go(wires.copy(res.at[pl.ds(0, edge)], halo2, sibling))
    hook("halo!")
    halo_back.wait_recv()

    for k in range(rim):
        own = pltpu.roll(res[pl.ds(k * LANES, LANES), :], LANES - 1, 0)
        other = pltpu.roll(halo2[pl.ds(k * LANES, LANES), :], LANES - 1, 0)
        res[pl.ds(tokens + k * LANES, LANES), :] = jnp.where(sub == LANES - 1, joins_next * other, own)
    acc_n1[...] = jnp.zeros_like(acc_n1)
    acc_t[...] = jnp.zeros_like(acc_t)

    def norm1_back(i):
        g0 = res[at(i), :]
        total = tap[0] * g0
        acc_t[0] += eights(g0 * n1h[at(i, edge), :])
        for k in range(1, rim + 1):
            total = total + tap[k] * res[at(i, k * LANES), :]
            acc_t[k] += eights(g0 * n1h[at(i, edge - k * LANES), :])
        v = take(xb, i)
        scale = lax.rsqrt(jnp.mean(v * v, axis=-1, keepdims=True) + epsilon)
        gg = total * gain1
        m = jnp.mean(gg * v, axis=-1, keepdims=True)
        acc_n1[...] += eights(total * v * scale)
        put(xb, i, gn2[at(i), :] + scale * gg - v * (scale * scale * scale * m))

    pl.loop(0, spans // 2, unroll=2)(norm1_back)
    hook("n1a")
    pl.loop(spans // 2, spans, unroll=2)(norm1_back)
    hook("n1b")

    pk[...] = jnp.zeros_like(pk)
    pk[pl.ds(0, 1), :] = jnp.sum(acc_n1[...], axis=0, keepdims=True)
    for k in range(rim + 1):
        pk[pl.ds(1 + k, 1), :] = jnp.sum(acc_t[k], axis=0, keepdims=True)
    pk[pl.ds(6, 1), :] = jnp.sum(acc_n2[...], axis=0, keepdims=True)
    for j in range(n):
        pk[pl.ds(8 + j, 1), pl.ds(0, hs)] = jnp.sum(acc_b[j], axis=0, keepdims=True)
    k1 = go(wires.copy(pk, pk_core, sibling))
    small_copies = {}

    def small_chip():
        k1.wait_recv()
        pk_chip[q] = pk[...] + pk_core[...]
        small_copies[2] = go(wires.copy(pk_chip.at[q], pk_chip.at[q], tensor(shard_of(1, c))))

    def small_x():
        small_copies[2].wait_recv()
        pk_x[0] = pk_chip[0] + pk_chip[1]
        small_copies[3] = go(wires.copy(pk_x.at[0], pk_x.at[1], partner))

    def small_z():
        small_copies[3].wait_recv()
        pk_z[z] = pk_x[0] + pk_x[1]
        small_copies[4] = [go(wires.copy(pk_z.at[z], pk_z.at[z], z_peer(d))) for d in range(1, z_count)]

    stages["pk", "chip"], stages["pk", "x"], stages["pk", "z"] = small_chip, small_x, small_z
    hook("pk")
    hook("drain")
    for copy in final_copies:
        copy.wait_recv()
    total = fsend[me]
    for d in range(n - 1):
        total = total + frecv[d]
    finals_ref[...] = total
    for copy in small_copies[4]:
        copy.wait_recv()
    value = pk_z[0]
    for k in range(1, z_count):
        value = value + pk_z[k]
    small_ref[...] = value
    for unit in (s_up, s_down, s_out, s_mix):
        unit.end()
    for copy in started:
        copy.wait_send()


def last_kernel(
    hs, output_in, igrad_in, finals_in, small, g_up, g_down, g_out, g_mix,
    output, finals, igrad, gain1, taps, mixer, bias, outw, gain2, up, down, mixer_v, outw_v, up_v, down_v, sem,
):
    width = up_v.shape[0]
    steps = output_in.shape[0]
    later = []
    for k, (src, dst) in enumerate(((output_in, output), (igrad_in, igrad))):
        for g in range(LANES):
            later.append(pltpu.make_async_copy(src.at[:, g, :], dst.at[pl.ds(g * steps, steps)], sem.at[8 + k * LANES + g]))
            later[-1].start()
    me = lax.axis_index("tensor")
    up_v[...] = rows_of(g_up[...], up_v.shape[1]).astype(F32)
    later.append(pltpu.make_async_copy(up_v, up, sem.at[2]))
    later[-1].start()
    both = rows_of(g_mix[...], 2 * hs).astype(F32)
    mixer_v[0] = both[:, :hs]
    mixer_v[1] = both[:, hs:]
    later.append(pltpu.make_async_copy(mixer_v, mixer, sem.at[5]))
    later[-1].start()
    down_v[...] = rows_of(g_down[...], width).astype(F32).T
    later.append(pltpu.make_async_copy(down_v, down, sem.at[6]))
    later[-1].start()
    outw_v[...] = rows_of(g_out[...], hs).astype(F32).T
    later.append(pltpu.make_async_copy(outw_v, outw, sem.at[7]))
    later[-1].start()
    finals[...] = finals_in[...]
    gain1[...] = small[pl.ds(0, 1), :]
    taps[...] = small[pl.ds(1, taps.shape[0]), :]
    gain2[...] = small[pl.ds(6, 1), :]
    bias[...] = small[pl.ds(8 + me, 1), pl.ds(0, hs)]
    for copy in later:
        copy.wait()


def fused(
    block_input, long_rows, short_rows, prev_states, norm1_gain, conv_weight, mixer_weight, gate_bias,
    out_weight, norm2_gain, up_weight, down_weight, cotangent,
):
    tokens, width = block_input.shape
    n = lax.axis_size("tensor")
    z_count = lax.axis_size("dp") // 2
    chips = n // 2
    slots, hs = prev_states.shape
    fs = up_weight.shape[1]
    rim = conv_weight.shape[0] - 1
    steps = tokens // LANES
    pk_rows = 8 + -(-n // 8) * 8
    units = [(CHUNKS[0], fs), (CHUNKS[1], fs), (CHUNKS[2], hs), (CHUNKS[3], 2 * hs)]

    def block(chunks, cols):
        return (chunks, 2, z_count, width // (2 * z_count * chunks), cols)

    def full(chunks, cols):
        return pltpu.VMEM((n,) + block(chunks, cols), BF16)

    def sums(chunks, cols, across=False):
        dims = block(chunks, cols)
        part = dims[2:]
        return [
            pltpu.VMEM((chips,) + dims, BF16),
            pltpu.VMEM((chunks,) + part if across else (chips - 1,) + dims, BF16),
            pltpu.VMEM((chunks,) + part, F32),
            pltpu.VMEM(((chips, chunks) if across else (chunks,)) + part, BF16),
            pltpu.VMEM((z_count - 1, chunks) + part[1:], BF16),
        ]

    def wide(rows, kind=F32):
        return pltpu.VMEM((rows, width), kind)

    permuted = pltpu.VMEM((steps, LANES, width), F32)
    per_block = pltpu.VMEM((n, tokens, hs), F32)
    scratch = [
        wide(tokens + rim * LANES), wide(tokens + rim * LANES), wide(tokens), wide(tokens),
        wide(tokens, BF16), wide(tokens, BF16), wide(tokens, BF16), pltpu.VMEM((tokens, fs), BF16), pltpu.VMEM((tokens, fs), BF16),
        per_block, pltpu.VMEM((n, tokens + LANES, hs), F32), per_block, per_block, pltpu.VMEM((n, tokens, hs), BF16),
        pltpu.VMEM((n, 4, width // 4, 2 * hs), BF16), pltpu.VMEM((n, 2, hs // 2, width), BF16), full(*units[3]), full(*units[3]),
        *[full(*unit) for unit in units[:3]],
        *sums(*units[0]), *sums(*units[1], True), *sums(*units[2]), *sums(*units[3])[1:],
        pltpu.VMEM((n, slots, hs), F32), pltpu.VMEM((n, 1, hs), F32), wide(rim * LANES), wide(rim * LANES),
        pltpu.VMEM((n, 1, hs), F32), pltpu.VMEM((n, 1, hs), F32), pltpu.VMEM((n, 1, hs), F32), pltpu.VMEM((n, 1, hs), F32),
        pltpu.VMEM((n, slots, hs), F32), pltpu.VMEM((n - 1, slots, hs), F32),
        wide(LANES), wide(LANES), pltpu.VMEM((rim + 1, LANES, width), F32), pltpu.VMEM((n, LANES, hs), F32),
        wide(pk_rows), wide(pk_rows), pltpu.VMEM((chips, pk_rows, width), F32), pltpu.VMEM((2, pk_rows, width), F32),
        pltpu.VMEM((z_count, pk_rows, width), F32),
        pltpu.SemaphoreType.DMA((WIRES,)), pltpu.SemaphoreType.DMA((WIRES,)), pltpu.SemaphoreType.DMA((5 + 4 * LANES,)),
    ]
    vmem = pl.BlockSpec(memory_space=pltpu.VMEM)
    smem = pl.BlockSpec(memory_space=pltpu.SMEM)
    hbm = pl.BlockSpec(memory_space=pl.ANY)

    def shape(dims, kind=F32):
        return jax.ShapeDtypeStruct(dims, kind)

    big = shape((tokens, width))
    outs = pl.pallas_call(
        functools.partial(block_kernel, (n, z_count, tokens, width, hs, fs, slots, rim)),
        out_shape=[permuted, permuted, pltpu.VMEM((slots, hs), F32), pltpu.VMEM((pk_rows, width), F32), *[pltpu.VMEM(block(*unit), BF16) for unit in units]],
        in_specs=[smem, smem, hbm, hbm, vmem, vmem, vmem, vmem, vmem, hbm, hbm, hbm, hbm],
        out_specs=[vmem] * 8,
        scratch_shapes=scratch,
        compiler_params=pltpu.CompilerParams(collective_id=0, has_side_effects=True, vmem_limit_bytes=VMEM_LIMIT),
    )(
        long_rows, short_rows, block_input, cotangent, prev_states, gate_bias[None], norm1_gain[None], conv_weight,
        norm2_gain[None], mixer_weight, out_weight, up_weight, down_weight,
    )
    outs = pl.pallas_call(
        functools.partial(last_kernel, hs),
        out_shape=[
            big, shape((slots, hs)), big, shape((1, width)), shape((rim + 1, width)), shape((2, width, hs)), shape((1, hs)),
            shape((hs, width)), shape((1, width)), shape((width, fs)), shape((fs, width)),
        ],
        in_specs=[vmem] * 8,
        out_specs=[hbm, vmem, hbm, vmem, vmem, hbm, vmem, hbm, vmem, hbm, hbm],
        scratch_shapes=[
            pltpu.VMEM((2, width, hs), F32), wide(hs), pltpu.VMEM((width, fs), F32), wide(fs),
            pltpu.SemaphoreType.DMA((8 + 2 * LANES,)),
        ],
        compiler_params=pltpu.CompilerParams(vmem_limit_bytes=VMEM_LAST),
    )(*outs)
    output, finals, input_grad, gain1, taps, mixer, bias, outw, gain2, up, down = outs
    return (output, finals, input_grad, gain1[0], taps, mixer, bias[0], outw, gain2[0], up, down)


def solution(mesh):
    takes_kernel = mesh.shape["tensor"] == 4 and mesh.shape["dp"] == 8
    rows = P(("dp", "tensor"), None)
    placed = (
        rows, P("dp"), P("dp"), P("dp", "tensor"), P(), P(), P(None, None, "tensor"), P("tensor"),
        P("tensor", None), P(), P(None, "tensor"), P("tensor", None), rows,
    )
    return jax.shard_map(
        fused if takes_kernel else plain,
        mesh=mesh,
        in_specs=placed,
        out_specs=(
            rows, P("dp", "tensor"), rows, P(), P(), P(None, None, "tensor"), P("tensor"), P("tensor", None),
            P(), P(None, "tensor"), P("tensor", None),
        ),
        check_vma=False,
    )
```

```python
import functools

import jax
import jax.numpy as jnp
from jax import lax
from jax.experimental import pallas as pl
from jax.experimental.pallas import tpu as pltpu
from jax.sharding import PartitionSpec as P

SHORT = 1024
LONG = 2048
VMEM_LIMIT = 58 * 1024 * 1024
VMEM_LAST = 24 * 1024 * 1024
epsilon = 1e-06
BF16 = jnp.bfloat16
F32 = jnp.float32


def rms_norm(values, gain):
    return values * lax.rsqrt(jnp.mean(values * values, axis=-1, keepdims=True) + epsilon) * gain


def contract(left, right, dims):
    return lax.dot_general(left, right, ((dims[:1], dims[1:]), ((), ())), preferred_element_type=F32)


def combine(before_pair, after_pair):
    return (before_pair[0] * after_pair[0], after_pair[0] * before_pair[1] + after_pair[1])


def row_facts(long_rows, short_rows, chunk):
    long_count, short_count = long_rows[0], short_rows[0]
    in_long = chunk < 2 * long_count
    in_row = chunk < 2 * long_count + short_count
    second = in_long & (chunk % 2 == 1)
    ends = in_row & (second | ~in_long)
    slot = jnp.where(in_long, chunk // 2, chunk - long_count)
    return in_row, second, ends, slot


def pair_swap(values, count):
    return lax.ppermute(values, "tensor", [(i, i ^ 1) for i in range(count)])


def plain(
    block_input, long_rows, short_rows, prev_states, norm1_gain, conv_weight, mixer_weight, gate_bias,
    out_weight, norm2_gain, up_weight, down_weight, cotangent,
):
    tokens, width = block_input.shape
    parts = lax.axis_size("tensor")
    me = lax.axis_index("tensor")
    rim = conv_weight.shape[0] - 1
    in_row, second, ends, slot = row_facts(long_rows, short_rows, me)
    mask = in_row.astype(F32)
    joined = second.astype(F32)
    even = (me % 2 == 0).astype(F32)
    slots = jnp.arange(prev_states.shape[0], dtype=jnp.int32)
    first_half = in_row & ~ends

    mixer_full = lax.all_gather(mixer_weight.astype(BF16), "tensor", axis=2, tiled=True)
    out_full = lax.all_gather(out_weight.astype(BF16), "tensor", axis=0, tiled=True)
    up_full = lax.all_gather(up_weight.astype(BF16), "tensor", axis=1, tiled=True)
    down_full = lax.all_gather(down_weight.astype(BF16), "tensor", axis=0, tiled=True)
    bias = lax.all_gather(gate_bias, "tensor", axis=0, tiled=True)
    prev = lax.all_gather(prev_states, "tensor", axis=1, tiled=True)
    start_state = jnp.sum(
        jnp.where((slots == slot)[:, None] & in_row & ~second, prev, 0.0), axis=0, keepdims=True
    )

    normed, norm1_back = jax.vjp(rms_norm, block_input, norm1_gain)
    rim_rows = pair_swap(normed[tokens - rim :], parts) * joined

    def convolve(extended, weight):
        total = weight[0] * extended[rim:]
        for tap in range(1, rim + 1):
            total = total + mask * weight[tap] * extended[rim - tap : rim - tap + tokens]
        return total

    conv_out, conv_back = jax.vjp(convolve, jnp.concatenate([rim_rows, normed], 0), conv_weight)
    conv_low = conv_out.astype(BF16)
    gate = contract(conv_low, mixer_full[0], (1, 0))
    cand = contract(conv_low, mixer_full[1], (1, 0))
    logit = gate + bias
    keep = jax.nn.sigmoid(-logit)
    opened = jax.nn.sigmoid(logit)
    soft = jax.nn.softplus(cand)
    factors, values = lax.associative_scan(combine, (keep, opened * soft), axis=0)
    ending = factors[-1:] * start_state + values[-1:]
    carry = start_state + joined * pair_swap(ending, parts)
    states = values + factors * carry
    before = jnp.concatenate([carry, states[:-1]], 0)
    end_table = jnp.where((slots == slot) & ends, 1.0, 0.0)[:, None]
    finals = lax.psum_scatter(end_table * states[-1:], "tensor", scatter_dimension=1, tiled=True)
    state_low = states.astype(BF16)
    mixed = contract(state_low, out_full, (1, 0))
    resid = block_input + mask * mixed
    normed_two, norm2_back = jax.vjp(rms_norm, resid, norm2_gain)
    normed_low = normed_two.astype(BF16)
    grad_branch = (mask * cotangent).astype(BF16)
    upward = contract(normed_low, up_full, (1, 0))
    activation, gelu_back = jax.vjp(lambda v: jax.nn.gelu(v, approximate=True), upward)
    activation_low = activation.astype(BF16)
    output = resid + mask * contract(activation_low, down_full, (1, 0))
    grad_act = contract(grad_branch, down_full, (1, 1))
    grad_up = gelu_back(grad_act)[0].astype(BF16)
    grad_norm_two = contract(grad_up, up_full, (1, 1))
    up_grad = contract(normed_low, grad_up, (0, 0))
    down_grad = contract(activation_low, grad_branch, (0, 0))
    grad_resid_norm, gain_two_part = norm2_back(grad_norm_two)
    grad_resid = cotangent + grad_resid_norm
    grad_mixed = (mask * grad_resid).astype(BF16)
    out_grad = contract(state_low, grad_mixed, (0, 0))
    grad_states = contract(grad_mixed, out_full, (1, 1))
    later_keep = jnp.concatenate([keep[1:], jnp.ones_like(keep[:1])], 0)
    back_factors, back_values = lax.associative_scan(combine, (later_keep, grad_states), axis=0, reverse=True)
    joins_next = (first_half & (me % 2 == 0)).astype(F32)
    back_carry = joins_next * pair_swap(keep[:1] * back_values[:1], parts)
    carried = back_values + back_factors * back_carry
    grad_logit = carried * (soft - before) * opened * (1 - opened)
    grad_cand = carried * opened * jax.nn.sigmoid(cand)
    bias_part = jnp.sum(grad_logit, axis=0)
    grad_logit_low = grad_logit.astype(BF16)
    grad_cand_low = grad_cand.astype(BF16)
    mixer_grad = jnp.stack([contract(conv_low, grad_logit_low, (0, 0)), contract(conv_low, grad_cand_low, (0, 0))])
    grad_conv = contract(grad_logit_low, mixer_full[0], (1, 1)) + contract(grad_cand_low, mixer_full[1], (1, 1))
    grad_extended, taps_part = conv_back(grad_conv)
    returned = joins_next * pair_swap(joined * grad_extended[:rim], parts)
    grad_normed = grad_extended[rim:] + jnp.concatenate(
        [jnp.zeros((tokens - rim, width), F32), returned], 0
    )
    grad_input_norm, gain_one_part = norm1_back(grad_normed)
    input_grad = grad_resid + grad_input_norm

    def scatter(grad, dim):
        return lax.psum_scatter(grad.astype(BF16), "tensor", scatter_dimension=dim, tiled=True)

    sharded = (
        scatter(mixer_grad, 2), scatter(out_grad, 0), scatter(up_grad, 1), scatter(down_grad, 0),
    )
    summed = tuple(g.astype(F32) for g in lax.psum(sharded, "dp"))
    shared = lax.psum((gain_one_part, taps_part, gain_two_part, bias_part), ("dp", "tensor"))
    channels = gate_bias.shape[0]
    bias_grad = lax.dynamic_slice_in_dim(shared[3], me * channels, channels)
    return (
        output, finals, input_grad, shared[0], shared[1], summed[0], bias_grad, summed[1], shared[2], summed[2], summed[3],
    )


LANES = 8
MESH = pl.DeviceIdType.MESH
CHUNKS = (2, 1, 2, 1, 2, 4)
FIRST = "yyxxy"
WIRES = 256
SCHEDULE = {
    "own0": (("g", "mix", "far", 0),),
    "gm": (("g", "mix", "far", 1),),
    "mixfar!": (("g", "mix", "across", 0), ("g", "out", "far", 0), ("g", "mix", "across", 1)),
    "rown": (("g", "up", "far", 0),),
    "scan2": (("g", "out", "across", 0), ("g", "up", "far", 1)),
    "end!": (("g", "up", "across", 0), ("g", "down", "far", 0)),
    "f00a": (("g", "up", "across", 1), ("g", "down", "far", 1)),
    "f01a": (("g", "down", "across", 0),),
    "updown!": (("down0", "xa", 0, 0), ("down0", "xa", 0, 1), ("g", "down", "across", 1)),
    "f10a": (("up0", "y", 0), ("up0", "y", 1), ("down0", "xa", 1, 0), ("down0", "xa", 1, 1)),
    "f12a": (("down0", "ya", 0), ("up0", "x", 0), ("down0", "ya", 1), ("down1", "xa", 1, 0), ("up1", "y", 0)),
    "f13a": (("up0", "x", 1),),
    "f13u": (("up0", "z", 0), ("down0", "z", 0)),
    "f13d": (("down1", "xa", 0, 0),),
    "B1a": (("down0", "z", 1),),
    "B1b": (("down1", "ya", 0),),
    "og0": (("up0", "zb", 0), ("up0", "z", 1)),
    "r1s": (("down0", "zb", 0),),
    "r1w!": (("up1", "x", 0), ("down0", "zb", 1), ("out", "y", 0), ("out", "y", 1)),
    "r1w0": (("up0", "xb", 0), ("down1", "z", 0)),
    "r1k1": (("up0", "zb", 1),),
    "r1e0": (("down0", "xb", 0), ("out", "x", 0), ("up1", "z", 0), ("mix", "y", 0), ("down0", "xb", 1), ("mix", "y", 1), ("mix", "y", 2), ("mix", "y", 3)),
    "r0s": (("out", "x", 1), ("down1", "zb", 0)),
    "r0w!": (("out", "z", 0), ("up0", "xb", 1)),
    "r0k1": (("out", "z", 1), ("up1", "zb", 0)),
    "r0e1": (("mix", "x", 0), ("mix", "x", 1), ("down1", "xb", 0)),
    "halo!": (("mix", "x", 2), ("out", "zb", 0)),
    "n1a": (("out", "zb", 1),),
    "n1b": (("mix", "z", 0), ("mix", "x", 3)),
    "drain": (("mix", "z", 1), ("up1", "xb", 0), ("pk", "chip"), ("out", "xb", 0), ("out", "xb", 1), ("mix", "z", 2), ("pk", "x"), ("mix", "zb", 0), ("mix", "z", 3), ("mix", "zb", 1), ("mix", "zb", 2), ("mix", "xb", 0), ("mix", "zb", 3), ("pk", "z"), ("mix", "xb", 1), ("mix", "xb", 2), ("mix", "xb", 3)),
}
GELU_A = 0.7978845608028654
GELU_B = 0.044715


def dot(left, right, dims=(1, 0)):
    return lax.dot_general(left, right, ((dims[:1], dims[1:]), ((), ())), preferred_element_type=F32)


def rows_of(block, width):
    return block.reshape(-1, width)


class Wires:
    def __init__(self, send, recv):
        self.send, self.recv, self.used = send, recv, 0

    def copy(self, src, dst, device):
        k = self.used
        self.used += 1
        return pltpu.make_async_remote_copy(
            src_ref=src, dst_ref=dst, send_sem=self.send.at[k], recv_sem=self.recv.at[k],
            device_id=device, device_id_type=MESH,
        )


def block_kernel(
    sizes, long_ref, short_ref, x_hbm, cot_hbm, prev_ref, bias_ref, gain1_ref, taps_ref, gain2_ref, mix_hbm, outw_hbm, up_hbm,
    down_hbm,
    cb, xb, finals_ref, small_ref, fin_up0, fin_up1, fin_down0, fin_down1, fin_out, fin_mix,
    n1h, res, gn2, fo, conv, n2, gm, act, gup, sig, st, ab, sp, sl,
    mix, outw, up, down,
    *rest,
):
    parts, rest = rest[:5], rest[5:]
    buffers, rest = [rest[5 * k : 5 * k + 5] for k in range(5)], rest[25:]
    (
        ry_mix, kx_mix, rx_mix, rz_mix,
        prev, biases, halo1, halo2, endrow, endin, brow, bin_, fsend, frecv,
        acc_n1, acc_n2, acc_t, acc_b, pk, pk_core, pk_chip, pk_x, pk_z,
        send_sem, recv_sem, local_sem,
    ) = rest
    n, z_count, tokens, width, hs, fs, slots, rim = sizes
    chips = n // 2
    steps = tokens // LANES
    tile = 256
    tiles = tokens // tile
    half_tiles = tiles // 2
    me = lax.axis_index("tensor")
    q, c = me // 2, me % 2
    dp = lax.axis_index("dp")
    z, x = dp // 2, dp % 2
    wires = Wires(send_sem, recv_sem)
    started = []

    def tensor(j):
        return (dp, j)

    sibling = tensor(me + 1 - 2 * c)
    partner = (dp + 1 - 2 * x, me)

    def z_peer(d):
        return ((((z + d) % z_count) * 2) + x, me)

    def shard_of(d, core):
        return ((q + d) % chips) * 2 + core

    def go(copy):
        copy.start()
        started.append(copy)
        return copy

    locals_ = [
        (mix_hbm.at[0], ab.at[0, pl.ds(0, width)]), (mix_hbm.at[1], ab.at[0, pl.ds(width, width)]),
        (outw_hbm, gn2.at[pl.ds(0, hs)]), (up_hbm, fo.at[pl.ds(0, width)]), (down_hbm, fo.at[pl.ds(width, fs)]),
    ]
    loads = [pltpu.make_async_copy(s, d, local_sem.at[i]) for i, (s, d) in enumerate(locals_)]

    def run(ref, g):
        return ref.at[pl.ds(g * steps, steps)]

    x_loads = [pltpu.make_async_copy(run(x_hbm, g), xb.at[:, g, :], local_sem.at[5 + g]) for g in range(LANES)]
    cot_loads = [pltpu.make_async_copy(run(cot_hbm, g), cb.at[:, g, :], local_sem.at[5 + LANES + g]) for g in range(LANES)]
    for copy in loads[:2] + x_loads + loads[2:] + cot_loads:
        copy.start()

    barrier = pltpu.get_barrier_semaphore()
    peers = [tensor((me + d) % n) for d in range(1, n)] + [partner] + [z_peer(d) for d in range(1, z_count)]
    for peer in peers:
        pl.semaphore_signal(barrier, inc=1, device_id=peer, device_id_type=MESH)

    long_count, short_count = long_ref[0], short_ref[0]
    is_long = jnp.where(me < 2 * long_count, 1.0, 0.0)
    in_row = jnp.where(me < 2 * long_count + short_count, 1.0, 0.0)
    odd = (me % 2).astype(F32)
    joined = is_long * odd
    joins_next = is_long * (1.0 - odd)
    starts = in_row * (1.0 - joined)
    ends = in_row * (1.0 - joins_next)
    slot = jnp.where(me < 2 * long_count, me // 2, me - long_count)
    slot_mask = [jnp.where(slot == s, 1.0, 0.0) for s in range(slots)]

    gathers = {}

    weight_copies = []

    def gather(name, ref):
        size = ref.shape[1] // 2
        far, across, passed = [], [], []
        for k in range(size):
            mine, r = ref.at[me, x * size + k], shard_of(1, c)
            ours, theirs = ref.at[r, x * size + k], ref.at[r, (1 - x) * size + k]
            far.append(go(wires.copy(mine, mine, tensor(r))))
            weight_copies.append(far[-1])
            across.append(wires.copy(ours, ours, partner))
            passed.append((wires.copy(ours, ours, sibling), wires.copy(theirs, theirs, sibling)))
        sib = go(wires.copy(ref.at[me], ref.at[me], sibling))
        weight_copies.append(sib)
        gathers[name] = (sib, far, across, passed)

    def gather_far(name, k):
        _, far, across, passed = gathers[name]
        far[k].wait_recv()
        weight_copies.extend((go(across[k]), go(passed[k][0])))

    def gather_across(name, k):
        _, far, across, passed = gathers[name]
        across[k].wait_recv()
        weight_copies.append(go(passed[k][1]))

    def gather_passed(name):
        for one, two in gathers[name][3]:
            one.wait_recv()
            two.wait_recv()

    stages = {("g", "far"): gather_far, ("g", "across"): gather_across}

    def run_stages(hook):
        for step in SCHEDULE.get(hook, ()):
            if step[0] == "g":
                stages["g", step[2]](step[1], *step[3:])
            else:
                stages[step[:2]](*step[2:])

    prev[me] = prev_ref[...]
    biases[me] = bias_ref[...]
    loads[0].wait()
    loads[1].wait()
    half = width // 2
    for h in range(2):
        mix[me, pl.ds(2 * h, 2)] = (
            jnp.concatenate([ab[0, pl.ds(h * half, half), :], ab[0, pl.ds(width + h * half, half), :]], axis=1)
            .astype(BF16)
            .reshape((2,) + mix.shape[2:])
        )
    pl.semaphore_wait(barrier, len(peers))
    gather("mix", mix)
    lead_copies = []
    for ref in (prev, biases):
        lead_copies += [go(wires.copy(ref.at[me], ref.at[me], tensor((me + d) % n))) for d in range(1, n)]
    loads[2].wait()
    outw[me] = gn2[pl.ds(0, hs), :].astype(BF16).reshape(2, hs // 2, width)
    gather("out", outw)
    loads[3].wait()
    up[me] = fo[pl.ds(0, width), :].astype(BF16).reshape(up.shape[1:])
    gather("up", up)
    loads[4].wait()
    down[me] = fo[pl.ds(width, fs), :].astype(BF16).reshape(down.shape[1:])
    gather("down", down)

    span = 64
    spans = tokens // span

    def at(i, shift=0, size=span):
        return pl.ds(pl.multiple_of(i * size + shift, LANES), size)

    def take(ref, i, size=span):
        return ref[pl.ds(i * (size // LANES), size // LANES)].reshape(size, width)

    def put(ref, i, value):
        ref[pl.ds(i * (span // LANES), span // LANES)] = value.reshape(span // LANES, LANES, width)

    def eights(value):
        return jnp.sum(value.reshape(-1, LANES, value.shape[-1]), axis=0)

    hook = run_stages
    for copy in x_loads:
        copy.wait()
    gain1 = gain1_ref[...]
    gain2 = gain2_ref[...]

    def norm1_rows(i):
        v = take(xb, i)
        scale = lax.rsqrt(jnp.mean(v * v, axis=-1, keepdims=True) + epsilon)
        n1h[at(i, rim * LANES), :] = v * scale * gain1

    for part, (begin, stop) in enumerate(((0, 6), (6, 11), (11, 16))):
        pl.loop(begin * spans // 16, stop * spans // 16, unroll=True)(norm1_rows)
        if part < 2:
            hook(f"n1a{part}")

    hook("norm1")
    edge = rim * LANES
    halo_copy = go(wires.copy(n1h.at[pl.ds(tokens, edge)], halo1, sibling))
    halo_copy.wait_recv()
    sub = lax.broadcasted_iota(jnp.int32, (LANES, width), 0)
    for k in range(rim):
        own = pltpu.roll(n1h[pl.ds(tokens + k * LANES, LANES), :], 1, 0)
        other = pltpu.roll(halo1[pl.ds(k * LANES, LANES), :], 1, 0)
        n1h[pl.ds(k * LANES, LANES), :] = jnp.where(sub == 0, joined * other, own)
    tap = [taps_ref[pl.ds(k, 1), :] * (1.0 if k == 0 else in_row) for k in range(rim + 1)]

    def conv_rows(i):
        total = tap[0] * n1h[at(i, edge), :]
        for k in range(1, rim + 1):
            total = total + tap[k] * n1h[at(i, edge - k * LANES), :]
        conv[at(i), :] = total.astype(BF16)

    pl.loop(0, spans // 2, unroll=4)(conv_rows)
    hook("cv0")
    pl.loop(spans // 2, spans, unroll=4)(conv_rows)

    def project(j, between=None):
        weight = rows_of(mix[j], 2 * hs)
        bias = biases[j]

        def some(t):
            rows = at(t, 0, tile)
            pre = dot(conv[rows, :], weight)
            logit = pre[:, :hs] + bias
            cand = pre[:, hs:]
            e = jnp.exp(-jnp.abs(logit))
            r = 1.0 / (1.0 + e)
            opened = jnp.where(logit >= 0, r, e * r)
            keep = jnp.where(logit >= 0, e * r, r)
            soft = jnp.maximum(cand, 0.0) + jnp.log1p(jnp.exp(-jnp.abs(cand)))
            sig[j, rows, :] = opened
            sp[j, rows, :] = soft
            ab[j, rows, :] = keep * in_row
            st[j, at(t, LANES, tile), :] = opened * soft

        if between is None:
            pl.loop(0, tiles, unroll=tiles)(some)
        else:
            pl.loop(0, half_tiles, unroll=half_tiles)(some)
            hook(between)
            pl.loop(half_tiles, tiles, unroll=half_tiles)(some)

    hook("conv")
    for copy in lead_copies:
        copy.wait_recv()
    project(me, "own0")
    hook("own")
    gathers["mix"][0].wait_recv()
    project(me + 1 - 2 * c, "sib0")
    hook("sib")

    def unrolled(count, step, carry, by=4):
        def some(i, carry):
            for k in range(by):
                carry = step(i * by + k, carry)
            return carry

        return lax.fori_loop(0, count // by, some, carry)

    one = jnp.ones((LANES, hs), F32)
    zero = jnp.zeros((LANES, hs), F32)

    def scan(js):
        def step(s, carry):
            rows = at(s, 0, LANES)
            later = at(s, LANES, LANES)
            out = []
            for j, (fac, val) in zip(js, carry):
                a = ab[j, rows, :]
                fac = a * fac
                val = a * val + st[j, later, :]
                ab[j, rows, :] = fac
                st[j, later, :] = val
                out.append((fac, val))
            return tuple(out)

        unrolled(steps, step, tuple((one, zero) for _ in js))

    scan([me, me + 1 - 2 * c])
    hook("scan1")
    for copy in cot_loads:
        copy.wait()

    @pl.loop(0, spans, unroll=4)
    def _(i):
        gm[at(i), :] = (in_row * take(cb, i)).astype(BF16)

    hook("gm")
    hook("mixfar!")
    project(shard_of(1, c))
    hook("rown")
    hook("mixpass!")
    gather_passed("mix")
    project(shard_of(1, 1 - c))
    hook("rsib")
    scan([shard_of(1, c), shard_of(1, 1 - c)])
    hook("scan2")
    last = pl.ds(tokens - LANES, LANES)

    def chain(j, carry, keep_rows):
        fac = ab[j, last, :]
        val = st[j, pl.ds(tokens, LANES), :]
        rows = []
        for g in range(LANES):
            rows.append(carry)
            carry = fac[g : g + 1] * carry + val[g : g + 1]
        if keep_rows:
            st[j, pl.ds(0, LANES), :] = jnp.concatenate(rows, axis=0)
        return carry

    first = []
    for j in range(n):
        begin = jnp.zeros((1, hs), F32)
        for s in range(slots):
            begin = begin + (starts * slot_mask[s]) * prev[j, pl.ds(s, 1), :]
        first.append(begin)
        endrow[j] = chain(j, begin, False)
    end_copy = go(wires.copy(endrow, endin, sibling))
    hook("chain")
    hook("end!")
    end_copy.wait_recv()
    for j in range(n):
        ending = chain(j, first[j] + joined * endin[j], True)
        for s in range(slots):
            fsend[j, pl.ds(s, 1), :] = (ends * slot_mask[s]) * ending
    final_copies = [
        go(wires.copy(fsend.at[(me + d) % n], frecv.at[d - 1], tensor((me + d) % n))) for d in range(1, n)
    ]

    hook("chain2")
    hook("out!")
    gathers["out"][0].wait_recv()
    gather_passed("out")
    @pl.loop(0, tiles, unroll=tiles)
    def _(t):
        rows = at(t, 0, tile)
        mixed = jnp.zeros((tile, width), F32)
        for j in range(n):
            into = st[j, pl.ds(0, LANES), :]
            value = st[j, at(t, LANES, tile), :] + (
                ab[j, rows, :].reshape(-1, LANES, hs) * into[None]
            ).reshape(tile, hs)
            st[j, at(t, LANES, tile), :] = value
            low = value.astype(BF16)
            sl[j, rows, :] = low
            mixed = mixed + dot(low, rows_of(outw[j], width))
        resid = take(xb, t, tile) + in_row * mixed
        res[rows, :] = resid
        scale = lax.rsqrt(jnp.mean(resid * resid, axis=-1, keepdims=True) + epsilon)
        n2[rows, :] = (resid * scale * gain2).astype(BF16)

    hook("states")
    gathers["up"][0].wait_recv()
    gathers["down"][0].wait_recv()

    def far_weights():
        hook("updown!")
        gather_passed("up")
        gather_passed("down")


    class Sum:
        def __init__(self, part, rc, ry, kx, rx, rz, fin):
            self.part, self.rc, self.ry, self.kx, self.rx, self.rz, self.fin = part, rc, ry, kx, rx, rz, fin
            self.chunks = fin.shape[0]
            self.c1 = [None] * chips
            self.c2, self.c3, self.c4, self.c5, self.c6 = {}, {}, {}, {}, {}
            self.first = wires.used
            wires.used += chips

        def one(self, d):
            copy = pltpu.make_async_remote_copy(
                src_ref=self.part.at[shard_of(d, 1 - c)], dst_ref=self.rc.at[d], send_sem=send_sem.at[self.first + d],
                recv_sem=recv_sem.at[self.first + d], device_id=sibling, device_id_type=MESH,
            )
            self.c1[d] = go(copy)

        def both(self, j, d, k, h):
            return self.part[j, k, h].astype(F32) + self.rc[d, k, h].astype(F32)

        def y(self, k=0):
            self.c2[k] = []
            for d in range(1, chips):
                if k == 0:
                    self.c1[d].wait_recv()
                j = shard_of(d, c)
                for h in range(2):
                    self.part[j, k, h] = self.both(j, d, k, h).astype(BF16)
                self.c2[k].append(go(wires.copy(self.part.at[j, k], self.ry.at[d - 1, k], tensor(j))))

        def total(self, k, h):
            v = self.both(me, 0, k, h)
            for d in range(chips - 1):
                v = v + self.ry[d, k, h].astype(F32)
            return v

        def x(self, k=0):
            if k == 0:
                self.c1[0].wait_recv()
            for copy in self.c2[k]:
                copy.wait_recv()
            self.part[me, k, 1 - x] = self.total(k, 1 - x).astype(BF16)
            self.c3[k] = go(wires.copy(self.part.at[me, k, 1 - x], self.rx.at[k], partner))
            self.kx[k] = self.total(k, x)

        def z(self, k=0):
            self.c3[k].wait_recv()
            self.spread(k, self.kx[k] + self.rx[k].astype(F32))

        def spread(self, k, v):
            self.kx[k] = v
            self.part[me, k, x] = v.astype(BF16)
            self.c4[k] = [
                go(wires.copy(self.part.at[me, k, x, (z + d) % z_count], self.rz.at[d - 1, k], z_peer(d)))
                for d in range(1, z_count)
            ]

        def zb(self, k=0):
            for copy in self.c4[k]:
                copy.wait_recv()
            v = self.kx[k, z]
            for d in range(z_count - 1):
                v = v + self.rz[d, k].astype(F32)
            self.fin[k, x, z] = v.astype(BF16)
            mine = self.fin.at[k, x, z]
            self.c5[k] = [go(wires.copy(mine, mine, z_peer(d))) for d in range(1, z_count)]
            self.c6[k] = [go(wires.copy(mine, mine, partner))]

        def xb(self, k=0):
            for d in range(1, z_count):
                self.c5[k][d - 1].wait_recv()
                theirs = self.fin.at[k, x, (z + z_count - d) % z_count]
                self.c6[k].append(go(wires.copy(theirs, theirs, partner)))

        def end(self):
            for k in range(self.chunks):
                for copy in self.c6[k]:
                    copy.wait_recv()

    class SumAcross(Sum):
        def xa(self, d, k=0):
            if k == 0:
                self.c1[d].wait_recv()
            j = shard_of(d, c)
            self.part[j, k, 1 - x] = self.both(j, d, k, 1 - x).astype(BF16)
            self.c3[d, k] = go(wires.copy(self.part.at[j, k, 1 - x], self.rx.at[d, k], partner))

        def ya(self, k=0):
            self.c3[1, k].wait_recv()
            j = shard_of(1, c)
            self.part[j, k, x] = (self.both(j, 1, k, x) + self.rx[1, k].astype(F32)).astype(BF16)
            self.c2[k] = go(wires.copy(self.part.at[j, k, x], self.ry.at[k], tensor(j)))

        def z(self, k=0):
            self.c3[0, k].wait_recv()
            self.c2[k].wait_recv()
            self.spread(k, self.both(me, 0, k, x) + self.rx[0, k].astype(F32) + self.ry[k].astype(F32))

    s_parts = [
        (SumAcross if first == "x" else Sum)(part, *refs, fin)
        for first, part, refs, fin in zip(FIRST, parts, buffers, (fin_up0, fin_up1, fin_down0, fin_down1, fin_out))
    ]
    s_out = s_parts[4]
    s_mix = Sum(up, down, ry_mix, kx_mix, rx_mix, rz_mix, fin_mix)
    for name, unit in zip(("up0", "up1", "down0", "down1", "out", "mix"), s_parts + [s_mix]):
        for stage in ("y", "x", "xa", "ya", "z", "zb", "xb"):
            stages[name, stage] = getattr(unit, stage, None)

    def weight_grad(unit, j, left, right):
        unit.part[j] = dot(left, right, (0, 0)).astype(BF16).reshape(unit.part.shape[1:])

    fh = fs // 2

    def feed(j, h, name, d=None, begin=False):
        cols = pl.ds(h * fh, fh)
        chunks = down.shape[1] // 2

        @pl.loop(0, tiles, unroll=tiles)
        def _(t):
            rows = at(t, 0, tile)
            upw = rows_of(up[j, :, :, :, :, cols], fh)
            downw = rows_of(down[j, pl.ds(h * chunks, chunks)], width)
            u = dot(n2[rows, :], upw)
            ga = dot(gm[rows, :], downw, (1, 1))
            u2 = u * u
            th = jnp.tanh(GELU_A * u * (1.0 + GELU_B * u2))
            hp = 0.5 + 0.5 * th
            a = (u * hp).astype(BF16)
            slope = hp + (0.5 * GELU_A) * u * (1.0 - th * th) * (1.0 + 3.0 * GELU_B * u2)
            gu = (ga * slope).astype(BF16)
            act[rows, cols] = a
            gup[rows, cols] = gu
            o = dot(a, downw)
            g = dot(gu, upw, (1, 1))
            if begin:
                fo[rows, :] = o
                gn2[rows, :] = g
            else:
                fo[rows, :] = fo[rows, :] + o
                gn2[rows, :] = gn2[rows, :] + g

        hook(name + "a")
        for unit, left, right, end in ((s_parts[h], n2, gup, "u"), (s_parts[2 + h], gm, act, "d")):
            weight_grad(unit, j, left[...], right[:, cols])
            if d is not None:
                unit.one(d)
            hook(name + end)

    feed(me + 1 - 2 * c, 0, "f00", 0, True)
    feed(me, 0, "f01")
    far_weights()
    feed(shard_of(1, 1 - c), 0, "f02", 1)
    feed(shard_of(1, c), 0, "f03")
    feed(shard_of(1, 1 - c), 1, "f10", 1)
    feed(shard_of(1, c), 1, "f11")
    feed(me + 1 - 2 * c, 1, "f12", 0)
    feed(me, 1, "f13")

    acc_n2[...] = jnp.zeros_like(acc_n2)

    def norm2_back(i):
        r = res[at(i), :]
        g = gn2[at(i), :]
        scale = lax.rsqrt(jnp.mean(r * r, axis=-1, keepdims=True) + epsilon)
        gg = g * gain2
        m = jnp.mean(gg * r, axis=-1, keepdims=True)
        gr = take(cb, i) + scale * gg - r * (scale * scale * scale * m)
        acc_n2[...] += eights(g * r * scale)
        gn2[at(i), :] = gr
        gm[at(i), :] = (in_row * gr).astype(BF16)
        put(cb, i, r + in_row * fo[at(i), :])

    pl.loop(0, spans // 2, unroll=2)(norm2_back)
    hook("B1a")
    pl.loop(spans // 2, spans, unroll=2)(norm2_back)
    hook("B1b")

    def store(ref, hbm, first):
        copies = [pltpu.make_async_copy(ref.at[:, g, :], run(hbm, g), local_sem.at[first + g]) for g in range(LANES)]
        for copy in copies:
            copy.start()
        return copies

    for copy in weight_copies:
        copy.wait_send()
    started[:] = [copy for copy in started if not any(copy is other for other in weight_copies)]

    for d in (1, 0):
        for core in (1 - c, c):
            j = shard_of(d, core)
            weight_grad(s_out, j, gm[...], sl[j])
        s_out.one(d)
    hook("og0")

    for j in range(n):
        acc_b[j] = jnp.zeros((LANES, hs), F32)

    def recur_back(d, begin, name):
        js = [shard_of(d, core) for core in range(2)]
        for k in range(2):
            ab[k] = dot(gm[...], rows_of(outw[js[k]], width), (1, 1))
        hook(name + "g")

        def back_step(i, carry):
            s = steps - 1 - i
            rows = at(s, 0, LANES)
            out = []
            for k in range(2):
                fac, val, keep = carry[k]
                fac = keep * fac
                val = ab[k, rows, :] + keep * val
                ab[2 + k, rows, :] = fac
                ab[k, rows, :] = val
                out.append((fac, val, 1.0 - sig[js[k], rows, :]))
            return tuple(out)

        unrolled(steps, back_step, ((one, zero, one), (one, zero, one)))
        hook(name + "s")

        def chain_back(k, carry, j):
            fac = ab[2 + k, pl.ds(0, LANES), :]
            val = ab[k, pl.ds(0, LANES), :]
            keep = 1.0 - sig[j, pl.ds(0, LANES), :]
            rows = []
            for g in reversed(range(LANES)):
                rows.append(carry)
                carry = keep[g : g + 1] * (val[g : g + 1] + fac[g : g + 1] * carry)
            return carry, jnp.concatenate(rows[::-1], axis=0)

        slot_ = 2 * d
        for k in range(2):
            brow[slot_ + k] = chain_back(k, jnp.zeros((1, hs), F32), js[k])[0]
        copy = go(wires.copy(brow.at[pl.ds(slot_, 2)], bin_.at[pl.ds(slot_, 2)], sibling))
        hook(name + "c")
        hook(name + "w!")
        copy.wait_recv()
        grads = (act, gup)
        order = [(1 - c, shard_of(d, 1 - c)), (c, shard_of(d, c))]
        for g, (k, j) in enumerate(order):
            into = chain_back(k, joins_next * bin_[slot_ + k], j)[1]

            @pl.loop(0, tiles, unroll=tiles)
            def _(t, j=j, k=k, g=g, into=into):
                rows = at(t, 0, tile)
                carried = ab[k, rows, :] + (ab[2 + k, rows, :].reshape(-1, LANES, hs) * into[None]).reshape(tile, hs)
                opened = sig[j, rows, :]
                soft = sp[j, rows, :]
                weighted = carried * opened
                gl = weighted * (soft - st[j, rows, :]) * (1.0 - opened)
                close = jnp.where(soft < 0.01, soft * (1.0 - soft * (0.5 - soft * (1.0 / 6.0))), 1.0 - jnp.exp(-soft))
                gc = weighted * close
                acc_b[j] += eights(gl)
                grads[g][rows, :] = jnp.concatenate([gl.astype(BF16), gc.astype(BF16)], axis=1)

            hook(f"{name}k{g}")
            weight_grad(s_mix, j, conv[...], grads[g][...])
            if g == 0:
                s_mix.one(d)
            hook(f"{name}w{g}")

        def gather_back(t):
            rows = at(t, 0, tile)
            back = sum(dot(left[rows, :], rows_of(mix[j], 2 * hs), (1, 1)) for left, (_, j) in zip(grads, order))
            res[rows, :] = back if begin else res[rows, :] + back

        pl.loop(0, half_tiles, unroll=half_tiles)(gather_back)
        hook(name + "e0")
        pl.loop(half_tiles, tiles, unroll=half_tiles)(gather_back)
        hook(name + "e1")

    recur_back(1, True, "r1")
    recur_back(0, False, "r0")
    halo_back = go(wires.copy(res.at[pl.ds(0, edge)], halo2, sibling))
    hook("halo!")
    halo_back.wait_recv()

    for k in range(rim):
        own = pltpu.roll(res[pl.ds(k * LANES, LANES), :], LANES - 1, 0)
        other = pltpu.roll(halo2[pl.ds(k * LANES, LANES), :], LANES - 1, 0)
        res[pl.ds(tokens + k * LANES, LANES), :] = jnp.where(sub == LANES - 1, joins_next * other, own)
    acc_n1[...] = jnp.zeros_like(acc_n1)
    acc_t[...] = jnp.zeros_like(acc_t)

    def norm1_back(i):
        g0 = res[at(i), :]
        total = tap[0] * g0
        acc_t[0] += eights(g0 * n1h[at(i, edge), :])
        for k in range(1, rim + 1):
            total = total + tap[k] * res[at(i, k * LANES), :]
            acc_t[k] += eights(g0 * n1h[at(i, edge - k * LANES), :])
        v = take(xb, i)
        scale = lax.rsqrt(jnp.mean(v * v, axis=-1, keepdims=True) + epsilon)
        gg = total * gain1
        m = jnp.mean(gg * v, axis=-1, keepdims=True)
        acc_n1[...] += eights(total * v * scale)
        put(xb, i, gn2[at(i), :] + scale * gg - v * (scale * scale * scale * m))

    pl.loop(0, spans // 2, unroll=2)(norm1_back)
    hook("n1a")
    pl.loop(spans // 2, spans, unroll=2)(norm1_back)
    hook("n1b")

    pk[...] = jnp.zeros_like(pk)
    pk[pl.ds(0, 1), :] = jnp.sum(acc_n1[...], axis=0, keepdims=True)
    for k in range(rim + 1):
        pk[pl.ds(1 + k, 1), :] = jnp.sum(acc_t[k], axis=0, keepdims=True)
    pk[pl.ds(6, 1), :] = jnp.sum(acc_n2[...], axis=0, keepdims=True)
    for j in range(n):
        pk[pl.ds(8 + j, 1), pl.ds(0, hs)] = jnp.sum(acc_b[j], axis=0, keepdims=True)
    k1 = go(wires.copy(pk, pk_core, sibling))
    small_copies = {}

    def small_chip():
        k1.wait_recv()
        pk_chip[q] = pk[...] + pk_core[...]
        small_copies[2] = go(wires.copy(pk_chip.at[q], pk_chip.at[q], tensor(shard_of(1, c))))

    def small_x():
        small_copies[2].wait_recv()
        pk_x[0] = pk_chip[0] + pk_chip[1]
        small_copies[3] = go(wires.copy(pk_x.at[0], pk_x.at[1], partner))

    def small_z():
        small_copies[3].wait_recv()
        pk_z[z] = pk_x[0] + pk_x[1]
        small_copies[4] = [go(wires.copy(pk_z.at[z], pk_z.at[z], z_peer(d))) for d in range(1, z_count)]

    stages["pk", "chip"], stages["pk", "x"], stages["pk", "z"] = small_chip, small_x, small_z
    hook("pk")
    hook("drain")
    for copy in final_copies:
        copy.wait_recv()
    total = fsend[me]
    for d in range(n - 1):
        total = total + frecv[d]
    finals_ref[...] = total
    for copy in small_copies[4]:
        copy.wait_recv()
    value = pk_z[0]
    for k in range(1, z_count):
        value = value + pk_z[k]
    small_ref[...] = value
    for unit in s_parts + [s_mix]:
        unit.end()
    for copy in started:
        copy.wait_send()


def last_kernel(
    hs, output_in, igrad_in, finals_in, small, g_up0, g_up1, g_down0, g_down1, g_out, g_mix,
    output, finals, igrad, gain1, taps, mixer, bias, outw, gain2, up, down, mixer_v, outw_v, up_v, down_v, sem,
):
    width = up_v.shape[0]
    steps = output_in.shape[0]
    later = []
    for k, (src, dst) in enumerate(((output_in, output), (igrad_in, igrad))):
        for g in range(LANES):
            later.append(pltpu.make_async_copy(src.at[:, g, :], dst.at[pl.ds(g * steps, steps)], sem.at[8 + k * LANES + g]))
            later[-1].start()
    me = lax.axis_index("tensor")
    fh = up_v.shape[1] // 2
    up_v[:, :fh] = rows_of(g_up0[...], fh).astype(F32)
    up_v[:, fh:] = rows_of(g_up1[...], fh).astype(F32)
    later.append(pltpu.make_async_copy(up_v, up, sem.at[2]))
    later[-1].start()
    both = rows_of(g_mix[...], 2 * hs).astype(F32)
    mixer_v[0] = both[:, :hs]
    mixer_v[1] = both[:, hs:]
    later.append(pltpu.make_async_copy(mixer_v, mixer, sem.at[5]))
    later[-1].start()
    down_v[:fh] = rows_of(g_down0[...], fh).astype(F32).T
    down_v[fh:] = rows_of(g_down1[...], fh).astype(F32).T
    later.append(pltpu.make_async_copy(down_v, down, sem.at[6]))
    later[-1].start()
    outw_v[...] = rows_of(g_out[...], hs).astype(F32).T
    later.append(pltpu.make_async_copy(outw_v, outw, sem.at[7]))
    later[-1].start()
    finals[...] = finals_in[...]
    gain1[...] = small[pl.ds(0, 1), :]
    taps[...] = small[pl.ds(1, taps.shape[0]), :]
    gain2[...] = small[pl.ds(6, 1), :]
    bias[...] = small[pl.ds(8 + me, 1), pl.ds(0, hs)]
    for copy in later:
        copy.wait()


def fused(
    block_input, long_rows, short_rows, prev_states, norm1_gain, conv_weight, mixer_weight, gate_bias,
    out_weight, norm2_gain, up_weight, down_weight, cotangent,
):
    tokens, width = block_input.shape
    n = lax.axis_size("tensor")
    z_count = lax.axis_size("dp") // 2
    chips = n // 2
    slots, hs = prev_states.shape
    fs = up_weight.shape[1]
    rim = conv_weight.shape[0] - 1
    steps = tokens // LANES
    pk_rows = 8 + -(-n // 8) * 8
    units = [(chunks, cols) for chunks, cols in zip(CHUNKS, (fs // 2,) * 4 + (hs, 2 * hs))]

    def block(chunks, cols):
        return (chunks, 2, z_count, width // (2 * z_count * chunks), cols)

    def full(chunks, cols):
        return pltpu.VMEM((n,) + block(chunks, cols), BF16)

    def sums(chunks, cols, across=False):
        dims = block(chunks, cols)
        part = dims[2:]
        return [
            pltpu.VMEM((chips,) + dims, BF16),
            pltpu.VMEM((chunks,) + part if across else (chips - 1,) + dims, BF16),
            pltpu.VMEM((chunks,) + part, F32),
            pltpu.VMEM(((chips, chunks) if across else (chunks,)) + part, BF16),
            pltpu.VMEM((z_count - 1, chunks) + part[1:], BF16),
        ]

    def wide(rows, kind=F32):
        return pltpu.VMEM((rows, width), kind)

    permuted = pltpu.VMEM((steps, LANES, width), F32)
    per_block = pltpu.VMEM((n, tokens, hs), F32)
    scratch = [
        wide(tokens + rim * LANES), wide(tokens + rim * LANES), wide(tokens), wide(tokens),
        wide(tokens, BF16), wide(tokens, BF16), wide(tokens, BF16), pltpu.VMEM((tokens, fs), BF16), pltpu.VMEM((tokens, fs), BF16),
        per_block, pltpu.VMEM((n, tokens + LANES, hs), F32), per_block, per_block, pltpu.VMEM((n, tokens, hs), BF16),
        pltpu.VMEM((n, 4, width // 4, 2 * hs), BF16), pltpu.VMEM((n, 2, hs // 2, width), BF16), full(*units[5]), full(*units[5]),
        *[full(*unit) for unit in units[:5]],
        *[ref for unit, first in zip(units[:5], FIRST) for ref in sums(*unit, first == "x")], *sums(*units[5])[1:],
        pltpu.VMEM((n, slots, hs), F32), pltpu.VMEM((n, 1, hs), F32), wide(rim * LANES), wide(rim * LANES),
        pltpu.VMEM((n, 1, hs), F32), pltpu.VMEM((n, 1, hs), F32), pltpu.VMEM((n, 1, hs), F32), pltpu.VMEM((n, 1, hs), F32),
        pltpu.VMEM((n, slots, hs), F32), pltpu.VMEM((n - 1, slots, hs), F32),
        wide(LANES), wide(LANES), pltpu.VMEM((rim + 1, LANES, width), F32), pltpu.VMEM((n, LANES, hs), F32),
        wide(pk_rows), wide(pk_rows), pltpu.VMEM((chips, pk_rows, width), F32), pltpu.VMEM((2, pk_rows, width), F32),
        pltpu.VMEM((z_count, pk_rows, width), F32),
        pltpu.SemaphoreType.DMA((WIRES,)), pltpu.SemaphoreType.DMA((WIRES,)), pltpu.SemaphoreType.DMA((5 + 4 * LANES,)),
    ]
    vmem = pl.BlockSpec(memory_space=pltpu.VMEM)
    smem = pl.BlockSpec(memory_space=pltpu.SMEM)
    hbm = pl.BlockSpec(memory_space=pl.ANY)

    def shape(dims, kind=F32):
        return jax.ShapeDtypeStruct(dims, kind)

    big = shape((tokens, width))
    outs = pl.pallas_call(
        functools.partial(block_kernel, (n, z_count, tokens, width, hs, fs, slots, rim)),
        out_shape=[permuted, permuted, pltpu.VMEM((slots, hs), F32), pltpu.VMEM((pk_rows, width), F32), *[pltpu.VMEM(block(*unit), BF16) for unit in units]],
        in_specs=[smem, smem, hbm, hbm, vmem, vmem, vmem, vmem, vmem, hbm, hbm, hbm, hbm],
        out_specs=[vmem] * 10,
        scratch_shapes=scratch,
        compiler_params=pltpu.CompilerParams(collective_id=0, has_side_effects=True, vmem_limit_bytes=VMEM_LIMIT),
    )(
        long_rows, short_rows, block_input, cotangent, prev_states, gate_bias[None], norm1_gain[None], conv_weight,
        norm2_gain[None], mixer_weight, out_weight, up_weight, down_weight,
    )
    outs = pl.pallas_call(
        functools.partial(last_kernel, hs),
        out_shape=[
            big, shape((slots, hs)), big, shape((1, width)), shape((rim + 1, width)), shape((2, width, hs)), shape((1, hs)),
            shape((hs, width)), shape((1, width)), shape((width, fs)), shape((fs, width)),
        ],
        in_specs=[vmem] * 10,
        out_specs=[hbm, vmem, hbm, vmem, vmem, hbm, vmem, hbm, vmem, hbm, hbm],
        scratch_shapes=[
            pltpu.VMEM((2, width, hs), F32), wide(hs), pltpu.VMEM((width, fs), F32), wide(fs),
            pltpu.SemaphoreType.DMA((8 + 2 * LANES,)),
        ],
        compiler_params=pltpu.CompilerParams(vmem_limit_bytes=VMEM_LAST),
    )(*outs)
    output, finals, input_grad, gain1, taps, mixer, bias, outw, gain2, up, down = outs
    return (output, finals, input_grad, gain1[0], taps, mixer, bias[0], outw, gain2[0], up, down)


def solution(mesh):
    takes_kernel = mesh.shape["tensor"] == 4 and mesh.shape["dp"] == 8
    rows = P(("dp", "tensor"), None)
    placed = (
        rows, P("dp"), P("dp"), P("dp", "tensor"), P(), P(), P(None, None, "tensor"), P("tensor"),
        P("tensor", None), P(), P(None, "tensor"), P("tensor", None), rows,
    )
    return jax.shard_map(
        fused if takes_kernel else plain,
        mesh=mesh,
        in_specs=placed,
        out_specs=(
            rows, P("dp", "tensor"), rows, P(), P(), P(None, None, "tensor"), P("tensor"), P("tensor", None),
            P(), P(None, "tensor"), P("tensor", None),
        ),
        check_vma=False,
    )
```

```python
import functools

import jax
import jax.numpy as jnp
from jax import lax
from jax.experimental import pallas as pl
from jax.experimental.pallas import tpu as pltpu
from jax.sharding import PartitionSpec as P

SHORT = 1024
LONG = 2048
VMEM_LIMIT = 58 * 1024 * 1024
VMEM_LAST = 24 * 1024 * 1024
epsilon = 1e-06
BF16 = jnp.bfloat16
F32 = jnp.float32


def rms_norm(values, gain):
    return values * lax.rsqrt(jnp.mean(values * values, axis=-1, keepdims=True) + epsilon) * gain


def contract(left, right, dims):
    return lax.dot_general(left, right, ((dims[:1], dims[1:]), ((), ())), preferred_element_type=F32)


def combine(before_pair, after_pair):
    return (before_pair[0] * after_pair[0], after_pair[0] * before_pair[1] + after_pair[1])


def row_facts(long_rows, short_rows, chunk):
    long_count, short_count = long_rows[0], short_rows[0]
    in_long = chunk < 2 * long_count
    in_row = chunk < 2 * long_count + short_count
    second = in_long & (chunk % 2 == 1)
    ends = in_row & (second | ~in_long)
    slot = jnp.where(in_long, chunk // 2, chunk - long_count)
    return in_row, second, ends, slot


def pair_swap(values, count):
    return lax.ppermute(values, "tensor", [(i, i ^ 1) for i in range(count)])


def plain(
    block_input, long_rows, short_rows, prev_states, norm1_gain, conv_weight, mixer_weight, gate_bias,
    out_weight, norm2_gain, up_weight, down_weight, cotangent,
):
    tokens, width = block_input.shape
    parts = lax.axis_size("tensor")
    me = lax.axis_index("tensor")
    rim = conv_weight.shape[0] - 1
    in_row, second, ends, slot = row_facts(long_rows, short_rows, me)
    mask = in_row.astype(F32)
    joined = second.astype(F32)
    even = (me % 2 == 0).astype(F32)
    slots = jnp.arange(prev_states.shape[0], dtype=jnp.int32)
    first_half = in_row & ~ends

    mixer_full = lax.all_gather(mixer_weight.astype(BF16), "tensor", axis=2, tiled=True)
    out_full = lax.all_gather(out_weight.astype(BF16), "tensor", axis=0, tiled=True)
    up_full = lax.all_gather(up_weight.astype(BF16), "tensor", axis=1, tiled=True)
    down_full = lax.all_gather(down_weight.astype(BF16), "tensor", axis=0, tiled=True)
    bias = lax.all_gather(gate_bias, "tensor", axis=0, tiled=True)
    prev = lax.all_gather(prev_states, "tensor", axis=1, tiled=True)
    start_state = jnp.sum(
        jnp.where((slots == slot)[:, None] & in_row & ~second, prev, 0.0), axis=0, keepdims=True
    )

    normed, norm1_back = jax.vjp(rms_norm, block_input, norm1_gain)
    rim_rows = pair_swap(normed[tokens - rim :], parts) * joined

    def convolve(extended, weight):
        total = weight[0] * extended[rim:]
        for tap in range(1, rim + 1):
            total = total + mask * weight[tap] * extended[rim - tap : rim - tap + tokens]
        return total

    conv_out, conv_back = jax.vjp(convolve, jnp.concatenate([rim_rows, normed], 0), conv_weight)
    conv_low = conv_out.astype(BF16)
    gate = contract(conv_low, mixer_full[0], (1, 0))
    cand = contract(conv_low, mixer_full[1], (1, 0))
    logit = gate + bias
    keep = jax.nn.sigmoid(-logit)
    opened = jax.nn.sigmoid(logit)
    soft = jax.nn.softplus(cand)
    factors, values = lax.associative_scan(combine, (keep, opened * soft), axis=0)
    ending = factors[-1:] * start_state + values[-1:]
    carry = start_state + joined * pair_swap(ending, parts)
    states = values + factors * carry
    before = jnp.concatenate([carry, states[:-1]], 0)
    end_table = jnp.where((slots == slot) & ends, 1.0, 0.0)[:, None]
    finals = lax.psum_scatter(end_table * states[-1:], "tensor", scatter_dimension=1, tiled=True)
    state_low = states.astype(BF16)
    mixed = contract(state_low, out_full, (1, 0))
    resid = block_input + mask * mixed
    normed_two, norm2_back = jax.vjp(rms_norm, resid, norm2_gain)
    normed_low = normed_two.astype(BF16)
    grad_branch = (mask * cotangent).astype(BF16)
    upward = contract(normed_low, up_full, (1, 0))
    activation, gelu_back = jax.vjp(lambda v: jax.nn.gelu(v, approximate=True), upward)
    activation_low = activation.astype(BF16)
    output = resid + mask * contract(activation_low, down_full, (1, 0))
    grad_act = contract(grad_branch, down_full, (1, 1))
    grad_up = gelu_back(grad_act)[0].astype(BF16)
    grad_norm_two = contract(grad_up, up_full, (1, 1))
    up_grad = contract(normed_low, grad_up, (0, 0))
    down_grad = contract(activation_low, grad_branch, (0, 0))
    grad_resid_norm, gain_two_part = norm2_back(grad_norm_two)
    grad_resid = cotangent + grad_resid_norm
    grad_mixed = (mask * grad_resid).astype(BF16)
    out_grad = contract(state_low, grad_mixed, (0, 0))
    grad_states = contract(grad_mixed, out_full, (1, 1))
    later_keep = jnp.concatenate([keep[1:], jnp.ones_like(keep[:1])], 0)
    back_factors, back_values = lax.associative_scan(combine, (later_keep, grad_states), axis=0, reverse=True)
    joins_next = (first_half & (me % 2 == 0)).astype(F32)
    back_carry = joins_next * pair_swap(keep[:1] * back_values[:1], parts)
    carried = back_values + back_factors * back_carry
    grad_logit = carried * (soft - before) * opened * (1 - opened)
    grad_cand = carried * opened * jax.nn.sigmoid(cand)
    bias_part = jnp.sum(grad_logit, axis=0)
    grad_logit_low = grad_logit.astype(BF16)
    grad_cand_low = grad_cand.astype(BF16)
    mixer_grad = jnp.stack([contract(conv_low, grad_logit_low, (0, 0)), contract(conv_low, grad_cand_low, (0, 0))])
    grad_conv = contract(grad_logit_low, mixer_full[0], (1, 1)) + contract(grad_cand_low, mixer_full[1], (1, 1))
    grad_extended, taps_part = conv_back(grad_conv)
    returned = joins_next * pair_swap(joined * grad_extended[:rim], parts)
    grad_normed = grad_extended[rim:] + jnp.concatenate(
        [jnp.zeros((tokens - rim, width), F32), returned], 0
    )
    grad_input_norm, gain_one_part = norm1_back(grad_normed)
    input_grad = grad_resid + grad_input_norm

    def scatter(grad, dim):
        return lax.psum_scatter(grad.astype(BF16), "tensor", scatter_dimension=dim, tiled=True)

    sharded = (
        scatter(mixer_grad, 2), scatter(out_grad, 0), scatter(up_grad, 1), scatter(down_grad, 0),
    )
    summed = tuple(g.astype(F32) for g in lax.psum(sharded, "dp"))
    shared = lax.psum((gain_one_part, taps_part, gain_two_part, bias_part), ("dp", "tensor"))
    channels = gate_bias.shape[0]
    bias_grad = lax.dynamic_slice_in_dim(shared[3], me * channels, channels)
    return (
        output, finals, input_grad, shared[0], shared[1], summed[0], bias_grad, summed[1], shared[2], summed[2], summed[3],
    )


LANES = 8
MESH = pl.DeviceIdType.MESH
CHUNKS = (2, 1, 2, 1, 2, 4)
FIRST = "yyxxy"
WIRES = 256
SCHEDULE = {
    "own0": (("g", "mix", "y"),),
    "sib": (("g", "out", "y"),),
    "mixfar!": (("g", "up", "y"), ("g", "mix", "x"), ("g", "mix", "z"), ("g", "out", "x"), ("g", "out", "z"), ("g", "down", "y"), ("g", "up", "x"), ("g", "up", "z"), ("g", "mix", "d")),
    "mixpass!": (("g", "out", "d"),),
    "chain": (("g", "down", "x"), ("g", "down", "z")),
    "end!": (("g", "up", "d"),),
    "states": (("g", "down", "d"),),
    "f02a": (("down0", "xa", 0, 0), ("down0", "xa", 0, 1)),
    "f10a": (("up0", "y", 0), ("up0", "y", 1), ("down0", "xa", 1, 0), ("down0", "xa", 1, 1)),
    "f12a": (("down0", "ya", 0), ("up0", "x", 0), ("down0", "ya", 1), ("down1", "xa", 1, 0), ("up1", "y", 0)),
    "f13a": (("up0", "x", 1),),
    "f13u": (("up0", "z", 0), ("down0", "z", 0)),
    "f13d": (("down1", "xa", 0, 0),),
    "B1a": (("down0", "z", 1),),
    "B1b": (("down1", "ya", 0),),
    "og0": (("up0", "zb", 0), ("up0", "z", 1)),
    "r1s": (("down0", "zb", 0),),
    "r1w!": (("up1", "x", 0), ("down0", "zb", 1), ("out", "y", 0), ("out", "y", 1)),
    "r1w0": (("up0", "xb", 0), ("down1", "z", 0)),
    "r1k1": (("up0", "zb", 1),),
    "r1e0": (("down0", "xb", 0), ("out", "x", 0), ("up1", "z", 0), ("mix", "y", 0), ("down0", "xb", 1), ("mix", "y", 1), ("mix", "y", 2), ("mix", "y", 3)),
    "r0s": (("out", "x", 1), ("down1", "zb", 0)),
    "r0w!": (("out", "z", 0), ("up0", "xb", 1)),
    "r0k1": (("out", "z", 1), ("up1", "zb", 0)),
    "r0e1": (("mix", "x", 0), ("mix", "x", 1), ("down1", "xb", 0)),
    "halo!": (("mix", "x", 2), ("out", "zb", 0)),
    "n1a": (("out", "zb", 1),),
    "n1b": (("mix", "z", 0), ("mix", "x", 3)),
    "drain": (("mix", "z", 1), ("up1", "xb", 0), ("pk", "chip"), ("out", "xb", 0), ("out", "xb", 1), ("mix", "z", 2), ("pk", "x"), ("mix", "zb", 0), ("mix", "z", 3), ("mix", "zb", 1), ("mix", "zb", 2), ("mix", "xb", 0), ("mix", "zb", 3), ("pk", "z"), ("mix", "xb", 1), ("mix", "xb", 2), ("mix", "xb", 3)),
}
GELU_A = 0.7978845608028654
GELU_B = 0.044715


def dot(left, right, dims=(1, 0)):
    return lax.dot_general(left, right, ((dims[:1], dims[1:]), ((), ())), preferred_element_type=F32)


def rows_of(block, width):
    return block.reshape(-1, width)


class Wires:
    def __init__(self, send, recv):
        self.send, self.recv, self.used = send, recv, 0

    def copy(self, src, dst, device):
        k = self.used
        self.used += 1
        return pltpu.make_async_remote_copy(
            src_ref=src, dst_ref=dst, send_sem=self.send.at[k], recv_sem=self.recv.at[k],
            device_id=device, device_id_type=MESH,
        )


def block_kernel(
    sizes, long_ref, short_ref, x_hbm, cot_hbm, prev_ref, bias_ref, gain1_ref, taps_ref, gain2_ref, mix_hbm, outw_hbm, up_hbm,
    down_hbm,
    cb, xb, finals_ref, small_ref, fin_up0, fin_up1, fin_down0, fin_down1, fin_out, fin_mix,
    n1h, res, gn2, fo, conv, n2, gm, act, gup, sig, st, ab, sp, sl,
    mix, outw, up, down,
    *rest,
):
    parts, rest = rest[:5], rest[5:]
    buffers, rest = [rest[5 * k : 5 * k + 5] for k in range(5)], rest[25:]
    (
        ry_mix, kx_mix, rx_mix, rz_mix,
        prev, biases, halo1, halo2, endrow, endin, brow, bin_, fsend, frecv,
        acc_n1, acc_n2, acc_t, acc_b, pk, pk_core, pk_chip, pk_x, pk_z,
        send_sem, recv_sem, local_sem,
    ) = rest
    n, z_count, tokens, width, hs, fs, slots, rim = sizes
    chips = n // 2
    steps = tokens // LANES
    tile = 256
    tiles = tokens // tile
    half_tiles = tiles // 2
    me = lax.axis_index("tensor")
    q, c = me // 2, me % 2
    dp = lax.axis_index("dp")
    z, x = dp // 2, dp % 2
    wires = Wires(send_sem, recv_sem)
    started = []

    def tensor(j):
        return (dp, j)

    sibling = tensor(me + 1 - 2 * c)
    partner = (dp + 1 - 2 * x, me)

    zb = z % 2
    z_partner = ((z + 1 - 2 * zb) * 2 + x, me)

    def z_peer(d):
        return ((((z + d) % z_count) * 2) + x, me)

    def shard_of(d, core):
        return ((q + d) % chips) * 2 + core

    def go(copy):
        copy.start()
        started.append(copy)
        return copy

    locals_ = [
        (mix_hbm.at[0], ab.at[0, pl.ds(0, width)]), (mix_hbm.at[1], ab.at[0, pl.ds(width, width)]),
        (outw_hbm, gn2.at[pl.ds(0, hs)]), (up_hbm, fo.at[pl.ds(0, width)]), (down_hbm, fo.at[pl.ds(width, fs)]),
    ]
    loads = [pltpu.make_async_copy(s, d, local_sem.at[i]) for i, (s, d) in enumerate(locals_)]

    def run(ref, g):
        return ref.at[pl.ds(g * steps, steps)]

    x_loads = [pltpu.make_async_copy(run(x_hbm, g), xb.at[:, g, :], local_sem.at[5 + g]) for g in range(LANES)]
    cot_loads = [pltpu.make_async_copy(run(cot_hbm, g), cb.at[:, g, :], local_sem.at[5 + LANES + g]) for g in range(LANES)]
    for copy in loads[:2] + x_loads + loads[2:] + cot_loads:
        copy.start()

    barrier = pltpu.get_barrier_semaphore()
    peers = [tensor((me + d) % n) for d in range(1, n)] + [partner] + [z_peer(d) for d in range(1, z_count)]
    for peer in peers:
        pl.semaphore_signal(barrier, inc=1, device_id=peer, device_id_type=MESH)

    long_count, short_count = long_ref[0], short_ref[0]
    is_long = jnp.where(me < 2 * long_count, 1.0, 0.0)
    in_row = jnp.where(me < 2 * long_count + short_count, 1.0, 0.0)
    odd = (me % 2).astype(F32)
    joined = is_long * odd
    joins_next = is_long * (1.0 - odd)
    starts = in_row * (1.0 - joined)
    ends = in_row * (1.0 - joins_next)
    slot = jnp.where(me < 2 * long_count, me // 2, me - long_count)
    slot_mask = [jnp.where(slot == s, 1.0, 0.0) for s in range(slots)]

    gathers = {}

    weight_copies = []

    def gather(name, ref):
        r = shard_of(1, c)
        mine, own = ref.at[me, 2 * x + zb], ref.at[r, 2 * x + zb]
        by_x, by_z, corner = ref.at[r, 2 * (1 - x) + zb], ref.at[r, 2 * x + 1 - zb], ref.at[r, 2 * (1 - x) + 1 - zb]
        far = go(wires.copy(mine, mine, tensor(r)))
        sib = go(wires.copy(ref.at[me], ref.at[me], sibling))
        weight_copies.extend((far, sib))
        gathers[name] = dict(
            far=far, sib=sib, ax=wires.copy(own, own, partner), az=wires.copy(own, own, z_partner),
            dz=wires.copy(by_x.at[0], by_x.at[0], z_partner), dx=wires.copy(by_z.at[1], by_z.at[1], partner),
            passed=[wires.copy(part, part, sibling) for part in (own, by_x, by_z, corner)],
        )

    def gather_step(arrived, *then):
        def step(name):
            copies = gathers[name]
            for key in arrived:
                copies[key].wait_recv()
            for key in then:
                weight_copies.append(go(copies["passed"][key] if isinstance(key, int) else copies[key]))

        return step

    def gather_passed(name):
        for copy in gathers[name]["passed"]:
            copy.wait_recv()

    stages = {
        ("g", "y"): gather_step(("far",), "ax", "az", 0), ("g", "x"): gather_step(("ax",), "dz", 1),
        ("g", "z"): gather_step(("az",), "dx", 2), ("g", "d"): gather_step(("dz", "dx"), 3),
    }

    def run_stages(hook):
        for step in SCHEDULE.get(hook, ()):
            if step[0] == "g":
                stages["g", step[2]](step[1], *step[3:])
            else:
                stages[step[:2]](*step[2:])

    prev[me] = prev_ref[...]
    biases[me] = bias_ref[...]
    loads[0].wait()
    loads[1].wait()
    half = width // 2
    for h in range(2):
        mix[me, pl.ds(2 * h, 2)] = (
            jnp.concatenate([ab[0, pl.ds(h * half, half), :], ab[0, pl.ds(width + h * half, half), :]], axis=1)
            .astype(BF16)
            .reshape((2,) + mix.shape[2:])
        )
    pl.semaphore_wait(barrier, len(peers))
    gather("mix", mix)
    lead_copies = []
    for ref in (prev, biases):
        lead_copies += [go(wires.copy(ref.at[me], ref.at[me], tensor((me + d) % n))) for d in range(1, n)]
    loads[2].wait()
    outw[me] = gn2[pl.ds(0, hs), :].astype(BF16).reshape(outw.shape[1:])
    gather("out", outw)
    loads[3].wait()
    up[me] = fo[pl.ds(0, width), :].astype(BF16).reshape(up.shape[1:])
    gather("up", up)
    loads[4].wait()
    down[me] = fo[pl.ds(width, fs), :].astype(BF16).reshape(down.shape[1:])
    gather("down", down)

    span = 64
    spans = tokens // span

    def at(i, shift=0, size=span):
        return pl.ds(pl.multiple_of(i * size + shift, LANES), size)

    def take(ref, i, size=span):
        return ref[pl.ds(i * (size // LANES), size // LANES)].reshape(size, width)

    def put(ref, i, value):
        ref[pl.ds(i * (span // LANES), span // LANES)] = value.reshape(span // LANES, LANES, width)

    def eights(value):
        return jnp.sum(value.reshape(-1, LANES, value.shape[-1]), axis=0)

    hook = run_stages
    for copy in x_loads:
        copy.wait()
    gain1 = gain1_ref[...]
    gain2 = gain2_ref[...]

    def norm1_rows(i):
        v = take(xb, i)
        scale = lax.rsqrt(jnp.mean(v * v, axis=-1, keepdims=True) + epsilon)
        n1h[at(i, rim * LANES), :] = v * scale * gain1

    for part, (begin, stop) in enumerate(((0, 6), (6, 11), (11, 16))):
        pl.loop(begin * spans // 16, stop * spans // 16, unroll=True)(norm1_rows)
        if part < 2:
            hook(f"n1a{part}")

    hook("norm1")
    edge = rim * LANES
    halo_copy = go(wires.copy(n1h.at[pl.ds(tokens, edge)], halo1, sibling))
    halo_copy.wait_recv()
    sub = lax.broadcasted_iota(jnp.int32, (LANES, width), 0)
    for k in range(rim):
        own = pltpu.roll(n1h[pl.ds(tokens + k * LANES, LANES), :], 1, 0)
        other = pltpu.roll(halo1[pl.ds(k * LANES, LANES), :], 1, 0)
        n1h[pl.ds(k * LANES, LANES), :] = jnp.where(sub == 0, joined * other, own)
    tap = [taps_ref[pl.ds(k, 1), :] * (1.0 if k == 0 else in_row) for k in range(rim + 1)]

    def conv_rows(i):
        total = tap[0] * n1h[at(i, edge), :]
        for k in range(1, rim + 1):
            total = total + tap[k] * n1h[at(i, edge - k * LANES), :]
        conv[at(i), :] = total.astype(BF16)

    pl.loop(0, spans // 2, unroll=4)(conv_rows)
    hook("cv0")
    pl.loop(spans // 2, spans, unroll=4)(conv_rows)

    def project(j, between=None):
        weight = rows_of(mix[j], 2 * hs)
        bias = biases[j]

        def some(t):
            rows = at(t, 0, tile)
            pre = dot(conv[rows, :], weight)
            logit = pre[:, :hs] + bias
            cand = pre[:, hs:]
            e = jnp.exp(-jnp.abs(logit))
            r = 1.0 / (1.0 + e)
            opened = jnp.where(logit >= 0, r, e * r)
            keep = jnp.where(logit >= 0, e * r, r)
            soft = jnp.maximum(cand, 0.0) + jnp.log1p(jnp.exp(-jnp.abs(cand)))
            sig[j, rows, :] = opened
            sp[j, rows, :] = soft
            ab[j, rows, :] = keep * in_row
            st[j, at(t, LANES, tile), :] = opened * soft

        if between is None:
            pl.loop(0, tiles, unroll=tiles)(some)
        else:
            pl.loop(0, half_tiles, unroll=half_tiles)(some)
            hook(between)
            pl.loop(half_tiles, tiles, unroll=half_tiles)(some)

    hook("conv")
    for copy in lead_copies:
        copy.wait_recv()
    project(me, "own0")
    hook("own")
    gathers["mix"]["sib"].wait_recv()
    project(me + 1 - 2 * c, "sib0")
    hook("sib")

    def unrolled(count, step, carry, by=4):
        def some(i, carry):
            for k in range(by):
                carry = step(i * by + k, carry)
            return carry

        return lax.fori_loop(0, count // by, some, carry)

    one = jnp.ones((LANES, hs), F32)
    zero = jnp.zeros((LANES, hs), F32)

    def scan(js):
        def step(s, carry):
            rows = at(s, 0, LANES)
            later = at(s, LANES, LANES)
            out = []
            for j, (fac, val) in zip(js, carry):
                a = ab[j, rows, :]
                fac = a * fac
                val = a * val + st[j, later, :]
                ab[j, rows, :] = fac
                st[j, later, :] = val
                out.append((fac, val))
            return tuple(out)

        unrolled(steps, step, tuple((one, zero) for _ in js))

    scan([me, me + 1 - 2 * c])
    hook("scan1")
    for copy in cot_loads:
        copy.wait()

    @pl.loop(0, spans, unroll=4)
    def _(i):
        gm[at(i), :] = (in_row * take(cb, i)).astype(BF16)

    hook("gm")
    hook("mixfar!")
    project(shard_of(1, c))
    hook("rown")
    hook("mixpass!")
    gather_passed("mix")
    project(shard_of(1, 1 - c))
    hook("rsib")
    scan([shard_of(1, c), shard_of(1, 1 - c)])
    hook("scan2")
    last = pl.ds(tokens - LANES, LANES)

    def chain(j, carry, keep_rows):
        fac = ab[j, last, :]
        val = st[j, pl.ds(tokens, LANES), :]
        rows = []
        for g in range(LANES):
            rows.append(carry)
            carry = fac[g : g + 1] * carry + val[g : g + 1]
        if keep_rows:
            st[j, pl.ds(0, LANES), :] = jnp.concatenate(rows, axis=0)
        return carry

    first = []
    for j in range(n):
        begin = jnp.zeros((1, hs), F32)
        for s in range(slots):
            begin = begin + (starts * slot_mask[s]) * prev[j, pl.ds(s, 1), :]
        first.append(begin)
        endrow[j] = chain(j, begin, False)
    end_copy = go(wires.copy(endrow, endin, sibling))
    hook("chain")
    hook("end!")
    end_copy.wait_recv()
    for j in range(n):
        ending = chain(j, first[j] + joined * endin[j], True)
        for s in range(slots):
            fsend[j, pl.ds(s, 1), :] = (ends * slot_mask[s]) * ending
    final_copies = [
        go(wires.copy(fsend.at[(me + d) % n], frecv.at[d - 1], tensor((me + d) % n))) for d in range(1, n)
    ]

    hook("chain2")
    hook("out!")
    gathers["out"]["sib"].wait_recv()
    gather_passed("out")
    @pl.loop(0, tiles, unroll=tiles)
    def _(t):
        rows = at(t, 0, tile)
        mixed = jnp.zeros((tile, width), F32)
        for j in range(n):
            into = st[j, pl.ds(0, LANES), :]
            value = st[j, at(t, LANES, tile), :] + (
                ab[j, rows, :].reshape(-1, LANES, hs) * into[None]
            ).reshape(tile, hs)
            st[j, at(t, LANES, tile), :] = value
            low = value.astype(BF16)
            sl[j, rows, :] = low
            mixed = mixed + dot(low, rows_of(outw[j], width))
        resid = take(xb, t, tile) + in_row * mixed
        res[rows, :] = resid
        scale = lax.rsqrt(jnp.mean(resid * resid, axis=-1, keepdims=True) + epsilon)
        n2[rows, :] = (resid * scale * gain2).astype(BF16)

    hook("states")
    gathers["up"]["sib"].wait_recv()
    gathers["down"]["sib"].wait_recv()

    def far_weights():
        hook("updown!")
        gather_passed("up")
        gather_passed("down")


    class Sum:
        def __init__(self, part, rc, ry, kx, rx, rz, fin):
            self.part, self.rc, self.ry, self.kx, self.rx, self.rz, self.fin = part, rc, ry, kx, rx, rz, fin
            self.chunks = fin.shape[0]
            self.c1 = [None] * chips
            self.c2, self.c3, self.c4, self.c5, self.c6 = {}, {}, {}, {}, {}
            self.first = wires.used
            wires.used += chips

        def one(self, d):
            copy = pltpu.make_async_remote_copy(
                src_ref=self.part.at[shard_of(d, 1 - c)], dst_ref=self.rc.at[d], send_sem=send_sem.at[self.first + d],
                recv_sem=recv_sem.at[self.first + d], device_id=sibling, device_id_type=MESH,
            )
            self.c1[d] = go(copy)

        def both(self, j, d, k, h):
            return self.part[j, k, h].astype(F32) + self.rc[d, k, h].astype(F32)

        def y(self, k=0):
            self.c2[k] = []
            for d in range(1, chips):
                if k == 0:
                    self.c1[d].wait_recv()
                j = shard_of(d, c)
                for h in range(2):
                    self.part[j, k, h] = self.both(j, d, k, h).astype(BF16)
                self.c2[k].append(go(wires.copy(self.part.at[j, k], self.ry.at[d - 1, k], tensor(j))))

        def total(self, k, h):
            v = self.both(me, 0, k, h)
            for d in range(chips - 1):
                v = v + self.ry[d, k, h].astype(F32)
            return v

        def x(self, k=0):
            if k == 0:
                self.c1[0].wait_recv()
            for copy in self.c2[k]:
                copy.wait_recv()
            self.part[me, k, 1 - x] = self.total(k, 1 - x).astype(BF16)
            self.c3[k] = go(wires.copy(self.part.at[me, k, 1 - x], self.rx.at[k], partner))
            self.kx[k] = self.total(k, x)

        def z(self, k=0):
            self.c3[k].wait_recv()
            self.spread(k, self.kx[k] + self.rx[k].astype(F32))

        def spread(self, k, v):
            self.kx[k] = v
            self.part[me, k, x] = v.astype(BF16)
            self.c4[k] = [
                go(wires.copy(self.part.at[me, k, x, (z + d) % z_count], self.rz.at[d - 1, k], z_peer(d)))
                for d in range(1, z_count)
            ]

        def zb(self, k=0):
            for copy in self.c4[k]:
                copy.wait_recv()
            v = self.kx[k, z]
            for d in range(z_count - 1):
                v = v + self.rz[d, k].astype(F32)
            self.fin[k, x, z] = v.astype(BF16)
            mine = self.fin.at[k, x, z]
            self.c5[k] = [go(wires.copy(mine, mine, z_peer(d))) for d in range(1, z_count)]
            self.c6[k] = [go(wires.copy(mine, mine, partner))]

        def xb(self, k=0):
            for d in range(1, z_count):
                self.c5[k][d - 1].wait_recv()
                theirs = self.fin.at[k, x, (z + z_count - d) % z_count]
                self.c6[k].append(go(wires.copy(theirs, theirs, partner)))

        def end(self):
            for k in range(self.chunks):
                for copy in self.c6[k]:
                    copy.wait_recv()

    class SumAcross(Sum):
        def xa(self, d, k=0):
            if k == 0:
                self.c1[d].wait_recv()
            j = shard_of(d, c)
            self.part[j, k, 1 - x] = self.both(j, d, k, 1 - x).astype(BF16)
            self.c3[d, k] = go(wires.copy(self.part.at[j, k, 1 - x], self.rx.at[d, k], partner))

        def ya(self, k=0):
            self.c3[1, k].wait_recv()
            j = shard_of(1, c)
            self.part[j, k, x] = (self.both(j, 1, k, x) + self.rx[1, k].astype(F32)).astype(BF16)
            self.c2[k] = go(wires.copy(self.part.at[j, k, x], self.ry.at[k], tensor(j)))

        def z(self, k=0):
            self.c3[0, k].wait_recv()
            self.c2[k].wait_recv()
            self.spread(k, self.both(me, 0, k, x) + self.rx[0, k].astype(F32) + self.ry[k].astype(F32))

    s_parts = [
        (SumAcross if first == "x" else Sum)(part, *refs, fin)
        for first, part, refs, fin in zip(FIRST, parts, buffers, (fin_up0, fin_up1, fin_down0, fin_down1, fin_out))
    ]
    s_out = s_parts[4]
    s_mix = Sum(up, down, ry_mix, kx_mix, rx_mix, rz_mix, fin_mix)
    for name, unit in zip(("up0", "up1", "down0", "down1", "out", "mix"), s_parts + [s_mix]):
        for stage in ("y", "x", "xa", "ya", "z", "zb", "xb"):
            stages[name, stage] = getattr(unit, stage, None)

    def weight_grad(unit, j, left, right):
        unit.part[j] = dot(left, right, (0, 0)).astype(BF16).reshape(unit.part.shape[1:])

    fh = fs // 2

    def feed(j, h, name, d=None, begin=False):
        cols = pl.ds(h * fh, fh)
        chunks = down.shape[1] // 2

        @pl.loop(0, tiles, unroll=tiles)
        def _(t):
            rows = at(t, 0, tile)
            upw = rows_of(up[j, :, :, :, :, cols], fh)
            downw = rows_of(down[j, pl.ds(h * chunks, chunks)], width)
            u = dot(n2[rows, :], upw)
            ga = dot(gm[rows, :], downw, (1, 1))
            u2 = u * u
            th = jnp.tanh(GELU_A * u * (1.0 + GELU_B * u2))
            hp = 0.5 + 0.5 * th
            a = (u * hp).astype(BF16)
            slope = hp + (0.5 * GELU_A) * u * (1.0 - th * th) * (1.0 + 3.0 * GELU_B * u2)
            gu = (ga * slope).astype(BF16)
            act[rows, cols] = a
            gup[rows, cols] = gu
            o = dot(a, downw)
            g = dot(gu, upw, (1, 1))
            if begin:
                fo[rows, :] = o
                gn2[rows, :] = g
            else:
                fo[rows, :] = fo[rows, :] + o
                gn2[rows, :] = gn2[rows, :] + g

        hook(name + "a")
        for unit, left, right, end in ((s_parts[h], n2, gup, "u"), (s_parts[2 + h], gm, act, "d")):
            weight_grad(unit, j, left[...], right[:, cols])
            if d is not None:
                unit.one(d)
            hook(name + end)

    feed(me + 1 - 2 * c, 0, "f00", 0, True)
    feed(me, 0, "f01")
    far_weights()
    feed(shard_of(1, 1 - c), 0, "f02", 1)
    feed(shard_of(1, c), 0, "f03")
    feed(shard_of(1, 1 - c), 1, "f10", 1)
    feed(shard_of(1, c), 1, "f11")
    feed(me + 1 - 2 * c, 1, "f12", 0)
    feed(me, 1, "f13")

    acc_n2[...] = jnp.zeros_like(acc_n2)

    def norm2_back(i):
        r = res[at(i), :]
        g = gn2[at(i), :]
        scale = lax.rsqrt(jnp.mean(r * r, axis=-1, keepdims=True) + epsilon)
        gg = g * gain2
        m = jnp.mean(gg * r, axis=-1, keepdims=True)
        gr = take(cb, i) + scale * gg - r * (scale * scale * scale * m)
        acc_n2[...] += eights(g * r * scale)
        gn2[at(i), :] = gr
        gm[at(i), :] = (in_row * gr).astype(BF16)
        put(cb, i, r + in_row * fo[at(i), :])

    pl.loop(0, spans // 2, unroll=2)(norm2_back)
    hook("B1a")
    pl.loop(spans // 2, spans, unroll=2)(norm2_back)
    hook("B1b")

    def store(ref, hbm, first):
        copies = [pltpu.make_async_copy(ref.at[:, g, :], run(hbm, g), local_sem.at[first + g]) for g in range(LANES)]
        for copy in copies:
            copy.start()
        return copies

    for copy in weight_copies:
        copy.wait_send()
    started[:] = [copy for copy in started if not any(copy is other for other in weight_copies)]

    for d in (1, 0):
        for core in (1 - c, c):
            j = shard_of(d, core)
            weight_grad(s_out, j, gm[...], sl[j])
        s_out.one(d)
    hook("og0")

    for j in range(n):
        acc_b[j] = jnp.zeros((LANES, hs), F32)

    def recur_back(d, begin, name):
        js = [shard_of(d, core) for core in range(2)]
        for k in range(2):
            ab[k] = dot(gm[...], rows_of(outw[js[k]], width), (1, 1))
        hook(name + "g")

        def back_step(i, carry):
            s = steps - 1 - i
            rows = at(s, 0, LANES)
            out = []
            for k in range(2):
                fac, val, keep = carry[k]
                fac = keep * fac
                val = ab[k, rows, :] + keep * val
                ab[2 + k, rows, :] = fac
                ab[k, rows, :] = val
                out.append((fac, val, 1.0 - sig[js[k], rows, :]))
            return tuple(out)

        unrolled(steps, back_step, ((one, zero, one), (one, zero, one)))
        hook(name + "s")

        def chain_back(k, carry, j):
            fac = ab[2 + k, pl.ds(0, LANES), :]
            val = ab[k, pl.ds(0, LANES), :]
            keep = 1.0 - sig[j, pl.ds(0, LANES), :]
            rows = []
            for g in reversed(range(LANES)):
                rows.append(carry)
                carry = keep[g : g + 1] * (val[g : g + 1] + fac[g : g + 1] * carry)
            return carry, jnp.concatenate(rows[::-1], axis=0)

        slot_ = 2 * d
        for k in range(2):
            brow[slot_ + k] = chain_back(k, jnp.zeros((1, hs), F32), js[k])[0]
        copy = go(wires.copy(brow.at[pl.ds(slot_, 2)], bin_.at[pl.ds(slot_, 2)], sibling))
        hook(name + "c")
        hook(name + "w!")
        copy.wait_recv()
        grads = (act, gup)
        order = [(1 - c, shard_of(d, 1 - c)), (c, shard_of(d, c))]
        for g, (k, j) in enumerate(order):
            into = chain_back(k, joins_next * bin_[slot_ + k], j)[1]

            @pl.loop(0, tiles, unroll=tiles)
            def _(t, j=j, k=k, g=g, into=into):
                rows = at(t, 0, tile)
                carried = ab[k, rows, :] + (ab[2 + k, rows, :].reshape(-1, LANES, hs) * into[None]).reshape(tile, hs)
                opened = sig[j, rows, :]
                soft = sp[j, rows, :]
                weighted = carried * opened
                gl = weighted * (soft - st[j, rows, :]) * (1.0 - opened)
                close = jnp.where(soft < 0.01, soft * (1.0 - soft * (0.5 - soft * (1.0 / 6.0))), 1.0 - jnp.exp(-soft))
                gc = weighted * close
                acc_b[j] += eights(gl)
                grads[g][rows, :] = jnp.concatenate([gl.astype(BF16), gc.astype(BF16)], axis=1)

            hook(f"{name}k{g}")
            weight_grad(s_mix, j, conv[...], grads[g][...])
            if g == 0:
                s_mix.one(d)
            hook(f"{name}w{g}")

        def gather_back(t):
            rows = at(t, 0, tile)
            back = sum(dot(left[rows, :], rows_of(mix[j], 2 * hs), (1, 1)) for left, (_, j) in zip(grads, order))
            res[rows, :] = back if begin else res[rows, :] + back

        pl.loop(0, half_tiles, unroll=half_tiles)(gather_back)
        hook(name + "e0")
        pl.loop(half_tiles, tiles, unroll=half_tiles)(gather_back)
        hook(name + "e1")

    recur_back(1, True, "r1")
    recur_back(0, False, "r0")
    halo_back = go(wires.copy(res.at[pl.ds(0, edge)], halo2, sibling))
    hook("halo!")
    halo_back.wait_recv()

    for k in range(rim):
        own = pltpu.roll(res[pl.ds(k * LANES, LANES), :], LANES - 1, 0)
        other = pltpu.roll(halo2[pl.ds(k * LANES, LANES), :], LANES - 1, 0)
        res[pl.ds(tokens + k * LANES, LANES), :] = jnp.where(sub == LANES - 1, joins_next * other, own)
    acc_n1[...] = jnp.zeros_like(acc_n1)
    acc_t[...] = jnp.zeros_like(acc_t)

    def norm1_back(i):
        g0 = res[at(i), :]
        total = tap[0] * g0
        acc_t[0] += eights(g0 * n1h[at(i, edge), :])
        for k in range(1, rim + 1):
            total = total + tap[k] * res[at(i, k * LANES), :]
            acc_t[k] += eights(g0 * n1h[at(i, edge - k * LANES), :])
        v = take(xb, i)
        scale = lax.rsqrt(jnp.mean(v * v, axis=-1, keepdims=True) + epsilon)
        gg = total * gain1
        m = jnp.mean(gg * v, axis=-1, keepdims=True)
        acc_n1[...] += eights(total * v * scale)
        put(xb, i, gn2[at(i), :] + scale * gg - v * (scale * scale * scale * m))

    pl.loop(0, spans // 2, unroll=2)(norm1_back)
    hook("n1a")
    pl.loop(spans // 2, spans, unroll=2)(norm1_back)
    hook("n1b")

    pk[...] = jnp.zeros_like(pk)
    pk[pl.ds(0, 1), :] = jnp.sum(acc_n1[...], axis=0, keepdims=True)
    for k in range(rim + 1):
        pk[pl.ds(1 + k, 1), :] = jnp.sum(acc_t[k], axis=0, keepdims=True)
    pk[pl.ds(6, 1), :] = jnp.sum(acc_n2[...], axis=0, keepdims=True)
    for j in range(n):
        pk[pl.ds(8 + j, 1), pl.ds(0, hs)] = jnp.sum(acc_b[j], axis=0, keepdims=True)
    k1 = go(wires.copy(pk, pk_core, sibling))
    small_copies = {}

    def small_chip():
        k1.wait_recv()
        pk_chip[q] = pk[...] + pk_core[...]
        small_copies[2] = go(wires.copy(pk_chip.at[q], pk_chip.at[q], tensor(shard_of(1, c))))

    def small_x():
        small_copies[2].wait_recv()
        pk_x[0] = pk_chip[0] + pk_chip[1]
        small_copies[3] = go(wires.copy(pk_x.at[0], pk_x.at[1], partner))

    def small_z():
        small_copies[3].wait_recv()
        pk_z[z] = pk_x[0] + pk_x[1]
        small_copies[4] = [go(wires.copy(pk_z.at[z], pk_z.at[z], z_peer(d))) for d in range(1, z_count)]

    stages["pk", "chip"], stages["pk", "x"], stages["pk", "z"] = small_chip, small_x, small_z
    hook("pk")
    hook("drain")
    for copy in final_copies:
        copy.wait_recv()
    total = fsend[me]
    for d in range(n - 1):
        total = total + frecv[d]
    finals_ref[...] = total
    for copy in small_copies[4]:
        copy.wait_recv()
    value = pk_z[0]
    for k in range(1, z_count):
        value = value + pk_z[k]
    small_ref[...] = value
    for unit in s_parts + [s_mix]:
        unit.end()
    for copy in started:
        copy.wait_send()


def last_kernel(
    hs, output_in, igrad_in, finals_in, small, g_up0, g_up1, g_down0, g_down1, g_out, g_mix,
    output, finals, igrad, gain1, taps, mixer, bias, outw, gain2, up, down, mixer_v, outw_v, up_v, down_v, sem,
):
    width = up_v.shape[0]
    steps = output_in.shape[0]
    later = []
    for k, (src, dst) in enumerate(((output_in, output), (igrad_in, igrad))):
        for g in range(LANES):
            later.append(pltpu.make_async_copy(src.at[:, g, :], dst.at[pl.ds(g * steps, steps)], sem.at[8 + k * LANES + g]))
            later[-1].start()
    me = lax.axis_index("tensor")
    fh = up_v.shape[1] // 2
    up_v[:, :fh] = rows_of(g_up0[...], fh).astype(F32)
    up_v[:, fh:] = rows_of(g_up1[...], fh).astype(F32)
    later.append(pltpu.make_async_copy(up_v, up, sem.at[2]))
    later[-1].start()
    both = rows_of(g_mix[...], 2 * hs).astype(F32)
    mixer_v[0] = both[:, :hs]
    mixer_v[1] = both[:, hs:]
    later.append(pltpu.make_async_copy(mixer_v, mixer, sem.at[5]))
    later[-1].start()
    down_v[:fh] = rows_of(g_down0[...], fh).astype(F32).T
    down_v[fh:] = rows_of(g_down1[...], fh).astype(F32).T
    later.append(pltpu.make_async_copy(down_v, down, sem.at[6]))
    later[-1].start()
    outw_v[...] = rows_of(g_out[...], hs).astype(F32).T
    later.append(pltpu.make_async_copy(outw_v, outw, sem.at[7]))
    later[-1].start()
    finals[...] = finals_in[...]
    gain1[...] = small[pl.ds(0, 1), :]
    taps[...] = small[pl.ds(1, taps.shape[0]), :]
    gain2[...] = small[pl.ds(6, 1), :]
    bias[...] = small[pl.ds(8 + me, 1), pl.ds(0, hs)]
    for copy in later:
        copy.wait()


def fused(
    block_input, long_rows, short_rows, prev_states, norm1_gain, conv_weight, mixer_weight, gate_bias,
    out_weight, norm2_gain, up_weight, down_weight, cotangent,
):
    tokens, width = block_input.shape
    n = lax.axis_size("tensor")
    z_count = lax.axis_size("dp") // 2
    chips = n // 2
    slots, hs = prev_states.shape
    fs = up_weight.shape[1]
    rim = conv_weight.shape[0] - 1
    steps = tokens // LANES
    pk_rows = 8 + -(-n // 8) * 8
    units = [(chunks, cols) for chunks, cols in zip(CHUNKS, (fs // 2,) * 4 + (hs, 2 * hs))]

    def block(chunks, cols):
        return (chunks, 2, z_count, width // (2 * z_count * chunks), cols)

    def full(chunks, cols):
        return pltpu.VMEM((n,) + block(chunks, cols), BF16)

    def sums(chunks, cols, across=False):
        dims = block(chunks, cols)
        part = dims[2:]
        return [
            pltpu.VMEM((chips,) + dims, BF16),
            pltpu.VMEM((chunks,) + part if across else (chips - 1,) + dims, BF16),
            pltpu.VMEM((chunks,) + part, F32),
            pltpu.VMEM(((chips, chunks) if across else (chunks,)) + part, BF16),
            pltpu.VMEM((z_count - 1, chunks) + part[1:], BF16),
        ]

    def wide(rows, kind=F32):
        return pltpu.VMEM((rows, width), kind)

    permuted = pltpu.VMEM((steps, LANES, width), F32)
    per_block = pltpu.VMEM((n, tokens, hs), F32)
    scratch = [
        wide(tokens + rim * LANES), wide(tokens + rim * LANES), wide(tokens), wide(tokens),
        wide(tokens, BF16), wide(tokens, BF16), wide(tokens, BF16), pltpu.VMEM((tokens, fs), BF16), pltpu.VMEM((tokens, fs), BF16),
        per_block, pltpu.VMEM((n, tokens + LANES, hs), F32), per_block, per_block, pltpu.VMEM((n, tokens, hs), BF16),
        pltpu.VMEM((n, 4, 2, width // 8, 2 * hs), BF16), pltpu.VMEM((n, 4, 2, hs // 8, width), BF16), full(*units[5]), full(*units[5]),
        *[full(*unit) for unit in units[:5]],
        *[ref for unit, first in zip(units[:5], FIRST) for ref in sums(*unit, first == "x")], *sums(*units[5])[1:],
        pltpu.VMEM((n, slots, hs), F32), pltpu.VMEM((n, 1, hs), F32), wide(rim * LANES), wide(rim * LANES),
        pltpu.VMEM((n, 1, hs), F32), pltpu.VMEM((n, 1, hs), F32), pltpu.VMEM((n, 1, hs), F32), pltpu.VMEM((n, 1, hs), F32),
        pltpu.VMEM((n, slots, hs), F32), pltpu.VMEM((n - 1, slots, hs), F32),
        wide(LANES), wide(LANES), pltpu.VMEM((rim + 1, LANES, width), F32), pltpu.VMEM((n, LANES, hs), F32),
        wide(pk_rows), wide(pk_rows), pltpu.VMEM((chips, pk_rows, width), F32), pltpu.VMEM((2, pk_rows, width), F32),
        pltpu.VMEM((z_count, pk_rows, width), F32),
        pltpu.SemaphoreType.DMA((WIRES,)), pltpu.SemaphoreType.DMA((WIRES,)), pltpu.SemaphoreType.DMA((5 + 4 * LANES,)),
    ]
    vmem = pl.BlockSpec(memory_space=pltpu.VMEM)
    smem = pl.BlockSpec(memory_space=pltpu.SMEM)
    hbm = pl.BlockSpec(memory_space=pl.ANY)

    def shape(dims, kind=F32):
        return jax.ShapeDtypeStruct(dims, kind)

    big = shape((tokens, width))
    outs = pl.pallas_call(
        functools.partial(block_kernel, (n, z_count, tokens, width, hs, fs, slots, rim)),
        out_shape=[permuted, permuted, pltpu.VMEM((slots, hs), F32), pltpu.VMEM((pk_rows, width), F32), *[pltpu.VMEM(block(*unit), BF16) for unit in units]],
        in_specs=[smem, smem, hbm, hbm, vmem, vmem, vmem, vmem, vmem, hbm, hbm, hbm, hbm],
        out_specs=[vmem] * 10,
        scratch_shapes=scratch,
        compiler_params=pltpu.CompilerParams(collective_id=0, has_side_effects=True, vmem_limit_bytes=VMEM_LIMIT),
    )(
        long_rows, short_rows, block_input, cotangent, prev_states, gate_bias[None], norm1_gain[None], conv_weight,
        norm2_gain[None], mixer_weight, out_weight, up_weight, down_weight,
    )
    outs = pl.pallas_call(
        functools.partial(last_kernel, hs),
        out_shape=[
            big, shape((slots, hs)), big, shape((1, width)), shape((rim + 1, width)), shape((2, width, hs)), shape((1, hs)),
            shape((hs, width)), shape((1, width)), shape((width, fs)), shape((fs, width)),
        ],
        in_specs=[vmem] * 10,
        out_specs=[hbm, vmem, hbm, vmem, vmem, hbm, vmem, hbm, vmem, hbm, hbm],
        scratch_shapes=[
            pltpu.VMEM((2, width, hs), F32), wide(hs), pltpu.VMEM((width, fs), F32), wide(fs),
            pltpu.SemaphoreType.DMA((8 + 2 * LANES,)),
        ],
        compiler_params=pltpu.CompilerParams(vmem_limit_bytes=VMEM_LAST),
    )(*outs)
    output, finals, input_grad, gain1, taps, mixer, bias, outw, gain2, up, down = outs
    return (output, finals, input_grad, gain1[0], taps, mixer, bias[0], outw, gain2[0], up, down)


def solution(mesh):
    takes_kernel = mesh.shape["tensor"] == 4 and mesh.shape["dp"] == 8
    rows = P(("dp", "tensor"), None)
    placed = (
        rows, P("dp"), P("dp"), P("dp", "tensor"), P(), P(), P(None, None, "tensor"), P("tensor"),
        P("tensor", None), P(), P(None, "tensor"), P("tensor", None), rows,
    )
    return jax.shard_map(
        fused if takes_kernel else plain,
        mesh=mesh,
        in_specs=placed,
        out_specs=(
            rows, P("dp", "tensor"), rows, P(), P(), P(None, None, "tensor"), P("tensor"), P("tensor", None),
            P(), P(None, "tensor"), P("tensor", None),
        ),
        check_vma=False,
    )
```

```python
import functools

import jax
import jax.numpy as jnp
from jax import lax
from jax.experimental import pallas as pl
from jax.experimental.pallas import tpu as pltpu
from jax.sharding import PartitionSpec as P

SHORT = 1024
LONG = 2048
VMEM_LIMIT = 58 * 1024 * 1024
VMEM_LAST = 24 * 1024 * 1024
epsilon = 1e-06
BF16 = jnp.bfloat16
F32 = jnp.float32


def rms_norm(values, gain):
    return values * lax.rsqrt(jnp.mean(values * values, axis=-1, keepdims=True) + epsilon) * gain


def contract(left, right, dims):
    return lax.dot_general(left, right, ((dims[:1], dims[1:]), ((), ())), preferred_element_type=F32)


def combine(before_pair, after_pair):
    return (before_pair[0] * after_pair[0], after_pair[0] * before_pair[1] + after_pair[1])


def row_facts(long_rows, short_rows, chunk):
    long_count, short_count = long_rows[0], short_rows[0]
    in_long = chunk < 2 * long_count
    in_row = chunk < 2 * long_count + short_count
    second = in_long & (chunk % 2 == 1)
    ends = in_row & (second | ~in_long)
    slot = jnp.where(in_long, chunk // 2, chunk - long_count)
    return in_row, second, ends, slot


def pair_swap(values, count):
    return lax.ppermute(values, "tensor", [(i, i ^ 1) for i in range(count)])


def plain(
    block_input, long_rows, short_rows, prev_states, norm1_gain, conv_weight, mixer_weight, gate_bias,
    out_weight, norm2_gain, up_weight, down_weight, cotangent,
):
    tokens, width = block_input.shape
    parts = lax.axis_size("tensor")
    me = lax.axis_index("tensor")
    rim = conv_weight.shape[0] - 1
    in_row, second, ends, slot = row_facts(long_rows, short_rows, me)
    mask = in_row.astype(F32)
    joined = second.astype(F32)
    even = (me % 2 == 0).astype(F32)
    slots = jnp.arange(prev_states.shape[0], dtype=jnp.int32)
    first_half = in_row & ~ends

    mixer_full = lax.all_gather(mixer_weight.astype(BF16), "tensor", axis=2, tiled=True)
    out_full = lax.all_gather(out_weight.astype(BF16), "tensor", axis=0, tiled=True)
    up_full = lax.all_gather(up_weight.astype(BF16), "tensor", axis=1, tiled=True)
    down_full = lax.all_gather(down_weight.astype(BF16), "tensor", axis=0, tiled=True)
    bias = lax.all_gather(gate_bias, "tensor", axis=0, tiled=True)
    prev = lax.all_gather(prev_states, "tensor", axis=1, tiled=True)
    start_state = jnp.sum(
        jnp.where((slots == slot)[:, None] & in_row & ~second, prev, 0.0), axis=0, keepdims=True
    )

    normed, norm1_back = jax.vjp(rms_norm, block_input, norm1_gain)
    rim_rows = pair_swap(normed[tokens - rim :], parts) * joined

    def convolve(extended, weight):
        total = weight[0] * extended[rim:]
        for tap in range(1, rim + 1):
            total = total + mask * weight[tap] * extended[rim - tap : rim - tap + tokens]
        return total

    conv_out, conv_back = jax.vjp(convolve, jnp.concatenate([rim_rows, normed], 0), conv_weight)
    conv_low = conv_out.astype(BF16)
    gate = contract(conv_low, mixer_full[0], (1, 0))
    cand = contract(conv_low, mixer_full[1], (1, 0))
    logit = gate + bias
    keep = jax.nn.sigmoid(-logit)
    opened = jax.nn.sigmoid(logit)
    soft = jax.nn.softplus(cand)
    factors, values = lax.associative_scan(combine, (keep, opened * soft), axis=0)
    ending = factors[-1:] * start_state + values[-1:]
    carry = start_state + joined * pair_swap(ending, parts)
    states = values + factors * carry
    before = jnp.concatenate([carry, states[:-1]], 0)
    end_table = jnp.where((slots == slot) & ends, 1.0, 0.0)[:, None]
    finals = lax.psum_scatter(end_table * states[-1:], "tensor", scatter_dimension=1, tiled=True)
    state_low = states.astype(BF16)
    mixed = contract(state_low, out_full, (1, 0))
    resid = block_input + mask * mixed
    normed_two, norm2_back = jax.vjp(rms_norm, resid, norm2_gain)
    normed_low = normed_two.astype(BF16)
    grad_branch = (mask * cotangent).astype(BF16)
    upward = contract(normed_low, up_full, (1, 0))
    activation, gelu_back = jax.vjp(lambda v: jax.nn.gelu(v, approximate=True), upward)
    activation_low = activation.astype(BF16)
    output = resid + mask * contract(activation_low, down_full, (1, 0))
    grad_act = contract(grad_branch, down_full, (1, 1))
    grad_up = gelu_back(grad_act)[0].astype(BF16)
    grad_norm_two = contract(grad_up, up_full, (1, 1))
    up_grad = contract(normed_low, grad_up, (0, 0))
    down_grad = contract(activation_low, grad_branch, (0, 0))
    grad_resid_norm, gain_two_part = norm2_back(grad_norm_two)
    grad_resid = cotangent + grad_resid_norm
    grad_mixed = (mask * grad_resid).astype(BF16)
    out_grad = contract(state_low, grad_mixed, (0, 0))
    grad_states = contract(grad_mixed, out_full, (1, 1))
    later_keep = jnp.concatenate([keep[1:], jnp.ones_like(keep[:1])], 0)
    back_factors, back_values = lax.associative_scan(combine, (later_keep, grad_states), axis=0, reverse=True)
    joins_next = (first_half & (me % 2 == 0)).astype(F32)
    back_carry = joins_next * pair_swap(keep[:1] * back_values[:1], parts)
    carried = back_values + back_factors * back_carry
    grad_logit = carried * (soft - before) * opened * (1 - opened)
    grad_cand = carried * opened * jax.nn.sigmoid(cand)
    bias_part = jnp.sum(grad_logit, axis=0)
    grad_logit_low = grad_logit.astype(BF16)
    grad_cand_low = grad_cand.astype(BF16)
    mixer_grad = jnp.stack([contract(conv_low, grad_logit_low, (0, 0)), contract(conv_low, grad_cand_low, (0, 0))])
    grad_conv = contract(grad_logit_low, mixer_full[0], (1, 1)) + contract(grad_cand_low, mixer_full[1], (1, 1))
    grad_extended, taps_part = conv_back(grad_conv)
    returned = joins_next * pair_swap(joined * grad_extended[:rim], parts)
    grad_normed = grad_extended[rim:] + jnp.concatenate(
        [jnp.zeros((tokens - rim, width), F32), returned], 0
    )
    grad_input_norm, gain_one_part = norm1_back(grad_normed)
    input_grad = grad_resid + grad_input_norm

    def scatter(grad, dim):
        return lax.psum_scatter(grad.astype(BF16), "tensor", scatter_dimension=dim, tiled=True)

    sharded = (
        scatter(mixer_grad, 2), scatter(out_grad, 0), scatter(up_grad, 1), scatter(down_grad, 0),
    )
    summed = tuple(g.astype(F32) for g in lax.psum(sharded, "dp"))
    shared = lax.psum((gain_one_part, taps_part, gain_two_part, bias_part), ("dp", "tensor"))
    channels = gate_bias.shape[0]
    bias_grad = lax.dynamic_slice_in_dim(shared[3], me * channels, channels)
    return (
        output, finals, input_grad, shared[0], shared[1], summed[0], bias_grad, summed[1], shared[2], summed[2], summed[3],
    )


LANES = 8
MESH = pl.DeviceIdType.MESH
CHUNKS = (2, 1, 2, 1, 2, 4)
FIRST = "yyxxy"
WIRES = 256
SCHEDULE = {
    "own0": (("g", "mix", "y"),),
    "sib": (("g", "out", "y"),),
    "mixfar!": (("g", "up", "y"), ("g", "mix", "x"), ("g", "mix", "z"), ("g", "out", "x"), ("g", "out", "z"), ("g", "down", "y"), ("g", "up", "x"), ("g", "up", "z"), ("g", "mix", "d")),
    "mixpass!": (("g", "out", "d"),),
    "chain": (("g", "down", "x"), ("g", "down", "z")),
    "end!": (("g", "up", "d"),),
    "states": (("g", "down", "d"),),
    "f02a": (("down0", "xa", 0, 0), ("down0", "xa", 0, 1)),
    "f10a": (("up0", "y", 0), ("up0", "y", 1), ("down0", "xa", 1, 0), ("down0", "xa", 1, 1)),
    "f12a": (("down0", "ya", 0), ("up0", "x", 0), ("down0", "ya", 1), ("down1", "xa", 1, 0), ("up1", "y", 0)),
    "f13a": (("up0", "x", 1),),
    "f13u": (("up0", "z", 0), ("down0", "z", 0)),
    "f13d": (("down1", "xa", 0, 0),),
    "B1a": (("down0", "z", 1),),
    "B1b": (("down1", "ya", 0),),
    "og0": (("up0", "zb", 0), ("up0", "z", 1)),
    "r1s": (("down0", "zb", 0),),
    "r1w!": (("up1", "x", 0), ("down0", "zb", 1), ("out", "y", 0), ("out", "y", 1)),
    "r1w0": (("up0", "xb", 0), ("down1", "z", 0)),
    "r1k1": (("up0", "zb", 1),),
    "r1e0": (("down0", "xb", 0), ("out", "x", 0), ("up1", "z", 0), ("mix", "y", 0), ("down0", "xb", 1), ("mix", "y", 1), ("mix", "y", 2), ("mix", "y", 3)),
    "r0s": (("out", "x", 1), ("down1", "zb", 0)),
    "r0w!": (("out", "z", 0), ("up0", "xb", 1)),
    "r0k1": (("out", "z", 1), ("up1", "zb", 0)),
    "r0e1": (("mix", "x", 0), ("mix", "x", 1), ("down1", "xb", 0)),
    "halo!": (("mix", "x", 2), ("out", "zb", 0)),
    "n1a": (("out", "zb", 1),),
    "n1b": (("mix", "z", 0), ("mix", "x", 3)),
    "drain": (("mix", "z", 1), ("up1", "xb", 0), ("pk", "chip"), ("out", "xb", 0), ("out", "xb", 1), ("mix", "z", 2), ("pk", "x"), ("mix", "zb", 0), ("mix", "z", 3), ("mix", "zb", 1), ("mix", "zb", 2), ("mix", "xb", 0), ("mix", "zb", 3), ("pk", "z"), ("mix", "xb", 1), ("mix", "xb", 2), ("mix", "xb", 3)),
}
GELU_A = 0.7978845608028654
GELU_B = 0.044715


def dot(left, right, dims=(1, 0)):
    return lax.dot_general(left, right, ((dims[:1], dims[1:]), ((), ())), preferred_element_type=F32)


def rows_of(block, width):
    return block.reshape(-1, width)


class Wires:
    def __init__(self, send, recv):
        self.send, self.recv, self.used = send, recv, 0

    def copy(self, src, dst, device):
        k = self.used
        self.used += 1
        return pltpu.make_async_remote_copy(
            src_ref=src, dst_ref=dst, send_sem=self.send.at[k], recv_sem=self.recv.at[k],
            device_id=device, device_id_type=MESH,
        )


def block_kernel(
    sizes, long_ref, short_ref, x_hbm, cot_hbm, prev_ref, bias_ref, gain1_ref, taps_ref, gain2_ref, mix_hbm, outw_hbm, up_hbm,
    down_hbm,
    cb, xb, finals_ref, small_ref, fin_up0, fin_up1, fin_down0, fin_down1, fin_out, fin_mix,
    n1h, res, gn2, fo, conv, n2, gm, act, gup, sig, st, ab, sp, sl,
    mix, outw, up, down,
    *rest,
):
    parts, rest = rest[:5], rest[5:]
    buffers, rest = [rest[5 * k : 5 * k + 5] for k in range(5)], rest[25:]
    (
        ry_mix, kx_mix, rx_mix, rz_mix,
        prev, biases, halo1, halo2, endrow, endin, brow, bin_, fsend, frecv,
        acc_n1, acc_n2, acc_t, acc_b, pk, pk_core, pk_chip, pk_x, pk_z,
        send_sem, recv_sem, local_sem,
    ) = rest
    n, z_count, tokens, width, hs, fs, slots, rim = sizes
    chips = n // 2
    steps = tokens // LANES
    tile = 256
    tiles = tokens // tile
    half_tiles = tiles // 2
    me = lax.axis_index("tensor")
    q, c = me // 2, me % 2
    dp = lax.axis_index("dp")
    z, x = dp // 2, dp % 2
    wires = Wires(send_sem, recv_sem)
    started = []

    def tensor(j):
        return (dp, j)

    sibling = tensor(me + 1 - 2 * c)
    partner = (dp + 1 - 2 * x, me)

    zb = z % 2
    z_partner = ((z + 1 - 2 * zb) * 2 + x, me)

    def z_peer(d):
        return ((((z + d) % z_count) * 2) + x, me)

    def shard_of(d, core):
        return ((q + d) % chips) * 2 + core

    def go(copy):
        copy.start()
        started.append(copy)
        return copy

    locals_ = [
        (mix_hbm.at[0], ab.at[0, pl.ds(0, width)]), (mix_hbm.at[1], ab.at[0, pl.ds(width, width)]),
        (outw_hbm, gn2.at[pl.ds(0, hs)]), (up_hbm, fo.at[pl.ds(0, width)]), (down_hbm, fo.at[pl.ds(width, fs)]),
    ]
    loads = [pltpu.make_async_copy(s, d, local_sem.at[i]) for i, (s, d) in enumerate(locals_)]

    def run(ref, g):
        return ref.at[pl.ds(g * steps, steps)]

    x_loads = [pltpu.make_async_copy(run(x_hbm, g), xb.at[:, g, :], local_sem.at[5 + g]) for g in range(LANES)]
    cot_loads = [pltpu.make_async_copy(run(cot_hbm, g), cb.at[:, g, :], local_sem.at[5 + LANES + g]) for g in range(LANES)]
    for copy in loads[:2] + x_loads + loads[2:] + cot_loads:
        copy.start()

    barrier = pltpu.get_barrier_semaphore()
    peers = [tensor((me + d) % n) for d in range(1, n)] + [partner] + [z_peer(d) for d in range(1, z_count)]
    for peer in peers:
        pl.semaphore_signal(barrier, inc=1, device_id=peer, device_id_type=MESH)

    long_count, short_count = long_ref[0], short_ref[0]
    is_long = jnp.where(me < 2 * long_count, 1.0, 0.0)
    in_row = jnp.where(me < 2 * long_count + short_count, 1.0, 0.0)
    odd = (me % 2).astype(F32)
    joined = is_long * odd
    joins_next = is_long * (1.0 - odd)
    starts = in_row * (1.0 - joined)
    ends = in_row * (1.0 - joins_next)
    slot = jnp.where(me < 2 * long_count, me // 2, me - long_count)
    slot_mask = [jnp.where(slot == s, 1.0, 0.0) for s in range(slots)]

    gathers = {}

    weight_copies = []

    def gather(name, ref):
        r = shard_of(1, c)
        mine, own = ref.at[me, 2 * x + zb], ref.at[r, 2 * x + zb]
        by_x, by_z, corner = ref.at[r, 2 * (1 - x) + zb], ref.at[r, 2 * x + 1 - zb], ref.at[r, 2 * (1 - x) + 1 - zb]
        far = go(wires.copy(mine, mine, tensor(r)))
        sib = go(wires.copy(ref.at[me], ref.at[me], sibling))
        weight_copies.extend((far, sib))
        gathers[name] = dict(
            far=far, sib=sib, ax=wires.copy(own, own, partner), az=wires.copy(own, own, z_partner),
            dz=wires.copy(by_x.at[0], by_x.at[0], z_partner), dx=wires.copy(by_z.at[1], by_z.at[1], partner),
            passed=[wires.copy(part, part, sibling) for part in (own, by_x, by_z, corner)],
        )

    def gather_step(arrived, *then):
        def step(name):
            copies = gathers[name]
            for key in arrived:
                copies[key].wait_recv()
            for key in then:
                weight_copies.append(go(copies["passed"][key] if isinstance(key, int) else copies[key]))

        return step

    def gather_passed(name):
        for copy in gathers[name]["passed"]:
            copy.wait_recv()

    stages = {
        ("g", "y"): gather_step(("far",), "ax", "az", 0), ("g", "x"): gather_step(("ax",), "dz", 1),
        ("g", "z"): gather_step(("az",), "dx", 2), ("g", "d"): gather_step(("dz", "dx"), 3),
    }

    def run_stages(hook):
        for step in SCHEDULE.get(hook, ()):
            if step[0] == "g":
                stages["g", step[2]](step[1], *step[3:])
            else:
                stages[step[:2]](*step[2:])

    prev[me] = prev_ref[...]
    biases[me] = bias_ref[...]
    loads[0].wait()
    loads[1].wait()
    half = width // 2
    for h in range(2):
        mix[me, pl.ds(2 * h, 2)] = (
            jnp.concatenate([ab[0, pl.ds(h * half, half), :], ab[0, pl.ds(width + h * half, half), :]], axis=1)
            .astype(BF16)
            .reshape((2,) + mix.shape[2:])
        )
    pl.semaphore_wait(barrier, len(peers))
    gather("mix", mix)
    lead_copies = []
    for ref in (prev, biases):
        lead_copies += [go(wires.copy(ref.at[me], ref.at[me], tensor((me + d) % n))) for d in range(1, n)]
    loads[2].wait()
    outw[me] = gn2[pl.ds(0, hs), :].astype(BF16).reshape(outw.shape[1:])
    gather("out", outw)
    loads[3].wait()
    up[me] = fo[pl.ds(0, width), :].astype(BF16).reshape(up.shape[1:])
    gather("up", up)
    loads[4].wait()
    down[me] = fo[pl.ds(width, fs), :].astype(BF16).reshape(down.shape[1:])
    gather("down", down)

    span = 64
    spans = tokens // span

    def at(i, shift=0, size=span):
        return pl.ds(pl.multiple_of(i * size + shift, LANES), size)

    def take(ref, i, size=span):
        return ref[pl.ds(i * (size // LANES), size // LANES)].reshape(size, width)

    def put(ref, i, value):
        ref[pl.ds(i * (span // LANES), span // LANES)] = value.reshape(span // LANES, LANES, width)

    def eights(value):
        return jnp.sum(value.reshape(-1, LANES, value.shape[-1]), axis=0)

    hook = run_stages
    for copy in x_loads:
        copy.wait()
    gain1 = gain1_ref[...]
    gain2 = gain2_ref[...]

    def norm1_rows(i):
        v = take(xb, i)
        scale = lax.rsqrt(jnp.mean(v * v, axis=-1, keepdims=True) + epsilon)
        n1h[at(i, rim * LANES), :] = v * scale * gain1

    for part, (begin, stop) in enumerate(((0, 6), (6, 11), (11, 16))):
        pl.loop(begin * spans // 16, stop * spans // 16, unroll=True)(norm1_rows)
        if part < 2:
            hook(f"n1a{part}")

    hook("norm1")
    edge = rim * LANES
    halo_copy = go(wires.copy(n1h.at[pl.ds(tokens, edge)], halo1, sibling))
    halo_copy.wait_recv()
    sub = lax.broadcasted_iota(jnp.int32, (LANES, width), 0)
    for k in range(rim):
        own = pltpu.roll(n1h[pl.ds(tokens + k * LANES, LANES), :], 1, 0)
        other = pltpu.roll(halo1[pl.ds(k * LANES, LANES), :], 1, 0)
        n1h[pl.ds(k * LANES, LANES), :] = jnp.where(sub == 0, joined * other, own)
    tap = [taps_ref[pl.ds(k, 1), :] * (1.0 if k == 0 else in_row) for k in range(rim + 1)]

    def conv_rows(i):
        total = tap[0] * n1h[at(i, edge), :]
        for k in range(1, rim + 1):
            total = total + tap[k] * n1h[at(i, edge - k * LANES), :]
        conv[at(i), :] = total.astype(BF16)

    pl.loop(0, spans // 2, unroll=4)(conv_rows)
    hook("cv0")
    pl.loop(spans // 2, spans, unroll=4)(conv_rows)

    def project(j, between=None):
        weight = rows_of(mix[j], 2 * hs)
        bias = biases[j]

        def some(t):
            rows = at(t, 0, tile)
            pre = dot(conv[rows, :], weight)
            logit = pre[:, :hs] + bias
            cand = pre[:, hs:]
            e = jnp.exp(-jnp.abs(logit))
            r = 1.0 / (1.0 + e)
            opened = jnp.where(logit >= 0, r, e * r)
            keep = jnp.where(logit >= 0, e * r, r)
            soft = jnp.maximum(cand, 0.0) + jnp.log1p(jnp.exp(-jnp.abs(cand)))
            sig[j, rows, :] = opened
            sp[j, rows, :] = soft
            ab[j, rows, :] = keep * in_row
            st[j, at(t, LANES, tile), :] = opened * soft

        if between is None:
            pl.loop(0, tiles, unroll=tiles)(some)
        else:
            pl.loop(0, half_tiles, unroll=half_tiles)(some)
            hook(between)
            pl.loop(half_tiles, tiles, unroll=half_tiles)(some)

    hook("conv")
    project(me, "own0")
    hook("own")
    for copy in lead_copies:
        copy.wait_recv()
    gathers["mix"]["sib"].wait_recv()
    project(me + 1 - 2 * c, "sib0")
    hook("sib")

    def unrolled(count, step, carry, by=4):
        def some(i, carry):
            for k in range(by):
                carry = step(i * by + k, carry)
            return carry

        return lax.fori_loop(0, count // by, some, carry)

    one = jnp.ones((LANES, hs), F32)
    zero = jnp.zeros((LANES, hs), F32)

    def scan(js):
        def step(s, carry):
            rows = at(s, 0, LANES)
            later = at(s, LANES, LANES)
            out = []
            for j, (fac, val) in zip(js, carry):
                a = ab[j, rows, :]
                fac = a * fac
                val = a * val + st[j, later, :]
                ab[j, rows, :] = fac
                st[j, later, :] = val
                out.append((fac, val))
            return tuple(out)

        unrolled(steps, step, tuple((one, zero) for _ in js))

    scan([me, me + 1 - 2 * c])
    hook("scan1")
    for copy in cot_loads:
        copy.wait()

    @pl.loop(0, spans, unroll=4)
    def _(i):
        gm[at(i), :] = (in_row * take(cb, i)).astype(BF16)

    hook("gm")
    hook("mixfar!")
    project(shard_of(1, c))
    hook("rown")
    hook("mixpass!")
    gather_passed("mix")
    project(shard_of(1, 1 - c))
    hook("rsib")
    scan([shard_of(1, c), shard_of(1, 1 - c)])
    hook("scan2")
    last = pl.ds(tokens - LANES, LANES)

    def chain(j, carry, keep_rows):
        fac = ab[j, last, :]
        val = st[j, pl.ds(tokens, LANES), :]
        rows = []
        for g in range(LANES):
            rows.append(carry)
            carry = fac[g : g + 1] * carry + val[g : g + 1]
        if keep_rows:
            st[j, pl.ds(0, LANES), :] = jnp.concatenate(rows, axis=0)
        return carry

    first = []
    for j in range(n):
        begin = jnp.zeros((1, hs), F32)
        for s in range(slots):
            begin = begin + (starts * slot_mask[s]) * prev[j, pl.ds(s, 1), :]
        first.append(begin)
        endrow[j] = chain(j, begin, False)
    end_copy = go(wires.copy(endrow, endin, sibling))
    hook("chain")
    hook("end!")
    end_copy.wait_recv()
    for j in range(n):
        ending = chain(j, first[j] + joined * endin[j], True)
        for s in range(slots):
            fsend[j, pl.ds(s, 1), :] = (ends * slot_mask[s]) * ending
    final_copies = [
        go(wires.copy(fsend.at[(me + d) % n], frecv.at[d - 1], tensor((me + d) % n))) for d in range(1, n)
    ]

    hook("chain2")
    hook("out!")
    gathers["out"]["sib"].wait_recv()
    gather_passed("out")
    @pl.loop(0, tiles, unroll=tiles)
    def _(t):
        rows = at(t, 0, tile)
        mixed = jnp.zeros((tile, width), F32)
        for j in range(n):
            into = st[j, pl.ds(0, LANES), :]
            value = st[j, at(t, LANES, tile), :] + (
                ab[j, rows, :].reshape(-1, LANES, hs) * into[None]
            ).reshape(tile, hs)
            st[j, at(t, LANES, tile), :] = value
            low = value.astype(BF16)
            sl[j, rows, :] = low
            mixed = mixed + dot(low, rows_of(outw[j], width))
        resid = take(xb, t, tile) + in_row * mixed
        res[rows, :] = resid
        scale = lax.rsqrt(jnp.mean(resid * resid, axis=-1, keepdims=True) + epsilon)
        n2[rows, :] = (resid * scale * gain2).astype(BF16)

    hook("states")
    gathers["up"]["sib"].wait_recv()
    gathers["down"]["sib"].wait_recv()

    def far_weights():
        hook("updown!")
        gather_passed("up")
        gather_passed("down")


    class Sum:
        def __init__(self, part, rc, ry, kx, rx, rz, fin):
            self.part, self.rc, self.ry, self.kx, self.rx, self.rz, self.fin = part, rc, ry, kx, rx, rz, fin
            self.chunks = fin.shape[0]
            self.c1 = [None] * chips
            self.c2, self.c3, self.c4, self.c5, self.c6 = {}, {}, {}, {}, {}
            self.first = wires.used
            wires.used += chips

        def one(self, d):
            copy = pltpu.make_async_remote_copy(
                src_ref=self.part.at[shard_of(d, 1 - c)], dst_ref=self.rc.at[d], send_sem=send_sem.at[self.first + d],
                recv_sem=recv_sem.at[self.first + d], device_id=sibling, device_id_type=MESH,
            )
            self.c1[d] = go(copy)

        def both(self, j, d, k, h):
            return self.part[j, k, h].astype(F32) + self.rc[d, k, h].astype(F32)

        def y(self, k=0):
            self.c2[k] = []
            for d in range(1, chips):
                if k == 0:
                    self.c1[d].wait_recv()
                j = shard_of(d, c)
                for h in range(2):
                    self.part[j, k, h] = self.both(j, d, k, h).astype(BF16)
                self.c2[k].append(go(wires.copy(self.part.at[j, k], self.ry.at[d - 1, k], tensor(j))))

        def total(self, k, h):
            v = self.both(me, 0, k, h)
            for d in range(chips - 1):
                v = v + self.ry[d, k, h].astype(F32)
            return v

        def x(self, k=0):
            if k == 0:
                self.c1[0].wait_recv()
            for copy in self.c2[k]:
                copy.wait_recv()
            self.part[me, k, 1 - x] = self.total(k, 1 - x).astype(BF16)
            self.c3[k] = go(wires.copy(self.part.at[me, k, 1 - x], self.rx.at[k], partner))
            self.kx[k] = self.total(k, x)

        def z(self, k=0):
            self.c3[k].wait_recv()
            self.spread(k, self.kx[k] + self.rx[k].astype(F32))

        def spread(self, k, v):
            self.kx[k] = v
            self.part[me, k, x] = v.astype(BF16)
            self.c4[k] = [
                go(wires.copy(self.part.at[me, k, x, (z + d) % z_count], self.rz.at[d - 1, k], z_peer(d)))
                for d in range(1, z_count)
            ]

        def zb(self, k=0):
            for copy in self.c4[k]:
                copy.wait_recv()
            v = self.kx[k, z]
            for d in range(z_count - 1):
                v = v + self.rz[d, k].astype(F32)
            self.fin[k, x, z] = v.astype(BF16)
            mine = self.fin.at[k, x, z]
            self.c5[k] = [go(wires.copy(mine, mine, z_peer(d))) for d in range(1, z_count)]
            self.c6[k] = [go(wires.copy(mine, mine, partner))]

        def xb(self, k=0):
            for d in range(1, z_count):
                self.c5[k][d - 1].wait_recv()
                theirs = self.fin.at[k, x, (z + z_count - d) % z_count]
                self.c6[k].append(go(wires.copy(theirs, theirs, partner)))

        def end(self):
            for k in range(self.chunks):
                for copy in self.c6[k]:
                    copy.wait_recv()

    class SumAcross(Sum):
        def xa(self, d, k=0):
            if k == 0:
                self.c1[d].wait_recv()
            j = shard_of(d, c)
            self.part[j, k, 1 - x] = self.both(j, d, k, 1 - x).astype(BF16)
            self.c3[d, k] = go(wires.copy(self.part.at[j, k, 1 - x], self.rx.at[d, k], partner))

        def ya(self, k=0):
            self.c3[1, k].wait_recv()
            j = shard_of(1, c)
            self.part[j, k, x] = (self.both(j, 1, k, x) + self.rx[1, k].astype(F32)).astype(BF16)
            self.c2[k] = go(wires.copy(self.part.at[j, k, x], self.ry.at[k], tensor(j)))

        def z(self, k=0):
            self.c3[0, k].wait_recv()
            self.c2[k].wait_recv()
            self.spread(k, self.both(me, 0, k, x) + self.rx[0, k].astype(F32) + self.ry[k].astype(F32))

    s_parts = [
        (SumAcross if first == "x" else Sum)(part, *refs, fin)
        for first, part, refs, fin in zip(FIRST, parts, buffers, (fin_up0, fin_up1, fin_down0, fin_down1, fin_out))
    ]
    s_out = s_parts[4]
    s_mix = Sum(up, down, ry_mix, kx_mix, rx_mix, rz_mix, fin_mix)
    for name, unit in zip(("up0", "up1", "down0", "down1", "out", "mix"), s_parts + [s_mix]):
        for stage in ("y", "x", "xa", "ya", "z", "zb", "xb"):
            stages[name, stage] = getattr(unit, stage, None)

    def weight_grad(unit, j, left, right):
        unit.part[j] = dot(left, right, (0, 0)).astype(BF16).reshape(unit.part.shape[1:])

    fh = fs // 2

    feed_tile = 512

    def feed(j, h, name, d=None, begin=False):
        cols = pl.ds(h * fh, fh)
        chunks = down.shape[1] // 2

        @pl.loop(0, tokens // feed_tile, unroll=tokens // feed_tile)
        def _(t):
            rows = at(t, 0, feed_tile)
            upw = rows_of(up[j, :, :, :, :, cols], fh)
            downw = rows_of(down[j, pl.ds(h * chunks, chunks)], width)
            u = dot(n2[rows, :], upw)
            ga = dot(gm[rows, :], downw, (1, 1))
            u2 = u * u
            th = jnp.tanh(GELU_A * u * (1.0 + GELU_B * u2))
            hp = 0.5 + 0.5 * th
            a = (u * hp).astype(BF16)
            slope = hp + (0.5 * GELU_A) * u * (1.0 - th * th) * (1.0 + 3.0 * GELU_B * u2)
            gu = (ga * slope).astype(BF16)
            act[rows, cols] = a
            gup[rows, cols] = gu
            o = dot(a, downw)
            g = dot(gu, upw, (1, 1))
            if begin:
                fo[rows, :] = o
                gn2[rows, :] = g
            else:
                fo[rows, :] = fo[rows, :] + o
                gn2[rows, :] = gn2[rows, :] + g

        hook(name + "a")
        for unit, left, right, end in ((s_parts[h], n2, gup, "u"), (s_parts[2 + h], gm, act, "d")):
            weight_grad(unit, j, left[...], right[:, cols])
            if d is not None:
                unit.one(d)
            hook(name + end)

    feed(me + 1 - 2 * c, 0, "f00", 0, True)
    feed(me, 0, "f01")
    far_weights()
    feed(shard_of(1, 1 - c), 0, "f02", 1)
    feed(shard_of(1, c), 0, "f03")
    feed(shard_of(1, 1 - c), 1, "f10", 1)
    feed(shard_of(1, c), 1, "f11")
    feed(me + 1 - 2 * c, 1, "f12", 0)
    feed(me, 1, "f13")

    acc_n2[...] = jnp.zeros_like(acc_n2)

    def norm2_back(i):
        r = res[at(i), :]
        g = gn2[at(i), :]
        scale = lax.rsqrt(jnp.mean(r * r, axis=-1, keepdims=True) + epsilon)
        gg = g * gain2
        m = jnp.mean(gg * r, axis=-1, keepdims=True)
        gr = take(cb, i) + scale * gg - r * (scale * scale * scale * m)
        acc_n2[...] += eights(g * r * scale)
        gn2[at(i), :] = gr
        gm[at(i), :] = (in_row * gr).astype(BF16)
        put(cb, i, r + in_row * fo[at(i), :])

    pl.loop(0, spans // 2, unroll=2)(norm2_back)
    hook("B1a")
    pl.loop(spans // 2, spans, unroll=2)(norm2_back)
    hook("B1b")

    def store(ref, hbm, first):
        copies = [pltpu.make_async_copy(ref.at[:, g, :], run(hbm, g), local_sem.at[first + g]) for g in range(LANES)]
        for copy in copies:
            copy.start()
        return copies

    for copy in weight_copies:
        copy.wait_send()
    started[:] = [copy for copy in started if not any(copy is other for other in weight_copies)]

    for d in (1, 0):
        for core in (1 - c, c):
            j = shard_of(d, core)
            weight_grad(s_out, j, gm[...], sl[j])
        s_out.one(d)
    hook("og0")

    for j in range(n):
        acc_b[j] = jnp.zeros((LANES, hs), F32)

    def recur_back(d, begin, name):
        js = [shard_of(d, core) for core in range(2)]
        for k in range(2):
            ab[k] = dot(gm[...], rows_of(outw[js[k]], width), (1, 1))
        hook(name + "g")

        def back_step(i, carry):
            s = steps - 1 - i
            rows = at(s, 0, LANES)
            out = []
            for k in range(2):
                fac, val, keep = carry[k]
                fac = keep * fac
                val = ab[k, rows, :] + keep * val
                ab[2 + k, rows, :] = fac
                ab[k, rows, :] = val
                out.append((fac, val, 1.0 - sig[js[k], rows, :]))
            return tuple(out)

        unrolled(steps, back_step, ((one, zero, one), (one, zero, one)))
        hook(name + "s")

        def chain_back(k, carry, j):
            fac = ab[2 + k, pl.ds(0, LANES), :]
            val = ab[k, pl.ds(0, LANES), :]
            keep = 1.0 - sig[j, pl.ds(0, LANES), :]
            rows = []
            for g in reversed(range(LANES)):
                rows.append(carry)
                carry = keep[g : g + 1] * (val[g : g + 1] + fac[g : g + 1] * carry)
            return carry, jnp.concatenate(rows[::-1], axis=0)

        slot_ = 2 * d
        for k in range(2):
            brow[slot_ + k] = chain_back(k, jnp.zeros((1, hs), F32), js[k])[0]
        copy = go(wires.copy(brow.at[pl.ds(slot_, 2)], bin_.at[pl.ds(slot_, 2)], sibling))
        hook(name + "c")
        hook(name + "w!")
        copy.wait_recv()
        grads = (act, gup)
        order = [(1 - c, shard_of(d, 1 - c)), (c, shard_of(d, c))]
        for g, (k, j) in enumerate(order):
            into = chain_back(k, joins_next * bin_[slot_ + k], j)[1]

            @pl.loop(0, tiles, unroll=tiles)
            def _(t, j=j, k=k, g=g, into=into):
                rows = at(t, 0, tile)
                carried = ab[k, rows, :] + (ab[2 + k, rows, :].reshape(-1, LANES, hs) * into[None]).reshape(tile, hs)
                opened = sig[j, rows, :]
                soft = sp[j, rows, :]
                weighted = carried * opened
                gl = weighted * (soft - st[j, rows, :]) * (1.0 - opened)
                close = jnp.where(soft < 0.01, soft * (1.0 - soft * (0.5 - soft * (1.0 / 6.0))), 1.0 - jnp.exp(-soft))
                gc = weighted * close
                acc_b[j] += eights(gl)
                grads[g][rows, :] = jnp.concatenate([gl.astype(BF16), gc.astype(BF16)], axis=1)

            hook(f"{name}k{g}")
            weight_grad(s_mix, j, conv[...], grads[g][...])
            if g == 0:
                s_mix.one(d)
            hook(f"{name}w{g}")

        def gather_back(t):
            rows = at(t, 0, tile)
            back = sum(dot(left[rows, :], rows_of(mix[j], 2 * hs), (1, 1)) for left, (_, j) in zip(grads, order))
            res[rows, :] = back if begin else res[rows, :] + back

        pl.loop(0, half_tiles, unroll=half_tiles)(gather_back)
        hook(name + "e0")
        pl.loop(half_tiles, tiles, unroll=half_tiles)(gather_back)
        hook(name + "e1")

    recur_back(1, True, "r1")
    recur_back(0, False, "r0")
    halo_back = go(wires.copy(res.at[pl.ds(0, edge)], halo2, sibling))
    hook("halo!")
    halo_back.wait_recv()

    for k in range(rim):
        own = pltpu.roll(res[pl.ds(k * LANES, LANES), :], LANES - 1, 0)
        other = pltpu.roll(halo2[pl.ds(k * LANES, LANES), :], LANES - 1, 0)
        res[pl.ds(tokens + k * LANES, LANES), :] = jnp.where(sub == LANES - 1, joins_next * other, own)
    acc_n1[...] = jnp.zeros_like(acc_n1)
    acc_t[...] = jnp.zeros_like(acc_t)

    def norm1_back(i):
        g0 = res[at(i), :]
        total = tap[0] * g0
        acc_t[0] += eights(g0 * n1h[at(i, edge), :])
        for k in range(1, rim + 1):
            total = total + tap[k] * res[at(i, k * LANES), :]
            acc_t[k] += eights(g0 * n1h[at(i, edge - k * LANES), :])
        v = take(xb, i)
        scale = lax.rsqrt(jnp.mean(v * v, axis=-1, keepdims=True) + epsilon)
        gg = total * gain1
        m = jnp.mean(gg * v, axis=-1, keepdims=True)
        acc_n1[...] += eights(total * v * scale)
        put(xb, i, gn2[at(i), :] + scale * gg - v * (scale * scale * scale * m))

    pl.loop(0, spans // 2, unroll=2)(norm1_back)
    hook("n1a")
    pl.loop(spans // 2, spans, unroll=2)(norm1_back)
    hook("n1b")

    pk[...] = jnp.zeros_like(pk)
    pk[pl.ds(0, 1), :] = jnp.sum(acc_n1[...], axis=0, keepdims=True)
    for k in range(rim + 1):
        pk[pl.ds(1 + k, 1), :] = jnp.sum(acc_t[k], axis=0, keepdims=True)
    pk[pl.ds(6, 1), :] = jnp.sum(acc_n2[...], axis=0, keepdims=True)
    for j in range(n):
        pk[pl.ds(8 + j, 1), pl.ds(0, hs)] = jnp.sum(acc_b[j], axis=0, keepdims=True)
    k1 = go(wires.copy(pk, pk_core, sibling))
    small_copies = {}

    def small_chip():
        k1.wait_recv()
        pk_chip[q] = pk[...] + pk_core[...]
        small_copies[2] = go(wires.copy(pk_chip.at[q], pk_chip.at[q], tensor(shard_of(1, c))))

    def small_x():
        small_copies[2].wait_recv()
        pk_x[0] = pk_chip[0] + pk_chip[1]
        small_copies[3] = go(wires.copy(pk_x.at[0], pk_x.at[1], partner))

    def small_z():
        small_copies[3].wait_recv()
        pk_z[z] = pk_x[0] + pk_x[1]
        small_copies[4] = [go(wires.copy(pk_z.at[z], pk_z.at[z], z_peer(d))) for d in range(1, z_count)]

    stages["pk", "chip"], stages["pk", "x"], stages["pk", "z"] = small_chip, small_x, small_z
    hook("pk")
    hook("drain")
    for copy in final_copies:
        copy.wait_recv()
    total = fsend[me]
    for d in range(n - 1):
        total = total + frecv[d]
    finals_ref[...] = total
    for copy in small_copies[4]:
        copy.wait_recv()
    value = pk_z[0]
    for k in range(1, z_count):
        value = value + pk_z[k]
    small_ref[...] = value
    for unit in s_parts + [s_mix]:
        unit.end()
    for copy in started:
        copy.wait_send()


def last_kernel(
    hs, output_in, igrad_in, finals_in, small, g_up0, g_up1, g_down0, g_down1, g_out, g_mix,
    output, finals, igrad, gain1, taps, mixer, bias, outw, gain2, up, down, mixer_v, outw_v, up_v, down_v, sem,
):
    width = up_v.shape[0]
    steps = output_in.shape[0]
    later = []
    for k, (src, dst) in enumerate(((output_in, output), (igrad_in, igrad))):
        for g in range(LANES):
            later.append(pltpu.make_async_copy(src.at[:, g, :], dst.at[pl.ds(g * steps, steps)], sem.at[8 + k * LANES + g]))
            later[-1].start()
    me = lax.axis_index("tensor")
    fh = up_v.shape[1] // 2
    up_v[:, :fh] = rows_of(g_up0[...], fh).astype(F32)
    up_v[:, fh:] = rows_of(g_up1[...], fh).astype(F32)
    later.append(pltpu.make_async_copy(up_v, up, sem.at[2]))
    later[-1].start()
    both = rows_of(g_mix[...], 2 * hs).astype(F32)
    mixer_v[0] = both[:, :hs]
    mixer_v[1] = both[:, hs:]
    later.append(pltpu.make_async_copy(mixer_v, mixer, sem.at[5]))
    later[-1].start()
    down_v[:fh] = rows_of(g_down0[...], fh).astype(F32).T
    down_v[fh:] = rows_of(g_down1[...], fh).astype(F32).T
    later.append(pltpu.make_async_copy(down_v, down, sem.at[6]))
    later[-1].start()
    outw_v[...] = rows_of(g_out[...], hs).astype(F32).T
    later.append(pltpu.make_async_copy(outw_v, outw, sem.at[7]))
    later[-1].start()
    finals[...] = finals_in[...]
    gain1[...] = small[pl.ds(0, 1), :]
    taps[...] = small[pl.ds(1, taps.shape[0]), :]
    gain2[...] = small[pl.ds(6, 1), :]
    bias[...] = small[pl.ds(8 + me, 1), pl.ds(0, hs)]
    for copy in later:
        copy.wait()


def fused(
    block_input, long_rows, short_rows, prev_states, norm1_gain, conv_weight, mixer_weight, gate_bias,
    out_weight, norm2_gain, up_weight, down_weight, cotangent,
):
    tokens, width = block_input.shape
    n = lax.axis_size("tensor")
    z_count = lax.axis_size("dp") // 2
    chips = n // 2
    slots, hs = prev_states.shape
    fs = up_weight.shape[1]
    rim = conv_weight.shape[0] - 1
    steps = tokens // LANES
    pk_rows = 8 + -(-n // 8) * 8
    units = [(chunks, cols) for chunks, cols in zip(CHUNKS, (fs // 2,) * 4 + (hs, 2 * hs))]

    def block(chunks, cols):
        return (chunks, 2, z_count, width // (2 * z_count * chunks), cols)

    def full(chunks, cols):
        return pltpu.VMEM((n,) + block(chunks, cols), BF16)

    def sums(chunks, cols, across=False):
        dims = block(chunks, cols)
        part = dims[2:]
        return [
            pltpu.VMEM((chips,) + dims, BF16),
            pltpu.VMEM((chunks,) + part if across else (chips - 1,) + dims, BF16),
            pltpu.VMEM((chunks,) + part, F32),
            pltpu.VMEM(((chips, chunks) if across else (chunks,)) + part, BF16),
            pltpu.VMEM((z_count - 1, chunks) + part[1:], BF16),
        ]

    def wide(rows, kind=F32):
        return pltpu.VMEM((rows, width), kind)

    permuted = pltpu.VMEM((steps, LANES, width), F32)
    per_block = pltpu.VMEM((n, tokens, hs), F32)
    scratch = [
        wide(tokens + rim * LANES), wide(tokens + rim * LANES), wide(tokens), wide(tokens),
        wide(tokens, BF16), wide(tokens, BF16), wide(tokens, BF16), pltpu.VMEM((tokens, fs), BF16), pltpu.VMEM((tokens, fs), BF16),
        per_block, pltpu.VMEM((n, tokens + LANES, hs), F32), per_block, per_block, pltpu.VMEM((n, tokens, hs), BF16),
        pltpu.VMEM((n, 4, 2, width // 8, 2 * hs), BF16), pltpu.VMEM((n, 4, 2, hs // 8, width), BF16), full(*units[5]), full(*units[5]),
        *[full(*unit) for unit in units[:5]],
        *[ref for unit, first in zip(units[:5], FIRST) for ref in sums(*unit, first == "x")], *sums(*units[5])[1:],
        pltpu.VMEM((n, slots, hs), F32), pltpu.VMEM((n, 1, hs), F32), wide(rim * LANES), wide(rim * LANES),
        pltpu.VMEM((n, 1, hs), F32), pltpu.VMEM((n, 1, hs), F32), pltpu.VMEM((n, 1, hs), F32), pltpu.VMEM((n, 1, hs), F32),
        pltpu.VMEM((n, slots, hs), F32), pltpu.VMEM((n - 1, slots, hs), F32),
        wide(LANES), wide(LANES), pltpu.VMEM((rim + 1, LANES, width), F32), pltpu.VMEM((n, LANES, hs), F32),
        wide(pk_rows), wide(pk_rows), pltpu.VMEM((chips, pk_rows, width), F32), pltpu.VMEM((2, pk_rows, width), F32),
        pltpu.VMEM((z_count, pk_rows, width), F32),
        pltpu.SemaphoreType.DMA((WIRES,)), pltpu.SemaphoreType.DMA((WIRES,)), pltpu.SemaphoreType.DMA((5 + 4 * LANES,)),
    ]
    vmem = pl.BlockSpec(memory_space=pltpu.VMEM)
    smem = pl.BlockSpec(memory_space=pltpu.SMEM)
    hbm = pl.BlockSpec(memory_space=pl.ANY)

    def shape(dims, kind=F32):
        return jax.ShapeDtypeStruct(dims, kind)

    big = shape((tokens, width))
    outs = pl.pallas_call(
        functools.partial(block_kernel, (n, z_count, tokens, width, hs, fs, slots, rim)),
        out_shape=[permuted, permuted, pltpu.VMEM((slots, hs), F32), pltpu.VMEM((pk_rows, width), F32), *[pltpu.VMEM(block(*unit), BF16) for unit in units]],
        in_specs=[smem, smem, hbm, hbm, vmem, vmem, vmem, vmem, vmem, hbm, hbm, hbm, hbm],
        out_specs=[vmem] * 10,
        scratch_shapes=scratch,
        compiler_params=pltpu.CompilerParams(collective_id=0, has_side_effects=True, vmem_limit_bytes=VMEM_LIMIT),
    )(
        long_rows, short_rows, block_input, cotangent, prev_states, gate_bias[None], norm1_gain[None], conv_weight,
        norm2_gain[None], mixer_weight, out_weight, up_weight, down_weight,
    )
    outs = pl.pallas_call(
        functools.partial(last_kernel, hs),
        out_shape=[
            big, shape((slots, hs)), big, shape((1, width)), shape((rim + 1, width)), shape((2, width, hs)), shape((1, hs)),
            shape((hs, width)), shape((1, width)), shape((width, fs)), shape((fs, width)),
        ],
        in_specs=[vmem] * 10,
        out_specs=[hbm, vmem, hbm, vmem, vmem, hbm, vmem, hbm, vmem, hbm, hbm],
        scratch_shapes=[
            pltpu.VMEM((2, width, hs), F32), wide(hs), pltpu.VMEM((width, fs), F32), wide(fs),
            pltpu.SemaphoreType.DMA((8 + 2 * LANES,)),
        ],
        compiler_params=pltpu.CompilerParams(vmem_limit_bytes=VMEM_LAST),
    )(*outs)
    output, finals, input_grad, gain1, taps, mixer, bias, outw, gain2, up, down = outs
    return (output, finals, input_grad, gain1[0], taps, mixer, bias[0], outw, gain2[0], up, down)


def solution(mesh):
    takes_kernel = mesh.shape["tensor"] == 4 and mesh.shape["dp"] == 8
    rows = P(("dp", "tensor"), None)
    placed = (
        rows, P("dp"), P("dp"), P("dp", "tensor"), P(), P(), P(None, None, "tensor"), P("tensor"),
        P("tensor", None), P(), P(None, "tensor"), P("tensor", None), rows,
    )
    return jax.shard_map(
        fused if takes_kernel else plain,
        mesh=mesh,
        in_specs=placed,
        out_specs=(
            rows, P("dp", "tensor"), rows, P(), P(), P(None, None, "tensor"), P("tensor"), P("tensor", None),
            P(), P(None, "tensor"), P("tensor", None),
        ),
        check_vma=False,
    )
```

```python
import functools

import jax
import jax.numpy as jnp
from jax import lax
from jax.experimental import pallas as pl
from jax.experimental.pallas import tpu as pltpu
from jax.sharding import PartitionSpec as P

SHORT = 1024
LONG = 2048
VMEM_LIMIT = 58 * 1024 * 1024
VMEM_LAST = 24 * 1024 * 1024
epsilon = 1e-06
BF16 = jnp.bfloat16
F32 = jnp.float32


def rms_norm(values, gain):
    return values * lax.rsqrt(jnp.mean(values * values, axis=-1, keepdims=True) + epsilon) * gain


def contract(left, right, dims):
    return lax.dot_general(left, right, ((dims[:1], dims[1:]), ((), ())), preferred_element_type=F32)


def combine(before_pair, after_pair):
    return (before_pair[0] * after_pair[0], after_pair[0] * before_pair[1] + after_pair[1])


def row_facts(long_rows, short_rows, chunk):
    long_count, short_count = long_rows[0], short_rows[0]
    in_long = chunk < 2 * long_count
    in_row = chunk < 2 * long_count + short_count
    second = in_long & (chunk % 2 == 1)
    ends = in_row & (second | ~in_long)
    slot = jnp.where(in_long, chunk // 2, chunk - long_count)
    return in_row, second, ends, slot


def pair_swap(values, count):
    return lax.ppermute(values, "tensor", [(i, i ^ 1) for i in range(count)])


def plain(
    block_input, long_rows, short_rows, prev_states, norm1_gain, conv_weight, mixer_weight, gate_bias,
    out_weight, norm2_gain, up_weight, down_weight, cotangent,
):
    tokens, width = block_input.shape
    parts = lax.axis_size("tensor")
    me = lax.axis_index("tensor")
    rim = conv_weight.shape[0] - 1
    in_row, second, ends, slot = row_facts(long_rows, short_rows, me)
    mask = in_row.astype(F32)
    joined = second.astype(F32)
    even = (me % 2 == 0).astype(F32)
    slots = jnp.arange(prev_states.shape[0], dtype=jnp.int32)
    first_half = in_row & ~ends

    mixer_full = lax.all_gather(mixer_weight.astype(BF16), "tensor", axis=2, tiled=True)
    out_full = lax.all_gather(out_weight.astype(BF16), "tensor", axis=0, tiled=True)
    up_full = lax.all_gather(up_weight.astype(BF16), "tensor", axis=1, tiled=True)
    down_full = lax.all_gather(down_weight.astype(BF16), "tensor", axis=0, tiled=True)
    bias = lax.all_gather(gate_bias, "tensor", axis=0, tiled=True)
    prev = lax.all_gather(prev_states, "tensor", axis=1, tiled=True)
    start_state = jnp.sum(
        jnp.where((slots == slot)[:, None] & in_row & ~second, prev, 0.0), axis=0, keepdims=True
    )

    normed, norm1_back = jax.vjp(rms_norm, block_input, norm1_gain)
    rim_rows = pair_swap(normed[tokens - rim :], parts) * joined

    def convolve(extended, weight):
        total = weight[0] * extended[rim:]
        for tap in range(1, rim + 1):
            total = total + mask * weight[tap] * extended[rim - tap : rim - tap + tokens]
        return total

    conv_out, conv_back = jax.vjp(convolve, jnp.concatenate([rim_rows, normed], 0), conv_weight)
    conv_low = conv_out.astype(BF16)
    gate = contract(conv_low, mixer_full[0], (1, 0))
    cand = contract(conv_low, mixer_full[1], (1, 0))
    logit = gate + bias
    keep = jax.nn.sigmoid(-logit)
    opened = jax.nn.sigmoid(logit)
    soft = jax.nn.softplus(cand)
    factors, values = lax.associative_scan(combine, (keep, opened * soft), axis=0)
    ending = factors[-1:] * start_state + values[-1:]
    carry = start_state + joined * pair_swap(ending, parts)
    states = values + factors * carry
    before = jnp.concatenate([carry, states[:-1]], 0)
    end_table = jnp.where((slots == slot) & ends, 1.0, 0.0)[:, None]
    finals = lax.psum_scatter(end_table * states[-1:], "tensor", scatter_dimension=1, tiled=True)
    state_low = states.astype(BF16)
    mixed = contract(state_low, out_full, (1, 0))
    resid = block_input + mask * mixed
    normed_two, norm2_back = jax.vjp(rms_norm, resid, norm2_gain)
    normed_low = normed_two.astype(BF16)
    grad_branch = (mask * cotangent).astype(BF16)
    upward = contract(normed_low, up_full, (1, 0))
    activation, gelu_back = jax.vjp(lambda v: jax.nn.gelu(v, approximate=True), upward)
    activation_low = activation.astype(BF16)
    output = resid + mask * contract(activation_low, down_full, (1, 0))
    grad_act = contract(grad_branch, down_full, (1, 1))
    grad_up = gelu_back(grad_act)[0].astype(BF16)
    grad_norm_two = contract(grad_up, up_full, (1, 1))
    up_grad = contract(normed_low, grad_up, (0, 0))
    down_grad = contract(activation_low, grad_branch, (0, 0))
    grad_resid_norm, gain_two_part = norm2_back(grad_norm_two)
    grad_resid = cotangent + grad_resid_norm
    grad_mixed = (mask * grad_resid).astype(BF16)
    out_grad = contract(state_low, grad_mixed, (0, 0))
    grad_states = contract(grad_mixed, out_full, (1, 1))
    later_keep = jnp.concatenate([keep[1:], jnp.ones_like(keep[:1])], 0)
    back_factors, back_values = lax.associative_scan(combine, (later_keep, grad_states), axis=0, reverse=True)
    joins_next = (first_half & (me % 2 == 0)).astype(F32)
    back_carry = joins_next * pair_swap(keep[:1] * back_values[:1], parts)
    carried = back_values + back_factors * back_carry
    grad_logit = carried * (soft - before) * opened * (1 - opened)
    grad_cand = carried * opened * jax.nn.sigmoid(cand)
    bias_part = jnp.sum(grad_logit, axis=0)
    grad_logit_low = grad_logit.astype(BF16)
    grad_cand_low = grad_cand.astype(BF16)
    mixer_grad = jnp.stack([contract(conv_low, grad_logit_low, (0, 0)), contract(conv_low, grad_cand_low, (0, 0))])
    grad_conv = contract(grad_logit_low, mixer_full[0], (1, 1)) + contract(grad_cand_low, mixer_full[1], (1, 1))
    grad_extended, taps_part = conv_back(grad_conv)
    returned = joins_next * pair_swap(joined * grad_extended[:rim], parts)
    grad_normed = grad_extended[rim:] + jnp.concatenate(
        [jnp.zeros((tokens - rim, width), F32), returned], 0
    )
    grad_input_norm, gain_one_part = norm1_back(grad_normed)
    input_grad = grad_resid + grad_input_norm

    def scatter(grad, dim):
        return lax.psum_scatter(grad.astype(BF16), "tensor", scatter_dimension=dim, tiled=True)

    sharded = (
        scatter(mixer_grad, 2), scatter(out_grad, 0), scatter(up_grad, 1), scatter(down_grad, 0),
    )
    summed = tuple(g.astype(F32) for g in lax.psum(sharded, "dp"))
    shared = lax.psum((gain_one_part, taps_part, gain_two_part, bias_part), ("dp", "tensor"))
    channels = gate_bias.shape[0]
    bias_grad = lax.dynamic_slice_in_dim(shared[3], me * channels, channels)
    return (
        output, finals, input_grad, shared[0], shared[1], summed[0], bias_grad, summed[1], shared[2], summed[2], summed[3],
    )


LANES = 8
MESH = pl.DeviceIdType.MESH
CHUNKS = (2, 1, 2, 1, 2, 4)
FIRST = "yyxxy"
WIRES = 256
SCHEDULE = {
    "own0": (("g", "mix", "y"),),
    "sib": (("g", "out", "y"),),
    "mixfar!": (("g", "up", "y"), ("g", "mix", "x"), ("g", "mix", "z"), ("g", "out", "x"), ("g", "out", "z"), ("g", "down", "y"), ("g", "up", "x"), ("g", "up", "z"), ("g", "mix", "d")),
    "mixpass!": (("g", "out", "d"),),
    "chain": (("g", "down", "x"), ("g", "down", "z")),
    "end!": (("g", "up", "d"),),
    "states": (("g", "down", "d"),),
    "f02a": (("down0", "xa", 0, 0), ("down0", "xa", 0, 1)),
    "f10a": (("up0", "y", 0), ("up0", "y", 1), ("down0", "xa", 1, 0), ("down0", "xa", 1, 1)),
    "f12a": (("down0", "ya", 0), ("up0", "x", 0), ("down0", "ya", 1), ("down1", "xa", 1, 0), ("up1", "y", 0)),
    "f13a": (("up0", "x", 1),),
    "f13u": (("up0", "z", 0), ("down0", "z", 0)),
    "f13d": (("down1", "xa", 0, 0),),
    "B1a": (("down0", "z", 1),),
    "B1b": (("down1", "ya", 0),),
    "og0": (("up0", "zb", 0), ("up0", "z", 1)),
    "r1s": (("down0", "zb", 0),),
    "r1w!": (("up1", "x", 0), ("down0", "zb", 1), ("out", "y", 0), ("out", "y", 1)),
    "r1w0": (("up0", "xb", 0), ("down1", "z", 0)),
    "r1k1": (("up0", "zb", 1),),
    "r1e0": (("down0", "xb", 0), ("out", "x", 0), ("up1", "z", 0), ("mix", "y", 0), ("down0", "xb", 1), ("mix", "y", 1), ("mix", "y", 2), ("mix", "y", 3)),
    "r0s": (("out", "x", 1), ("down1", "zb", 0)),
    "r0w!": (("out", "z", 0), ("up0", "xb", 1)),
    "r0k1": (("out", "z", 1), ("up1", "zb", 0)),
    "r0e1": (("mix", "x", 0), ("mix", "x", 1), ("down1", "xb", 0)),
    "halo!": (("mix", "x", 2), ("out", "zb", 0)),
    "n1a": (("out", "zb", 1),),
    "n1b": (("mix", "z", 0), ("mix", "x", 3)),
    "drain": (("mix", "z", 1), ("up1", "xb", 0), ("pk", "chip"), ("out", "xb", 0), ("out", "xb", 1), ("mix", "z", 2), ("pk", "x"), ("mix", "zb", 0), ("mix", "z", 3), ("mix", "zb", 1), ("mix", "zb", 2), ("mix", "xb", 0), ("mix", "zb", 3), ("pk", "z"), ("mix", "xb", 1), ("mix", "xb", 2), ("mix", "xb", 3)),
}
GELU_A = 0.7978845608028654
GELU_B = 0.044715


def dot(left, right, dims=(1, 0)):
    return lax.dot_general(left, right, ((dims[:1], dims[1:]), ((), ())), preferred_element_type=F32)


def rows_of(block, width):
    return block.reshape(-1, width)


class Wires:
    def __init__(self, send, recv):
        self.send, self.recv, self.used = send, recv, 0

    def copy(self, src, dst, device):
        k = self.used
        self.used += 1
        return pltpu.make_async_remote_copy(
            src_ref=src, dst_ref=dst, send_sem=self.send.at[k], recv_sem=self.recv.at[k],
            device_id=device, device_id_type=MESH,
        )


def block_kernel(
    sizes, long_ref, short_ref, x_hbm, cot_hbm, prev_ref, bias_ref, gain1_ref, taps_ref, gain2_ref, mix_hbm, outw_hbm, up_hbm,
    down_hbm,
    cb, xb, finals_ref, small_ref, fin_up0, fin_up1, fin_down0, fin_down1, fin_out, fin_mix,
    n1h, res, gn2, fo, conv, n2, gm, act, gup, sig, st, ab, sp, sl,
    mix, outw, up, down,
    *rest,
):
    parts, rest = rest[:5], rest[5:]
    buffers, rest = [rest[5 * k : 5 * k + 5] for k in range(5)], rest[25:]
    (
        ry_mix, kx_mix, rx_mix, rz_mix,
        prev, biases, halo1, halo2, endrow, endin, brow, bin_, fsend, frecv,
        acc_n1, acc_n2, acc_t, acc_b, pk, pk_core, pk_chip, pk_x, pk_z,
        send_sem, recv_sem, local_sem,
    ) = rest
    n, z_count, tokens, width, hs, fs, slots, rim = sizes
    chips = n // 2
    steps = tokens // LANES
    tile = 256
    tiles = tokens // tile
    half_tiles = tiles // 2
    me = lax.axis_index("tensor")
    q, c = me // 2, me % 2
    dp = lax.axis_index("dp")
    z, x = dp // 2, dp % 2
    wires = Wires(send_sem, recv_sem)
    started = []

    def tensor(j):
        return (dp, j)

    sibling = tensor(me + 1 - 2 * c)
    partner = (dp + 1 - 2 * x, me)

    zb = z % 2
    z_partner = ((z + 1 - 2 * zb) * 2 + x, me)

    def z_peer(d):
        return ((((z + d) % z_count) * 2) + x, me)

    def shard_of(d, core):
        return ((q + d) % chips) * 2 + core

    def go(copy):
        copy.start()
        started.append(copy)
        return copy

    locals_ = [
        (mix_hbm.at[0], ab.at[0, pl.ds(0, width)]), (mix_hbm.at[1], ab.at[0, pl.ds(width, width)]),
        (outw_hbm, gn2.at[pl.ds(0, hs)]), (up_hbm, fo.at[pl.ds(0, width)]), (down_hbm, fo.at[pl.ds(width, fs)]),
    ]
    loads = [pltpu.make_async_copy(s, d, local_sem.at[i]) for i, (s, d) in enumerate(locals_)]

    def run(ref, g):
        return ref.at[pl.ds(g * steps, steps)]

    x_loads = [pltpu.make_async_copy(run(x_hbm, g), xb.at[:, g, :], local_sem.at[5 + g]) for g in range(LANES)]
    cot_loads = [pltpu.make_async_copy(run(cot_hbm, g), cb.at[:, g, :], local_sem.at[5 + LANES + g]) for g in range(LANES)]
    for copy in loads[:2] + x_loads + loads[2:] + cot_loads:
        copy.start()

    barrier = pltpu.get_barrier_semaphore()
    peers = [tensor((me + d) % n) for d in range(1, n)] + [partner] + [z_peer(d) for d in range(1, z_count)]
    for peer in peers:
        pl.semaphore_signal(barrier, inc=1, device_id=peer, device_id_type=MESH)

    long_count, short_count = long_ref[0], short_ref[0]
    is_long = jnp.where(me < 2 * long_count, 1.0, 0.0)
    in_row = jnp.where(me < 2 * long_count + short_count, 1.0, 0.0)
    odd = (me % 2).astype(F32)
    joined = is_long * odd
    joins_next = is_long * (1.0 - odd)
    starts = in_row * (1.0 - joined)
    ends = in_row * (1.0 - joins_next)
    slot = jnp.where(me < 2 * long_count, me // 2, me - long_count)
    slot_mask = [jnp.where(slot == s, 1.0, 0.0) for s in range(slots)]

    gathers = {}

    weight_copies = []

    def gather(name, ref):
        r = shard_of(1, c)
        mine, own = ref.at[me, 2 * x + zb], ref.at[r, 2 * x + zb]
        by_x, by_z, corner = ref.at[r, 2 * (1 - x) + zb], ref.at[r, 2 * x + 1 - zb], ref.at[r, 2 * (1 - x) + 1 - zb]
        far = go(wires.copy(mine, mine, tensor(r)))
        sib = go(wires.copy(ref.at[me], ref.at[me], sibling))
        weight_copies.extend((far, sib))
        gathers[name] = dict(
            far=far, sib=sib, ax=wires.copy(own, own, partner), az=wires.copy(own, own, z_partner),
            dz=wires.copy(by_x.at[0], by_x.at[0], z_partner), dx=wires.copy(by_z.at[1], by_z.at[1], partner),
            passed=[wires.copy(part, part, sibling) for part in (own, by_x, by_z, corner)],
        )

    def gather_step(arrived, *then):
        def step(name):
            copies = gathers[name]
            for key in arrived:
                copies[key].wait_recv()
            for key in then:
                weight_copies.append(go(copies["passed"][key] if isinstance(key, int) else copies[key]))

        return step

    def gather_passed(name):
        for copy in gathers[name]["passed"]:
            copy.wait_recv()

    stages = {
        ("g", "y"): gather_step(("far",), "ax", "az", 0), ("g", "x"): gather_step(("ax",), "dz", 1),
        ("g", "z"): gather_step(("az",), "dx", 2), ("g", "d"): gather_step(("dz", "dx"), 3),
    }

    def run_stages(hook):
        for step in SCHEDULE.get(hook, ()):
            if step[0] == "g":
                stages["g", step[2]](step[1], *step[3:])
            else:
                stages[step[:2]](*step[2:])

    prev[me] = prev_ref[...]
    biases[me] = bias_ref[...]
    loads[0].wait()
    loads[1].wait()
    half = width // 2
    for h in range(2):
        mix[me, pl.ds(2 * h, 2)] = (
            jnp.concatenate([ab[0, pl.ds(h * half, half), :], ab[0, pl.ds(width + h * half, half), :]], axis=1)
            .astype(BF16)
            .reshape((2,) + mix.shape[2:])
        )
    pl.semaphore_wait(barrier, len(peers))
    gather("mix", mix)
    lead_copies = []
    for ref in (prev, biases):
        lead_copies += [go(wires.copy(ref.at[me], ref.at[me], tensor((me + d) % n))) for d in range(1, n)]
    loads[2].wait()
    outw[me] = gn2[pl.ds(0, hs), :].astype(BF16).reshape(outw.shape[1:])
    gather("out", outw)
    loads[3].wait()
    up[me] = fo[pl.ds(0, width), :].astype(BF16).reshape(up.shape[1:])
    gather("up", up)
    loads[4].wait()
    down[me] = fo[pl.ds(width, fs), :].astype(BF16).reshape(down.shape[1:])
    gather("down", down)

    span = 64
    spans = tokens // span

    def at(i, shift=0, size=span):
        return pl.ds(pl.multiple_of(i * size + shift, LANES), size)

    def take(ref, i, size=span):
        return ref[pl.ds(i * (size // LANES), size // LANES)].reshape(size, width)

    def put(ref, i, value):
        ref[pl.ds(i * (span // LANES), span // LANES)] = value.reshape(span // LANES, LANES, width)

    def eights(value):
        return jnp.sum(value.reshape(-1, LANES, value.shape[-1]), axis=0)

    hook = run_stages
    for copy in x_loads:
        copy.wait()
    gain1 = gain1_ref[...]
    gain2 = gain2_ref[...]

    def norm1_rows(i):
        v = take(xb, i)
        scale = lax.rsqrt(jnp.mean(v * v, axis=-1, keepdims=True) + epsilon)
        n1h[at(i, rim * LANES), :] = v * scale * gain1

    for part, (begin, stop) in enumerate(((0, 6), (6, 11), (11, 16))):
        pl.loop(begin * spans // 16, stop * spans // 16, unroll=True)(norm1_rows)
        if part < 2:
            hook(f"n1a{part}")

    hook("norm1")
    edge = rim * LANES
    halo_copy = go(wires.copy(n1h.at[pl.ds(tokens, edge)], halo1, sibling))
    halo_copy.wait_recv()
    sub = lax.broadcasted_iota(jnp.int32, (LANES, width), 0)
    for k in range(rim):
        own = pltpu.roll(n1h[pl.ds(tokens + k * LANES, LANES), :], 1, 0)
        other = pltpu.roll(halo1[pl.ds(k * LANES, LANES), :], 1, 0)
        n1h[pl.ds(k * LANES, LANES), :] = jnp.where(sub == 0, joined * other, own)
    tap = [taps_ref[pl.ds(k, 1), :] * (1.0 if k == 0 else in_row) for k in range(rim + 1)]

    def conv_rows(i):
        total = tap[0] * n1h[at(i, edge), :]
        for k in range(1, rim + 1):
            total = total + tap[k] * n1h[at(i, edge - k * LANES), :]
        conv[at(i), :] = total.astype(BF16)

    pl.loop(0, spans // 2, unroll=4)(conv_rows)
    hook("cv0")
    pl.loop(spans // 2, spans, unroll=4)(conv_rows)

    def project(j, between=None):
        weight = rows_of(mix[j], 2 * hs)
        bias = biases[j]

        def some(t):
            rows = at(t, 0, tile)
            pre = dot(conv[rows, :], weight)
            logit = pre[:, :hs] + bias
            cand = pre[:, hs:]
            e = jnp.exp(-jnp.abs(logit))
            r = 1.0 / (1.0 + e)
            opened = jnp.where(logit >= 0, r, e * r)
            keep = jnp.where(logit >= 0, e * r, r)
            soft = jnp.maximum(cand, 0.0) + jnp.log1p(jnp.exp(-jnp.abs(cand)))
            sig[j, rows, :] = opened
            sp[j, rows, :] = soft
            ab[j, rows, :] = keep * in_row
            st[j, at(t, LANES, tile), :] = opened * soft

        if between is None:
            pl.loop(0, tiles, unroll=tiles)(some)
        else:
            pl.loop(0, half_tiles, unroll=half_tiles)(some)
            hook(between)
            pl.loop(half_tiles, tiles, unroll=half_tiles)(some)

    hook("conv")
    project(me, "own0")
    hook("own")
    for copy in lead_copies:
        copy.wait_recv()
    gathers["mix"]["sib"].wait_recv()
    project(me + 1 - 2 * c, "sib0")
    hook("sib")

    def unrolled(count, step, carry, by=4):
        def some(i, carry):
            for k in range(by):
                carry = step(i * by + k, carry)
            return carry

        return lax.fori_loop(0, count // by, some, carry)

    one = jnp.ones((LANES, hs), F32)
    zero = jnp.zeros((LANES, hs), F32)

    def scan(js):
        def step(s, carry):
            rows = at(s, 0, LANES)
            later = at(s, LANES, LANES)
            out = []
            for j, (fac, val) in zip(js, carry):
                a = ab[j, rows, :]
                fac = a * fac
                val = a * val + st[j, later, :]
                ab[j, rows, :] = fac
                st[j, later, :] = val
                out.append((fac, val))
            return tuple(out)

        unrolled(steps, step, tuple((one, zero) for _ in js))

    scan([me, me + 1 - 2 * c])
    hook("scan1")
    for copy in cot_loads:
        copy.wait()

    @pl.loop(0, spans, unroll=4)
    def _(i):
        gm[at(i), :] = (in_row * take(cb, i)).astype(BF16)

    hook("gm")
    hook("mixfar!")
    project(shard_of(1, c))
    hook("rown")
    hook("mixpass!")
    gather_passed("mix")
    project(shard_of(1, 1 - c))
    hook("rsib")
    scan([shard_of(1, c), shard_of(1, 1 - c)])
    hook("scan2")
    last = pl.ds(tokens - LANES, LANES)

    def chain(j, carry, keep_rows):
        fac = ab[j, last, :]
        val = st[j, pl.ds(tokens, LANES), :]
        rows = []
        for g in range(LANES):
            rows.append(carry)
            carry = fac[g : g + 1] * carry + val[g : g + 1]
        if keep_rows:
            st[j, pl.ds(0, LANES), :] = jnp.concatenate(rows, axis=0)
        return carry

    first = []
    for j in range(n):
        begin = jnp.zeros((1, hs), F32)
        for s in range(slots):
            begin = begin + (starts * slot_mask[s]) * prev[j, pl.ds(s, 1), :]
        first.append(begin)
        endrow[j] = chain(j, begin, False)
    end_copy = go(wires.copy(endrow, endin, sibling))
    hook("chain")
    hook("end!")
    end_copy.wait_recv()
    for j in range(n):
        ending = chain(j, first[j] + joined * endin[j], True)
        for s in range(slots):
            fsend[j, pl.ds(s, 1), :] = (ends * slot_mask[s]) * ending
    final_copies = [
        go(wires.copy(fsend.at[(me + d) % n], frecv.at[d - 1], tensor((me + d) % n))) for d in range(1, n)
    ]

    hook("chain2")
    hook("out!")
    gathers["out"]["sib"].wait_recv()
    gather_passed("out")
    @pl.loop(0, tiles, unroll=tiles)
    def _(t):
        rows = at(t, 0, tile)
        mixed = jnp.zeros((tile, width), F32)
        for j in range(n):
            into = st[j, pl.ds(0, LANES), :]
            value = st[j, at(t, LANES, tile), :] + (
                ab[j, rows, :].reshape(-1, LANES, hs) * into[None]
            ).reshape(tile, hs)
            st[j, at(t, LANES, tile), :] = value
            low = value.astype(BF16)
            sl[j, rows, :] = low
            mixed = mixed + dot(low, rows_of(outw[j], width))
        resid = take(xb, t, tile) + in_row * mixed
        res[rows, :] = resid
        scale = lax.rsqrt(jnp.mean(resid * resid, axis=-1, keepdims=True) + epsilon)
        n2[rows, :] = (resid * scale * gain2).astype(BF16)

    hook("states")
    gathers["up"]["sib"].wait_recv()
    gathers["down"]["sib"].wait_recv()

    def far_weights():
        hook("updown!")
        gather_passed("up")
        gather_passed("down")


    class Sum:
        def __init__(self, part, rc, ry, kx, rx, rz, fin):
            self.part, self.rc, self.ry, self.kx, self.rx, self.rz, self.fin = part, rc, ry, kx, rx, rz, fin
            self.chunks = fin.shape[0]
            self.c1 = [None] * chips
            self.c2, self.c3, self.c4, self.c5, self.c6 = {}, {}, {}, {}, {}
            self.first = wires.used
            wires.used += chips

        def one(self, d):
            copy = pltpu.make_async_remote_copy(
                src_ref=self.part.at[shard_of(d, 1 - c)], dst_ref=self.rc.at[d], send_sem=send_sem.at[self.first + d],
                recv_sem=recv_sem.at[self.first + d], device_id=sibling, device_id_type=MESH,
            )
            self.c1[d] = go(copy)

        def both(self, j, d, k, h):
            return self.part[j, k, h].astype(F32) + self.rc[d, k, h].astype(F32)

        def y(self, k=0):
            self.c2[k] = []
            for d in range(1, chips):
                if k == 0:
                    self.c1[d].wait_recv()
                j = shard_of(d, c)
                for h in range(2):
                    self.part[j, k, h] = self.both(j, d, k, h).astype(BF16)
                self.c2[k].append(go(wires.copy(self.part.at[j, k], self.ry.at[d - 1, k], tensor(j))))

        def total(self, k, h):
            v = self.both(me, 0, k, h)
            for d in range(chips - 1):
                v = v + self.ry[d, k, h].astype(F32)
            return v

        def x(self, k=0):
            if k == 0:
                self.c1[0].wait_recv()
            for copy in self.c2[k]:
                copy.wait_recv()
            self.part[me, k, 1 - x] = self.total(k, 1 - x).astype(BF16)
            self.c3[k] = go(wires.copy(self.part.at[me, k, 1 - x], self.rx.at[k], partner))
            self.kx[k] = self.total(k, x)

        def z(self, k=0):
            self.c3[k].wait_recv()
            self.spread(k, self.kx[k] + self.rx[k].astype(F32))

        def spread(self, k, v):
            self.kx[k] = v
            self.part[me, k, x] = v.astype(BF16)
            self.c4[k] = [
                go(wires.copy(self.part.at[me, k, x, (z + d) % z_count], self.rz.at[d - 1, k], z_peer(d)))
                for d in range(1, z_count)
            ]

        def zb(self, k=0):
            for copy in self.c4[k]:
                copy.wait_recv()
            v = self.kx[k, z]
            for d in range(z_count - 1):
                v = v + self.rz[d, k].astype(F32)
            self.fin[k, x, z] = v.astype(BF16)
            mine = self.fin.at[k, x, z]
            self.c5[k] = [go(wires.copy(mine, mine, z_peer(d))) for d in range(1, z_count)]
            self.c6[k] = [go(wires.copy(mine, mine, partner))]

        def xb(self, k=0):
            for d in range(1, z_count):
                self.c5[k][d - 1].wait_recv()
                theirs = self.fin.at[k, x, (z + z_count - d) % z_count]
                self.c6[k].append(go(wires.copy(theirs, theirs, partner)))

        def end(self):
            for k in range(self.chunks):
                for copy in self.c6[k]:
                    copy.wait_recv()

    class SumAcross(Sum):
        def xa(self, d, k=0):
            if k == 0:
                self.c1[d].wait_recv()
            j = shard_of(d, c)
            self.part[j, k, 1 - x] = self.both(j, d, k, 1 - x).astype(BF16)
            self.c3[d, k] = go(wires.copy(self.part.at[j, k, 1 - x], self.rx.at[d, k], partner))

        def ya(self, k=0):
            self.c3[1, k].wait_recv()
            j = shard_of(1, c)
            self.part[j, k, x] = (self.both(j, 1, k, x) + self.rx[1, k].astype(F32)).astype(BF16)
            self.c2[k] = go(wires.copy(self.part.at[j, k, x], self.ry.at[k], tensor(j)))

        def z(self, k=0):
            self.c3[0, k].wait_recv()
            self.c2[k].wait_recv()
            self.spread(k, self.both(me, 0, k, x) + self.rx[0, k].astype(F32) + self.ry[k].astype(F32))

    s_parts = [
        (SumAcross if first == "x" else Sum)(part, *refs, fin)
        for first, part, refs, fin in zip(FIRST, parts, buffers, (fin_up0, fin_up1, fin_down0, fin_down1, fin_out))
    ]
    s_out = s_parts[4]
    s_mix = Sum(up, down, ry_mix, kx_mix, rx_mix, rz_mix, fin_mix)
    for name, unit in zip(("up0", "up1", "down0", "down1", "out", "mix"), s_parts + [s_mix]):
        for stage in ("y", "x", "xa", "ya", "z", "zb", "xb"):
            stages[name, stage] = getattr(unit, stage, None)

    def weight_grad(unit, j, left, right):
        unit.part[j] = dot(left, right, (0, 0)).astype(BF16).reshape(unit.part.shape[1:])

    fh = fs // 2

    feed_tile = 512

    def feed(j, h, name, d=None, begin=False):
        cols = pl.ds(h * fh, fh)
        chunks = down.shape[1] // 2

        @pl.loop(0, tokens // feed_tile, unroll=tokens // feed_tile)
        def _(t):
            rows = at(t, 0, feed_tile)
            upw = rows_of(up[j, :, :, :, :, cols], fh)
            downw = rows_of(down[j, pl.ds(h * chunks, chunks)], width)
            u = dot(n2[rows, :], upw)
            ga = dot(gm[rows, :], downw, (1, 1))
            u2 = u * u
            th = jnp.tanh(GELU_A * u * (1.0 + GELU_B * u2))
            hp = 0.5 + 0.5 * th
            a = (u * hp).astype(BF16)
            slope = hp + (0.5 * GELU_A) * u * (1.0 - th * th) * (1.0 + 3.0 * GELU_B * u2)
            gu = (ga * slope).astype(BF16)
            act[rows, cols] = a
            gup[rows, cols] = gu
            o = dot(a, downw)
            g = dot(gu, upw, (1, 1))
            if begin:
                fo[rows, :] = o
                gn2[rows, :] = g
            else:
                fo[rows, :] = fo[rows, :] + o
                gn2[rows, :] = gn2[rows, :] + g

        hook(name + "a")
        for unit, left, right, end in ((s_parts[h], n2, gup, "u"), (s_parts[2 + h], gm, act, "d")):
            weight_grad(unit, j, left[...], right[:, cols])
            if d is not None:
                unit.one(d)
            hook(name + end)

    feed(me + 1 - 2 * c, 0, "f00", 0, True)
    feed(me, 0, "f01")
    far_weights()
    feed(shard_of(1, 1 - c), 0, "f02", 1)
    feed(shard_of(1, c), 0, "f03")
    feed(shard_of(1, 1 - c), 1, "f10", 1)
    feed(shard_of(1, c), 1, "f11")
    feed(me + 1 - 2 * c, 1, "f12", 0)
    feed(me, 1, "f13")

    acc_n2[...] = jnp.zeros_like(acc_n2)

    def norm2_back(i):
        r = res[at(i), :]
        g = gn2[at(i), :]
        scale = lax.rsqrt(jnp.mean(r * r, axis=-1, keepdims=True) + epsilon)
        gg = g * gain2
        m = jnp.mean(gg * r, axis=-1, keepdims=True)
        gr = take(cb, i) + scale * gg - r * (scale * scale * scale * m)
        acc_n2[...] += eights(g * r * scale)
        gn2[at(i), :] = gr
        gm[at(i), :] = (in_row * gr).astype(BF16)
        put(cb, i, r + in_row * fo[at(i), :])

    pl.loop(0, spans // 2, unroll=4)(norm2_back)
    hook("B1a")
    pl.loop(spans // 2, spans, unroll=4)(norm2_back)
    hook("B1b")

    def store(ref, hbm, first):
        copies = [pltpu.make_async_copy(ref.at[:, g, :], run(hbm, g), local_sem.at[first + g]) for g in range(LANES)]
        for copy in copies:
            copy.start()
        return copies

    for copy in weight_copies:
        copy.wait_send()
    started[:] = [copy for copy in started if not any(copy is other for other in weight_copies)]

    for d in (1, 0):
        for core in (1 - c, c):
            j = shard_of(d, core)
            weight_grad(s_out, j, gm[...], sl[j])
        s_out.one(d)
    hook("og0")

    for j in range(n):
        acc_b[j] = jnp.zeros((LANES, hs), F32)

    def recur_back(d, begin, name):
        js = [shard_of(d, core) for core in range(2)]
        for k in range(2):
            ab[k] = dot(gm[...], rows_of(outw[js[k]], width), (1, 1))
        hook(name + "g")

        def back_step(i, carry):
            s = steps - 1 - i
            rows = at(s, 0, LANES)
            out = []
            for k in range(2):
                fac, val, keep = carry[k]
                fac = keep * fac
                val = ab[k, rows, :] + keep * val
                ab[2 + k, rows, :] = fac
                ab[k, rows, :] = val
                out.append((fac, val, 1.0 - sig[js[k], rows, :]))
            return tuple(out)

        unrolled(steps, back_step, ((one, zero, one), (one, zero, one)))
        hook(name + "s")

        def chain_back(k, carry, j):
            fac = ab[2 + k, pl.ds(0, LANES), :]
            val = ab[k, pl.ds(0, LANES), :]
            keep = 1.0 - sig[j, pl.ds(0, LANES), :]
            rows = []
            for g in reversed(range(LANES)):
                rows.append(carry)
                carry = keep[g : g + 1] * (val[g : g + 1] + fac[g : g + 1] * carry)
            return carry, jnp.concatenate(rows[::-1], axis=0)

        slot_ = 2 * d
        for k in range(2):
            brow[slot_ + k] = chain_back(k, jnp.zeros((1, hs), F32), js[k])[0]
        copy = go(wires.copy(brow.at[pl.ds(slot_, 2)], bin_.at[pl.ds(slot_, 2)], sibling))
        hook(name + "c")
        hook(name + "w!")
        copy.wait_recv()
        grads = (act, gup)
        order = [(1 - c, shard_of(d, 1 - c)), (c, shard_of(d, c))]
        for g, (k, j) in enumerate(order):
            into = chain_back(k, joins_next * bin_[slot_ + k], j)[1]

            @pl.loop(0, tiles, unroll=tiles)
            def _(t, j=j, k=k, g=g, into=into):
                rows = at(t, 0, tile)
                carried = ab[k, rows, :] + (ab[2 + k, rows, :].reshape(-1, LANES, hs) * into[None]).reshape(tile, hs)
                opened = sig[j, rows, :]
                soft = sp[j, rows, :]
                weighted = carried * opened
                gl = weighted * (soft - st[j, rows, :]) * (1.0 - opened)
                close = jnp.where(soft < 0.01, soft * (1.0 - soft * (0.5 - soft * (1.0 / 6.0))), 1.0 - jnp.exp(-soft))
                gc = weighted * close
                acc_b[j] += eights(gl)
                grads[g][rows, :] = jnp.concatenate([gl.astype(BF16), gc.astype(BF16)], axis=1)

            hook(f"{name}k{g}")
            weight_grad(s_mix, j, conv[...], grads[g][...])
            if g == 0:
                s_mix.one(d)
            hook(f"{name}w{g}")

        def gather_back(t):
            rows = pl.ds(t * feed_tile, feed_tile)
            back = sum(dot(left[rows, :], rows_of(mix[j], 2 * hs), (1, 1)) for left, (_, j) in zip(grads, order))
            res[rows, :] = back if begin else res[rows, :] + back

        gather_back(0)
        hook(name + "e0")
        gather_back(1)
        hook(name + "e1")

    recur_back(1, True, "r1")
    recur_back(0, False, "r0")
    halo_back = go(wires.copy(res.at[pl.ds(0, edge)], halo2, sibling))
    hook("halo!")
    halo_back.wait_recv()

    for k in range(rim):
        own = pltpu.roll(res[pl.ds(k * LANES, LANES), :], LANES - 1, 0)
        other = pltpu.roll(halo2[pl.ds(k * LANES, LANES), :], LANES - 1, 0)
        res[pl.ds(tokens + k * LANES, LANES), :] = jnp.where(sub == LANES - 1, joins_next * other, own)
    acc_n1[...] = jnp.zeros_like(acc_n1)
    acc_t[...] = jnp.zeros_like(acc_t)

    def norm1_back(i):
        g0 = res[at(i), :]
        total = tap[0] * g0
        acc_t[0] += eights(g0 * n1h[at(i, edge), :])
        for k in range(1, rim + 1):
            total = total + tap[k] * res[at(i, k * LANES), :]
            acc_t[k] += eights(g0 * n1h[at(i, edge - k * LANES), :])
        v = take(xb, i)
        scale = lax.rsqrt(jnp.mean(v * v, axis=-1, keepdims=True) + epsilon)
        gg = total * gain1
        m = jnp.mean(gg * v, axis=-1, keepdims=True)
        acc_n1[...] += eights(total * v * scale)
        put(xb, i, gn2[at(i), :] + scale * gg - v * (scale * scale * scale * m))

    pl.loop(0, spans // 2, unroll=4)(norm1_back)
    hook("n1a")
    pl.loop(spans // 2, spans, unroll=4)(norm1_back)
    hook("n1b")

    pk[...] = jnp.zeros_like(pk)
    pk[pl.ds(0, 1), :] = jnp.sum(acc_n1[...], axis=0, keepdims=True)
    for k in range(rim + 1):
        pk[pl.ds(1 + k, 1), :] = jnp.sum(acc_t[k], axis=0, keepdims=True)
    pk[pl.ds(6, 1), :] = jnp.sum(acc_n2[...], axis=0, keepdims=True)
    for j in range(n):
        pk[pl.ds(8 + j, 1), pl.ds(0, hs)] = jnp.sum(acc_b[j], axis=0, keepdims=True)
    k1 = go(wires.copy(pk, pk_core, sibling))
    small_copies = {}

    def small_chip():
        k1.wait_recv()
        pk_chip[q] = pk[...] + pk_core[...]
        small_copies[2] = go(wires.copy(pk_chip.at[q], pk_chip.at[q], tensor(shard_of(1, c))))

    def small_x():
        small_copies[2].wait_recv()
        pk_x[0] = pk_chip[0] + pk_chip[1]
        small_copies[3] = go(wires.copy(pk_x.at[0], pk_x.at[1], partner))

    def small_z():
        small_copies[3].wait_recv()
        pk_z[z] = pk_x[0] + pk_x[1]
        small_copies[4] = [go(wires.copy(pk_z.at[z], pk_z.at[z], z_peer(d))) for d in range(1, z_count)]

    stages["pk", "chip"], stages["pk", "x"], stages["pk", "z"] = small_chip, small_x, small_z
    hook("pk")
    hook("drain")
    for copy in final_copies:
        copy.wait_recv()
    total = fsend[me]
    for d in range(n - 1):
        total = total + frecv[d]
    finals_ref[...] = total
    for copy in small_copies[4]:
        copy.wait_recv()
    value = pk_z[0]
    for k in range(1, z_count):
        value = value + pk_z[k]
    small_ref[...] = value
    for unit in s_parts + [s_mix]:
        unit.end()
    for copy in started:
        copy.wait_send()


def last_kernel(
    hs, output_in, igrad_in, finals_in, small, g_up0, g_up1, g_down0, g_down1, g_out, g_mix,
    output, finals, igrad, gain1, taps, mixer, bias, outw, gain2, up, down, mixer_v, outw_v, up_v, down_v, sem,
):
    width = up_v.shape[0]
    steps = output_in.shape[0]
    later = []
    for k, (src, dst) in enumerate(((output_in, output), (igrad_in, igrad))):
        for g in range(LANES):
            later.append(pltpu.make_async_copy(src.at[:, g, :], dst.at[pl.ds(g * steps, steps)], sem.at[8 + k * LANES + g]))
            later[-1].start()
    me = lax.axis_index("tensor")
    fh = up_v.shape[1] // 2
    up_v[:, :fh] = rows_of(g_up0[...], fh).astype(F32)
    up_v[:, fh:] = rows_of(g_up1[...], fh).astype(F32)
    later.append(pltpu.make_async_copy(up_v, up, sem.at[2]))
    later[-1].start()
    both = rows_of(g_mix[...], 2 * hs).astype(F32)
    mixer_v[0] = both[:, :hs]
    mixer_v[1] = both[:, hs:]
    later.append(pltpu.make_async_copy(mixer_v, mixer, sem.at[5]))
    later[-1].start()
    down_v[:fh] = rows_of(g_down0[...], fh).astype(F32).T
    down_v[fh:] = rows_of(g_down1[...], fh).astype(F32).T
    later.append(pltpu.make_async_copy(down_v, down, sem.at[6]))
    later[-1].start()
    outw_v[...] = rows_of(g_out[...], hs).astype(F32).T
    later.append(pltpu.make_async_copy(outw_v, outw, sem.at[7]))
    later[-1].start()
    finals[...] = finals_in[...]
    gain1[...] = small[pl.ds(0, 1), :]
    taps[...] = small[pl.ds(1, taps.shape[0]), :]
    gain2[...] = small[pl.ds(6, 1), :]
    bias[...] = small[pl.ds(8 + me, 1), pl.ds(0, hs)]
    for copy in later:
        copy.wait()


def fused(
    block_input, long_rows, short_rows, prev_states, norm1_gain, conv_weight, mixer_weight, gate_bias,
    out_weight, norm2_gain, up_weight, down_weight, cotangent,
):
    tokens, width = block_input.shape
    n = lax.axis_size("tensor")
    z_count = lax.axis_size("dp") // 2
    chips = n // 2
    slots, hs = prev_states.shape
    fs = up_weight.shape[1]
    rim = conv_weight.shape[0] - 1
    steps = tokens // LANES
    pk_rows = 8 + -(-n // 8) * 8
    units = [(chunks, cols) for chunks, cols in zip(CHUNKS, (fs // 2,) * 4 + (hs, 2 * hs))]

    def block(chunks, cols):
        return (chunks, 2, z_count, width // (2 * z_count * chunks), cols)

    def full(chunks, cols):
        return pltpu.VMEM((n,) + block(chunks, cols), BF16)

    def sums(chunks, cols, across=False):
        dims = block(chunks, cols)
        part = dims[2:]
        return [
            pltpu.VMEM((chips,) + dims, BF16),
            pltpu.VMEM((chunks,) + part if across else (chips - 1,) + dims, BF16),
            pltpu.VMEM((chunks,) + part, F32),
            pltpu.VMEM(((chips, chunks) if across else (chunks,)) + part, BF16),
            pltpu.VMEM((z_count - 1, chunks) + part[1:], BF16),
        ]

    def wide(rows, kind=F32):
        return pltpu.VMEM((rows, width), kind)

    permuted = pltpu.VMEM((steps, LANES, width), F32)
    per_block = pltpu.VMEM((n, tokens, hs), F32)
    scratch = [
        wide(tokens + rim * LANES), wide(tokens + rim * LANES), wide(tokens), wide(tokens),
        wide(tokens, BF16), wide(tokens, BF16), wide(tokens, BF16), pltpu.VMEM((tokens, fs), BF16), pltpu.VMEM((tokens, fs), BF16),
        per_block, pltpu.VMEM((n, tokens + LANES, hs), F32), per_block, per_block, pltpu.VMEM((n, tokens, hs), BF16),
        pltpu.VMEM((n, 4, 2, width // 8, 2 * hs), BF16), pltpu.VMEM((n, 4, 2, hs // 8, width), BF16), full(*units[5]), full(*units[5]),
        *[full(*unit) for unit in units[:5]],
        *[ref for unit, first in zip(units[:5], FIRST) for ref in sums(*unit, first == "x")], *sums(*units[5])[1:],
        pltpu.VMEM((n, slots, hs), F32), pltpu.VMEM((n, 1, hs), F32), wide(rim * LANES), wide(rim * LANES),
        pltpu.VMEM((n, 1, hs), F32), pltpu.VMEM((n, 1, hs), F32), pltpu.VMEM((n, 1, hs), F32), pltpu.VMEM((n, 1, hs), F32),
        pltpu.VMEM((n, slots, hs), F32), pltpu.VMEM((n - 1, slots, hs), F32),
        wide(LANES), wide(LANES), pltpu.VMEM((rim + 1, LANES, width), F32), pltpu.VMEM((n, LANES, hs), F32),
        wide(pk_rows), wide(pk_rows), pltpu.VMEM((chips, pk_rows, width), F32), pltpu.VMEM((2, pk_rows, width), F32),
        pltpu.VMEM((z_count, pk_rows, width), F32),
        pltpu.SemaphoreType.DMA((WIRES,)), pltpu.SemaphoreType.DMA((WIRES,)), pltpu.SemaphoreType.DMA((5 + 4 * LANES,)),
    ]
    vmem = pl.BlockSpec(memory_space=pltpu.VMEM)
    smem = pl.BlockSpec(memory_space=pltpu.SMEM)
    hbm = pl.BlockSpec(memory_space=pl.ANY)

    def shape(dims, kind=F32):
        return jax.ShapeDtypeStruct(dims, kind)

    big = shape((tokens, width))
    outs = pl.pallas_call(
        functools.partial(block_kernel, (n, z_count, tokens, width, hs, fs, slots, rim)),
        out_shape=[permuted, permuted, pltpu.VMEM((slots, hs), F32), pltpu.VMEM((pk_rows, width), F32), *[pltpu.VMEM(block(*unit), BF16) for unit in units]],
        in_specs=[smem, smem, hbm, hbm, vmem, vmem, vmem, vmem, vmem, hbm, hbm, hbm, hbm],
        out_specs=[vmem] * 10,
        scratch_shapes=scratch,
        compiler_params=pltpu.CompilerParams(collective_id=0, has_side_effects=True, vmem_limit_bytes=VMEM_LIMIT),
    )(
        long_rows, short_rows, block_input, cotangent, prev_states, gate_bias[None], norm1_gain[None], conv_weight,
        norm2_gain[None], mixer_weight, out_weight, up_weight, down_weight,
    )
    outs = pl.pallas_call(
        functools.partial(last_kernel, hs),
        out_shape=[
            big, shape((slots, hs)), big, shape((1, width)), shape((rim + 1, width)), shape((2, width, hs)), shape((1, hs)),
            shape((hs, width)), shape((1, width)), shape((width, fs)), shape((fs, width)),
        ],
        in_specs=[vmem] * 10,
        out_specs=[hbm, vmem, hbm, vmem, vmem, hbm, vmem, hbm, vmem, hbm, hbm],
        scratch_shapes=[
            pltpu.VMEM((2, width, hs), F32), wide(hs), pltpu.VMEM((width, fs), F32), wide(fs),
            pltpu.SemaphoreType.DMA((8 + 2 * LANES,)),
        ],
        compiler_params=pltpu.CompilerParams(vmem_limit_bytes=VMEM_LAST),
    )(*outs)
    output, finals, input_grad, gain1, taps, mixer, bias, outw, gain2, up, down = outs
    return (output, finals, input_grad, gain1[0], taps, mixer, bias[0], outw, gain2[0], up, down)


def solution(mesh):
    takes_kernel = mesh.shape["tensor"] == 4 and mesh.shape["dp"] == 8
    rows = P(("dp", "tensor"), None)
    placed = (
        rows, P("dp"), P("dp"), P("dp", "tensor"), P(), P(), P(None, None, "tensor"), P("tensor"),
        P("tensor", None), P(), P(None, "tensor"), P("tensor", None), rows,
    )
    return jax.shard_map(
        fused if takes_kernel else plain,
        mesh=mesh,
        in_specs=placed,
        out_specs=(
            rows, P("dp", "tensor"), rows, P(), P(), P(None, None, "tensor"), P("tensor"), P("tensor", None),
            P(), P(None, "tensor"), P("tensor", None),
        ),
        check_vma=False,
    )
```
